32 devices in a mesh: mol: 8 (over z, y), row: 4 (over x, core).
Axes of the slice: x: 2, y: 2, z: 4, core: 2. Of those that a mesh axis runs over, the one named last changes fastest.
Arguments:
- node_feats: bfloat16 [1024, 29, 128], P(('mol', 'row')), may hold values from -3 to 3
- edge_feats: bfloat16 [5, 65536], P(None, 'mol'), may hold values from -6 to 6
- edge_ends: int32 [2, 1024, 64], P(None, 'mol'), may hold values from 0 to 29, as said below
- atom_counts: int32 [1024], P(('mol', 'row')), may hold values from 8 to 29, as said below
- dataset_flags: int32 [1024], P(('mol', 'row')), may hold values 0 or 1
- targets: float32 [1024, 12], P(('mol', 'row')), may hold values from 0.5 to 2.5
- present: int32 [1024, 12], P(('mol', 'row')), may hold values 0 or 1
- edge_in: float32 [5, 128], replicated, may hold values from -2.5 to 2.5
- edge_out: float32 [128, 16384], P(None, 'row'), may hold values from -0.046875 to 0.046875
- edge_bias: float32 [16384], P('row'), may hold values from -0.75 to 0.75
- gru_weights: float32 [2, 128, 384], replicated, may hold values from -0.5 to 0.5
- lstm_weights: float32 [384, 512], replicated, may hold values from -0.3125 to 0.3125
- head_first: float32 [256, 128], replicated, may hold values from -0.375 to 0.375
- head_second: float32 [128, 12], replicated, may hold values from -0.5 to 0.5
- biases: float32 [1572], replicated, may hold values from -4 to 4
- moment_edge_in: float32 [5, 128], replicated, may hold values from -0.00010681152 to 0.00010681152
- moment_edge_out: float32 [128, 16384], P(None, 'row'), may hold values from -0.00010681152 to 0.00010681152
- moment_edge_bias: float32 [16384], P('row'), may hold values from -0.00010681152 to 0.00010681152
- moment_gru: float32 [2, 128, 384], replicated, may hold values from -0.00010681152 to 0.00010681152
- moment_lstm: float32 [384, 512], replicated, may hold values from -0.00010681152 to 0.00010681152
- moment_head_first: float32 [256, 128], replicated, may hold values from -0.00010681152 to 0.00010681152
- moment_head_second: float32 [128, 12], replicated, may hold values from -0.00010681152 to 0.00010681152
- moment_biases: float32 [1572], replicated, may hold values from -0.00390625 to 0.00390625
- second_edge_in: float32 [5, 128], replicated, may hold values from 4.09004e-12 to 1.636016e-11
- second_edge_out: float32 [128, 16384], P(None, 'row'), may hold values from 4.09004e-12 to 1.636016e-11
- second_edge_bias: float32 [16384], P('row'), may hold values from 4.09004e-12 to 1.636016e-11
- second_gru: float32 [2, 128, 384], replicated, may hold values from 4.09004e-12 to 1.636016e-11
- second_lstm: float32 [384, 512], replicated, may hold values from 4.09004e-12 to 1.636016e-11
- second_head_first: float32 [256, 128], replicated, may hold values from 4.09004e-12 to 1.636016e-11
- second_head_second: float32 [128, 12], replicated, may hold values from 4.09004e-12 to 1.636016e-11
- second_biases: float32 [1572], replicated, may hold values from 6.361323e-09 to 2.5445292e-08
Outputs:
- new_edge_in: float32 [5, 128], replicated
- new_edge_out: float32 [128, 16384], P(None, 'row')
- new_edge_bias: float32 [16384], P('row')
- new_gru: float32 [2, 128, 384], replicated
- new_lstm: float32 [384, 512], replicated
- new_head_first: float32 [256, 128], replicated
- new_head_second: float32 [128, 12], replicated
- new_biases: float32 [1572], replicated
- new_moment_edge_in: float32 [5, 128], replicated
- new_moment_edge_out: float32 [128, 16384], P(None, 'row')
- new_moment_edge_bias: float32 [16384], P('row')
- new_moment_gru: float32 [2, 128, 384], replicated
- new_moment_lstm: float32 [384, 512], replicated
- new_moment_head_first: float32 [256, 128], replicated
- new_moment_head_second: float32 [128, 12], replicated
- new_moment_biases: float32 [1572], replicated
- new_second_edge_in: float32 [5, 128], replicated
- new_second_edge_out: float32 [128, 16384], P(None, 'row')
- new_second_edge_bias: float32 [16384], P('row')
- new_second_gru: float32 [2, 128, 384], replicated
- new_second_lstm: float32 [384, 512], replicated
- new_second_head_first: float32 [256, 128], replicated
- new_second_head_second: float32 [128, 12], replicated
- new_second_biases: float32 [1572], replicated
- loss_sum: float32 [], replicated
- target_count: float32 [], replicated
- grad_norm: float32 [], replicated
The draws below stay inside these ranges and needn't reach their ends.
Inputs may be any that keep to these rules, and one draw needn't show every extreme that they name: `atom_counts`: some molecule has 29 atoms in every draw. `edge_ends`: slot k of a molecule of c atoms is live exactly when k < 2 (c - 1); empty slots hold 29 in both rows; the live slots hold both directions of the bonds of a tree over the molecule's atoms, each atom j >= 1 bonded to one atom below it.
All inputs are finite; a program needn't handle non-finite values. No bound on the sum of `dataset_flags` or of `present` on one device may be relied on, other than what follows from the above.
Results may differ from the reference program's by a relative error of at most 0.0025.
Values may be sent and summed in bfloat16 or wider, within the bound.
No kernel may reach another device: no remote copies, remote signals or barrier semaphores. Data moves between devices by JAX's collectives and lax.ppermute only.
A program may use at most 256 MiB of HBM per device.

```python
import math
import jax
import jax.numpy as jnp
from jax import lax

H = 128
EH = 128
EIN = 5
NT = 12
STEPS = 6
ATOMS = 29
EM = 64
LAYERS = 2
STEP_COUNT = 10
MOLS = 1024
EDGES = 65536
HH = 16384
BIASES = 1572
NPARAM = 2444964


def edge_layout(key):
    counts = jax.random.randint(jax.random.fold_in(key, 11), (MOLS,), 8, ATOMS + 1)
    widest = jax.random.randint(jax.random.fold_in(key, 12), (), 0, MOLS)
    counts = jnp.where(jnp.arange(MOLS) == widest, ATOMS, counts).astype(jnp.int32)
    raw = jax.random.randint(jax.random.fold_in(key, 13), (MOLS, ATOMS), 0, 1 << 20)
    parents = raw % jnp.maximum(jnp.arange(ATOMS), 1)[None, :]
    slots = jnp.arange(EM)
    child = jnp.minimum(slots // 2 + 1, ATOMS - 1)
    parent = jnp.take(parents, child, axis=1)
    live = slots[None, :] < 2 * (counts[:, None] - 1)
    upward = (slots % 2 == 0)[None, :]
    source = jnp.where(upward, child[None, :], parent)
    target = jnp.where(upward, parent, child[None, :])
    source = jnp.where(live, source, ATOMS)
    target = jnp.where(live, target, ATOMS)
    return (counts, jnp.stack([source, target]).astype(jnp.int32))


def draw_atom_counts(key, part):
    return edge_layout(key)[0]


def draw_edge_ends(key, part):
    return edge_layout(key)[1]


def place_ends(entries, rng, low, high):
    index_at = [jax.random.randint(jax.random.fold_in(rng, axis), (), 0, length) for axis, length in enumerate(entries.shape)]
    longest = entries.shape.index(max(entries.shape))
    beside = index_at[:longest] + [(index_at[longest] + 1) % entries.shape[longest]] + index_at[longest + 1:]
    return entries.at[tuple(index_at)].set(low).at[tuple(beside)].set(high)


def shard_levels(rng, shape, cuts, low, largest):
    level, own = 1.0, jax.random.fold_in(rng, 6)
    for dim, shards_of in cuts:
        heights = jnp.exp(jax.random.uniform(jax.random.fold_in(own, dim), (shards_of,), jnp.float32, low / len(cuts), largest / len(cuts)))
        level = level * jnp.repeat(heights, shape[dim] // shards_of).reshape([-1 if axis == dim else 1 for axis in range(len(shape))])
    return level


def normal_values(stream_key, shape, scale, reach, cuts=(), kind=jnp.bfloat16):
    loudness = shard_levels(stream_key, shape, cuts, -0.22, 0.18) if cuts else 1.0
    values = jax.random.normal(stream_key, shape, jnp.float32) * scale * loudness
    return jnp.minimum(jnp.maximum(values, -reach), reach).astype(kind)


def setup_inputs(seed: int = 0) -> dict:
    keys = jax.random.split(jax.random.key(seed), 32)
    node_feats = normal_values(keys[0], (MOLS, ATOMS, H), 0.5, 3.0, ((0, 32),))
    edge_feats = normal_values(keys[1], (EIN, EDGES), 1.0, 6.0, ((1, 8),))
    edge_ends = draw_edge_ends(jax.random.fold_in(keys[31], 71), 0)
    atom_counts = draw_atom_counts(jax.random.fold_in(keys[31], 71), 0)
    dataset_flags = place_ends((jax.random.randint(keys[4], (MOLS,), 0, 2) < 1).astype(jnp.int32), jax.random.fold_in(keys[4], 1), 0, 1)
    targets = jnp.clip(0.5 + 2.0 * jax.random.uniform(keys[5], (MOLS, NT), jnp.float32) ** shard_levels(keys[5], (MOLS, NT), ((0, 32),), -0.2, 0.2), 0.5, 2.5)
    present = place_ends((jax.random.randint(keys[6], (MOLS, NT), 0, 4) < 3).astype(jnp.int32), jax.random.fold_in(keys[6], 1), 0, 1)
    edge_in = normal_values(keys[7], (EIN, EH), EIN ** -0.5, 2.5, (), jnp.float32)
    edge_out = normal_values(keys[8], (EH, HH), (EH * H) ** -0.5, 0.046875, ((1, 4),), jnp.float32)
    edge_bias = normal_values(keys[9], (HH,), 0.05, 0.75, ((0, 4),), jnp.float32)
    gru_weights = normal_values(keys[10], (2, H, 3 * H), H ** -0.5, 0.5, (), jnp.float32)
    lstm_weights = normal_values(keys[11], (3 * H, 4 * H), (3 * H) ** -0.5, 0.3125, (), jnp.float32)
    head_first = normal_values(keys[12], (2 * H, H), (2 * H) ** -0.5, 0.375, (), jnp.float32)
    head_second = normal_values(keys[13], (H, NT), H ** -0.5, 0.5, (), jnp.float32)
    biases = normal_values(keys[14], (BIASES,), 0.3, 4.0, (), jnp.float32)
    moment_edge_in = normal_values(keys[15], (EIN, EH), (0.011 / NPARAM ** 0.5), 0.00010681152, (), jnp.float32)
    moment_edge_out = normal_values(keys[16], (EH, HH), (0.011 / NPARAM ** 0.5), 0.00010681152, ((1, 4),), jnp.float32)
    moment_edge_bias = normal_values(keys[17], (HH,), (0.011 / NPARAM ** 0.5), 0.00010681152, ((0, 4),), jnp.float32)
    moment_gru = normal_values(keys[18], (2, H, 3 * H), (0.011 / NPARAM ** 0.5), 0.00010681152, (), jnp.float32)
    moment_lstm = normal_values(keys[19], (3 * H, 4 * H), (0.011 / NPARAM ** 0.5), 0.00010681152, (), jnp.float32)
    moment_head_first = normal_values(keys[20], (2 * H, H), (0.011 / NPARAM ** 0.5), 0.00010681152, (), jnp.float32)
    moment_head_second = normal_values(keys[21], (H, NT), (0.011 / NPARAM ** 0.5), 0.00010681152, (), jnp.float32)
    moment_biases = normal_values(keys[22], (BIASES,), (0.011 / BIASES ** 0.5), 0.00390625, (), jnp.float32)
    second_edge_in = jnp.clip(jnp.exp(jax.random.uniform(keys[23], (EIN, EH), jnp.float32, math.log(4.090039938675627e-12), math.log(1.6360159754702508e-11))), 4.090039938675627e-12, 1.6360159754702508e-11)
    second_edge_out = jnp.clip(jnp.exp(math.log(1.6360159754702508e-11) - 1.3862944 * jax.random.uniform(keys[24], (EH, HH), jnp.float32) ** shard_levels(keys[24], (EH, HH), ((1, 4),), -0.2, 0.2)), 4.090039938675627e-12, 1.6360159754702508e-11)
    second_edge_bias = jnp.clip(jnp.exp(math.log(1.6360159754702508e-11) - 1.3862944 * jax.random.uniform(keys[25], (HH,), jnp.float32) ** shard_levels(keys[25], (HH,), ((0, 4),), -0.2, 0.2)), 4.090039938675627e-12, 1.6360159754702508e-11)
    second_gru = jnp.clip(jnp.exp(jax.random.uniform(keys[26], (2, H, 3 * H), jnp.float32, math.log(4.090039938675627e-12), math.log(1.6360159754702508e-11))), 4.090039938675627e-12, 1.6360159754702508e-11)
    second_lstm = jnp.clip(jnp.exp(jax.random.uniform(keys[27], (3 * H, 4 * H), jnp.float32, math.log(4.090039938675627e-12), math.log(1.6360159754702508e-11))), 4.090039938675627e-12, 1.6360159754702508e-11)
    second_head_first = jnp.clip(jnp.exp(jax.random.uniform(keys[28], (2 * H, H), jnp.float32, math.log(4.090039938675627e-12), math.log(1.6360159754702508e-11))), 4.090039938675627e-12, 1.6360159754702508e-11)
    second_head_second = jnp.clip(jnp.exp(jax.random.uniform(keys[29], (H, NT), jnp.float32, math.log(4.090039938675627e-12), math.log(1.6360159754702508e-11))), 4.090039938675627e-12, 1.6360159754702508e-11)
    second_biases = jnp.clip(jnp.exp(jax.random.uniform(keys[30], (BIASES,), jnp.float32, math.log(6.361323023895693e-09), math.log(2.5445292095582772e-08))), 6.361323023895693e-09, 2.5445292095582772e-08)
    return dict(node_feats=node_feats, edge_feats=edge_feats, edge_ends=edge_ends, atom_counts=atom_counts, dataset_flags=dataset_flags, targets=targets, present=present, edge_in=edge_in, edge_out=edge_out, edge_bias=edge_bias, gru_weights=gru_weights, lstm_weights=lstm_weights, head_first=head_first, head_second=head_second, biases=biases, moment_edge_in=moment_edge_in, moment_edge_out=moment_edge_out, moment_edge_bias=moment_edge_bias, moment_gru=moment_gru, moment_lstm=moment_lstm, moment_head_first=moment_head_first, moment_head_second=moment_head_second, moment_biases=moment_biases, second_edge_in=second_edge_in, second_edge_out=second_edge_out, second_edge_bias=second_edge_bias, second_gru=second_gru, second_lstm=second_lstm, second_head_first=second_head_first, second_head_second=second_head_second, second_biases=second_biases)


highest = lax.Precision.HIGHEST
beta_one = 0.9
beta_two = 0.999
rate = 0.05
epsilon = 1e-08
decay = 0.01
clip_norm = 0.1

@jax.custom_vjp
def low(v):
    return lax.optimization_barrier(v.astype(jnp.bfloat16)).astype(jnp.float32)

@jax.custom_vjp
def low_back(v):
    return v

def low_keep(v):
    return (low(v), None)

def low_pass(kept, grad):
    return (grad,)

def back_keep(v):
    return (v, None)

def back_low(kept, grad):
    return (low(grad),)
low.defvjp(low_keep, low_pass)
low_back.defvjp(back_keep, back_low)

def split_biases(biases):
    start = 0
    pieces = []
    for width in (EH, 6 * H, 4 * H, H, NT, 2 * NT):
        pieces.append(biases[start:start + width])
        start = start + width
    return pieces

def gru_cell(message, state_low, state, weights_low, gru_bias):
    from_input = jnp.einsum('mvi,ig->mvg', message, weights_low[0], precision=highest) + gru_bias[:3 * H]
    from_state = jnp.einsum('mvi,ig->mvg', state_low, weights_low[1], precision=highest) + gru_bias[3 * H:]
    reset = jax.nn.sigmoid(from_input[..., :H] + from_state[..., :H])
    update = jax.nn.sigmoid(from_input[..., H:2 * H] + from_state[..., H:2 * H])
    fresh = jnp.tanh(from_input[..., 2 * H:] + reset * from_state[..., 2 * H:])
    return (1.0 - update) * fresh + update * state

def readout(state, counts, flags, targets, present, lstm_weights, head_first, head_second, biases):
    pieces = split_biases(biases)
    live = jnp.arange(ATOMS)[None, :] < counts[:, None]
    live_f = live.astype(jnp.float32)
    molecules = state.shape[0]
    query = jnp.zeros((molecules, 2 * H), jnp.float32)
    hidden = jnp.zeros((molecules, H), jnp.float32)
    cell = jnp.zeros((molecules, H), jnp.float32)
    for repeat in range(STEPS):
        gates = jnp.dot(jnp.concatenate([query, hidden], 1), lstm_weights, precision=highest) + pieces[2]
        in_gate = jax.nn.sigmoid(gates[:, :H])
        forget = jax.nn.sigmoid(gates[:, H:2 * H])
        cell_part = jnp.tanh(gates[:, 2 * H:3 * H])
        out_gate = jax.nn.sigmoid(gates[:, 3 * H:])
        cell = forget * cell + in_gate * cell_part
        hidden = out_gate * jnp.tanh(cell)
        scores = jnp.einsum('mah,mh->ma', state, hidden, precision=highest)
        scores = jnp.where(live, scores, -1e+30)
        weights = jnp.exp(scores - lax.optimization_barrier(jnp.max(scores, 1, keepdims=True))) * live_f
        weights = weights / lax.optimization_barrier(jnp.sum(weights, 1, keepdims=True))
        read = jnp.einsum('ma,mah->mh', weights, state, precision=highest)
        query = jnp.concatenate([hidden, read], 1)
    inner = jax.nn.silu(jnp.dot(query, head_first, precision=highest) + pieces[3])
    offsets = pieces[5].reshape(2, NT)
    chosen = jnp.where(flags[:, None] == 1, offsets[1][None, :], offsets[0][None, :])
    predicted = jnp.dot(inner, head_second, precision=highest) + pieces[4] + chosen
    return jnp.sum(present * (predicted - targets) ** 2)

def block_loss(params, block):
    features, ends, nodes, counts, flags, targets, present = block
    atoms = jnp.arange(ATOMS)
    src_hot = (ends[0][..., None] == atoms).astype(jnp.float32)
    dst_hot = (ends[1][..., None] == atoms).astype(jnp.float32)
    pieces = split_biases(params[7])
    before = jnp.einsum('mkc,ch->mkh', features, params[0], precision=highest) + pieces[0]
    hidden = low(jax.nn.silu(before))
    amat = jnp.einsum('mkh,hf->mkf', hidden, low(params[1]), precision=highest) + params[2]
    amat = low(low_back(amat)).reshape(features.shape[0], EM, H, H)
    gru_low = low(params[3])
    state = nodes
    for layer in range(LAYERS):
        state_low = low(state)
        source = jnp.einsum('mka,mah->mkh', src_hot, state_low, precision=highest)
        moved = jnp.einsum('mkij,mkj->mki', amat, source, precision=highest)
        summed = jnp.einsum('mkv,mki->mvi', dst_hot, moved, precision=highest)
        message = low(low_back(summed))
        state = gru_cell(message, state_low, state, gru_low, pieces[1])
    return readout(state, counts, flags, targets, present, params[4], params[5], params[6], params[7])

def total_loss(params, blocks):

    def advance(carry, block):
        return (carry + jax.checkpoint(block_loss)(params, block), None)
    total, unused = lax.scan(advance, jnp.zeros((), jnp.float32), blocks)
    return total

def adamw(weight, grad, moment, second):
    moment_new = beta_one * moment + (1.0 - beta_one) * grad
    second_new = beta_two * second + (1.0 - beta_two) * grad * grad
    mean_hat = moment_new / (1.0 - beta_one ** STEP_COUNT)
    square_hat = second_new / (1.0 - beta_two ** STEP_COUNT)
    return (weight - rate * (mean_hat / (jnp.sqrt(square_hat) + epsilon) + decay * weight), moment_new, second_new)

def reference(node_feats, edge_feats, edge_ends, atom_counts, dataset_flags, targets, present, edge_in, edge_out, edge_bias, gru_weights, lstm_weights, head_first, head_second, biases, moment_edge_in, moment_edge_out, moment_edge_bias, moment_gru, moment_lstm, moment_head_first, moment_head_second, moment_biases, second_edge_in, second_edge_out, second_edge_bias, second_gru, second_lstm, second_head_first, second_head_second, second_biases):
    molecules = atom_counts.shape[0]
    block_size = math.gcd(molecules, 64)
    count = molecules // block_size
    features = edge_feats.astype(jnp.float32).reshape(EIN, molecules, EM).transpose(1, 2, 0)
    features = features.reshape(count, block_size, EM, EIN)
    ends = edge_ends.reshape(2, count, block_size, EM).transpose(1, 0, 2, 3)
    nodes = node_feats.astype(jnp.float32).reshape(count, block_size, ATOMS, H)
    present_f = present.astype(jnp.float32)
    blocks = (features, ends, nodes, atom_counts.reshape(count, block_size), dataset_flags.reshape(count, block_size), targets.reshape(count, block_size, NT), present_f.reshape(count, block_size, NT))
    params = (edge_in, edge_out, edge_bias, gru_weights, lstm_weights, head_first, head_second, biases)
    loss_total, pullback = jax.vjp(lambda weights: total_loss(weights, blocks), params)
    sums = pullback(jnp.ones((), jnp.float32))[0]
    total_count = jnp.sum(present_f)
    grads = [grad / total_count for grad in sums]
    norm = jnp.sqrt(sum((jnp.sum(grad * grad) for grad in grads)))
    factor = jnp.minimum(1.0, clip_norm / norm)
    moments = (moment_edge_in, moment_edge_out, moment_edge_bias, moment_gru, moment_lstm, moment_head_first, moment_head_second, moment_biases)
    seconds = (second_edge_in, second_edge_out, second_edge_bias, second_gru, second_lstm, second_head_first, second_head_second, second_biases)
    result = [adamw(params[index], grads[index] * factor, moments[index], seconds[index]) for index in range(8)]
    return (result[0][0], result[1][0], result[2][0], result[3][0], result[4][0], result[5][0], result[6][0], result[7][0], result[0][1], result[1][1], result[2][1], result[3][1], result[4][1], result[5][1], result[6][1], result[7][1], result[0][2], result[1][2], result[2][2], result[3][2], result[4][2], result[5][2], result[6][2], result[7][2], loss_total, total_count, norm)
```

```python
import functools
import math

import jax
import jax.numpy as jnp
from jax import lax
from jax.experimental import pallas as pl
from jax.experimental.pallas import tpu as pltpu
from jax.sharding import PartitionSpec as P

H = 128
EH = 128
EIN = 5
NT = 12
STEPS = 6
ATOMS = 29
EM = 64
LAYERS = 2
STEP_COUNT = 10

PAD = 32
LIVE = 2 * (ATOMS - 1)
LB = 256
MIB = 2**20

f32 = jnp.float32
bf16 = jnp.bfloat16
highest = lax.Precision.HIGHEST
beta_one = 0.9
beta_two = 0.999
rate = 0.05
epsilon = 1e-08
decay = 0.01
clip_norm = 0.1

R_LSTM, R_FIRST, R_GRU, R_SECOND, R_MISC, R_EBIAS, R_END = 0, 1024, 1280, 2048, 2176, 2192, 2320

NN = ((1,), (0,))
NTR = ((1,), (1,))
TN = ((0,), (0,))


def mm(a, b, dims=NN):
    return lax.dot_general(a, b, (dims, ((), ())), preferred_element_type=f32)


def split(x):
    high = x.astype(bf16)
    return high, (x - high.astype(f32)).astype(bf16)


def mm3(a, b, dims=NN):
    return mm(a[0], b[0], dims) + (mm(a[0], b[1], dims) + mm(a[1], b[0], dims))


def mm2(a, b, dims=NN):
    high, low = split(a)
    return mm(high, b, dims) + mm(low, b, dims)


def columns(start, size):
    return pl.ds(pl.multiple_of(start, size), size)


def sigmoid(v):
    return jax.nn.sigmoid(v)


def body_main(
    mols,
    counts_s,
    counts_col,
    flags_col,
    targets,
    present,
    tab,
    nodes,
    edge_in_t,
    b_in_col,
    w_fwd,
    w_back,
    ebias,
    gru_t,
    gru_n,
    gbias_col,
    lstm,
    c_lstm,
    first,
    c_head,
    second,
    c_out,
    offsets,
    pack,
    src_o,
    g_o,
    hid_o,
    before_o,
    feat_o,
    z,
    hot_src,
    hot_dst,
    st,
    low,
    msg,
    keep,
    acc,
    dst_acc,
    gm,
    w_all,
    ds_all,
):
    atoms = mols * PAD
    total = jnp.int32(0)
    for m in range(mols):
        total = total + 2 * (counts_s[m] - 1)
    blocks = lax.div(total + (LB - 1), jnp.int32(LB))

    live_col = 2.0 * (counts_col[...].astype(f32) - 1.0)
    below = (
        lax.broadcasted_iota(jnp.int32, (mols, mols), 1)
        < lax.broadcasted_iota(jnp.int32, (mols, mols), 0)
    ).astype(bf16)
    start_col = mm(below, jnp.broadcast_to(live_col, (mols, 128)).astype(bf16))[:, :1]
    e_high, e_low = split(edge_in_t[...])
    e_rest = (edge_in_t[...] - e_high.astype(f32) - e_low.astype(f32)).astype(bf16)

    def prepare(b, carry):
        c = columns(b * LB, LB)
        place = (lax.broadcasted_iota(jnp.int32, (mols, LB), 1) + b * LB).astype(f32)
        mol_hot = ((place >= start_col) & (place < start_col + live_col)).astype(f32)
        rows = mm(tab[...], mol_hot.astype(bf16))
        start_row = jnp.sum(mol_hot * start_col, axis=0, keepdims=True)
        mol_row = jnp.sum(
            mol_hot * lax.broadcasted_iota(jnp.int32, (mols, LB), 0).astype(f32),
            axis=0,
            keepdims=True,
        )
        valid = jnp.sum(mol_hot, axis=0, keepdims=True)
        slot = place[:1] - start_row
        slot_hot = (lax.broadcasted_iota(jnp.int32, (EM, LB), 0).astype(f32) == slot).astype(f32)
        picked = [
            jnp.sum(rows[r * EM : (r + 1) * EM] * slot_hot, axis=0, keepdims=True)
            for r in range(EIN + 2)
        ]
        feat = jnp.concatenate(
            picked[:EIN] + [valid, jnp.zeros((2, LB), f32)], axis=0
        )
        feat_o[:, c] = feat
        feat_low = feat.astype(bf16)
        before = (
            mm(e_high, feat_low) + mm(e_low, feat_low) + mm(e_rest, feat_low) + b_in_col[...]
        )
        before_o[:, c] = before
        hid_o[:, c] = (before * sigmoid(before)).astype(bf16)
        atom = lax.broadcasted_iota(jnp.int32, (atoms, LB), 0)
        base = mol_row * PAD
        src = jnp.where(valid > 0.5, base + picked[EIN], -1.0).astype(jnp.int32)
        dst = jnp.where(valid > 0.5, base + picked[EIN + 1], -1.0).astype(jnp.int32)
        hot_src[:, c] = (atom == src).astype(f32).astype(bf16)
        hot_dst[:, c] = (atom == dst).astype(f32).astype(bf16)
        return carry

    lax.fori_loop(0, blocks, prepare, 0)

    b_high, b_low = split(ebias[...])
    chunks = atoms // LB

    low[0] = nodes[...]
    st[0] = nodes[...].astype(f32)
    for layer in range(LAYERS):
        acc[...] = jnp.zeros_like(acc)

        def move(b, carry, layer=layer):
            c = columns(b * LB, LB)
            source = mm(low[layer], hot_src[:, c]).astype(bf16)
            src_o[layer, :, c] = source
            for h in range(EH):
                z[h * H : (h + 1) * H, :] = hid_o[pl.ds(h, 1), c] * source
            moved = mm(w_fwd[...], z[...])
            moved = moved + (mm(b_high, source) + mm(b_low, source))
            acc[...] += mm2(moved, hot_dst[:, c], NTR)
            return carry

        lax.fori_loop(0, blocks, move, 0)
        msg[layer] = acc[...].astype(bf16)

        def update(k, carry, layer=layer):
            c = columns(k * LB, LB)
            from_in = mm(gru_t[0], msg[layer, :, c]) + gbias_col[0]
            from_st = mm(gru_t[1], low[layer, :, c]) + gbias_col[1]
            reset = sigmoid(from_in[:H] + from_st[:H])
            upd = sigmoid(from_in[H : 2 * H] + from_st[H : 2 * H])
            fresh = jnp.tanh(from_in[2 * H :] + reset * from_st[2 * H :])
            new = (1.0 - upd) * fresh + upd * st[layer, :, c]
            st[layer + 1, :, c] = new
            if layer + 1 < LAYERS:
                low[layer + 1, :, c] = new.astype(bf16)
            keep[layer, 0, :, c] = reset
            keep[layer, 1, :, c] = upd
            keep[layer, 2, :, c] = fresh
            keep[layer, 3, :, c] = from_st[2 * H :]
            return carry

        lax.fori_loop(0, chunks, update, 0)

    lane = lax.broadcasted_iota(jnp.int32, (mols, atoms), 1)
    own = lax.broadcasted_iota(jnp.int32, (mols, atoms), 0)
    slot_of = lane - own * PAD
    alive = (slot_of >= 0) & (slot_of < counts_col[...])
    x = split(st[LAYERS])
    lstm_w = split(lstm[...])
    zeros = jnp.zeros((mols, H), f32)
    hidden, read, cell = zeros, zeros, zeros
    saved = []
    for step in range(STEPS):
        query = jnp.concatenate([hidden, read], axis=1)
        if step == 0:
            gates = jnp.broadcast_to(c_lstm[...], (mols, 4 * H))
        else:
            gates = mm3(split(query), lstm_w) + c_lstm[...]
        in_gate = sigmoid(gates[:, :H])
        forget = sigmoid(gates[:, H : 2 * H])
        part = jnp.tanh(gates[:, 2 * H : 3 * H])
        out_gate = sigmoid(gates[:, 3 * H :])
        before_cell = cell
        cell = forget * cell + in_gate * part
        squashed = jnp.tanh(cell)
        hidden = out_gate * squashed
        scores = jnp.where(alive, mm3(split(hidden), x), -1e30)
        weights = jnp.where(alive, jnp.exp(scores - jnp.max(scores, axis=1, keepdims=True)), 0.0)
        weights = weights / jnp.sum(weights, axis=1, keepdims=True)
        w_all[step * mols : (step + 1) * mols, :] = weights
        read = mm3(split(weights), x, NTR)
        saved.append((query, in_gate, forget, part, out_gate, before_cell, squashed, hidden))
    query = jnp.concatenate([hidden, read], axis=1)
    first_w = split(first[...])
    second_w = split(second[...])
    query_s = split(query)
    inner_pre = mm3(query_s, first_w) + c_head[...]
    inner_sig = sigmoid(inner_pre)
    inner = inner_pre * inner_sig
    inner_s = split(inner)
    is_one = flags_col[...] == 1
    predicted = (
        mm3(inner_s, second_w)
        + c_out[...]
        + jnp.where(is_one, offsets[1:2, :], offsets[0:1, :])
    )
    there = present[...].astype(f32)
    diff = predicted - targets[...]
    loss = jnp.sum(jnp.sum(there * diff * diff, axis=1, keepdims=True), axis=0, keepdims=True)
    count = jnp.sum(jnp.sum(there, axis=1, keepdims=True), axis=0, keepdims=True)

    d_pred = 2.0 * there * diff
    d_pred_s = split(d_pred)
    pack[R_SECOND:R_MISC, :] = jnp.zeros((H, 128), f32)
    pack[R_SECOND:R_MISC, :NT] = mm3(inner_s, d_pred_s, TN)
    misc = jnp.zeros((16, 128), f32)
    pack[R_MISC:R_EBIAS, :] = misc
    pack[R_MISC + 11 : R_MISC + 12, :NT] = jnp.sum(d_pred, axis=0, keepdims=True)
    pack[R_MISC + 12 : R_MISC + 13, :NT] = jnp.sum(
        jnp.where(is_one, 0.0, d_pred), axis=0, keepdims=True
    )
    pack[R_MISC + 13 : R_MISC + 14, :NT] = jnp.sum(
        jnp.where(is_one, d_pred, 0.0), axis=0, keepdims=True
    )
    pack[R_MISC + 14 : R_MISC + 15, 0:1] = loss
    pack[R_MISC + 14 : R_MISC + 15, 1:2] = count
    d_inner = mm3(d_pred_s, second_w, NTR)
    d_pre = d_inner * inner_sig * (1.0 + inner_pre * (1.0 - inner_sig))
    d_pre_s = split(d_pre)
    pack[R_FIRST:R_GRU, :] = mm3(query_s, d_pre_s, TN)
    pack[R_MISC + 10 : R_MISC + 11, :] = jnp.sum(d_pre, axis=0, keepdims=True)
    d_query = mm3(d_pre_s, first_w, NTR)
    d_hidden, d_read = d_query[:, :H], d_query[:, H:]
    d_cell = zeros
    d_gates_all = [None] * STEPS
    d_reads = [None] * STEPS
    for step in reversed(range(STEPS)):
        query, in_gate, forget, part, out_gate, before_cell, squashed, hid_t = saved[step]
        weights = w_all[step * mols : (step + 1) * mols, :]
        d_read_s = split(d_read)
        d_reads[step] = d_read
        d_weights = mm3(d_read_s, x)
        d_scores = weights * (d_weights - jnp.sum(weights * d_weights, axis=1, keepdims=True))
        ds_all[step * mols : (step + 1) * mols, :] = d_scores
        d_hidden = d_hidden + mm3(split(d_scores), x, NTR)
        d_out = d_hidden * squashed * out_gate * (1.0 - out_gate)
        d_cell = d_cell + d_hidden * out_gate * (1.0 - squashed * squashed)
        d_forget = d_cell * before_cell * forget * (1.0 - forget)
        d_in = d_cell * part * in_gate * (1.0 - in_gate)
        d_part = d_cell * in_gate * (1.0 - part * part)
        d_cell = d_cell * forget
        d_gates = jnp.concatenate([d_in, d_forget, d_part, d_out], axis=1)
        d_gates_all[step] = d_gates
        if step > 0:
            d_query = mm3(split(d_gates), lstm_w, NTR)
            d_hidden, d_read = d_query[:, :H], d_query[:, H:]
    queries = split(jnp.concatenate([saved[s][0] for s in range(STEPS)], axis=0))
    d_gates_cat = jnp.concatenate(d_gates_all, axis=0)
    d_gates_s = split(d_gates_cat)
    grad_lstm = mm3(queries, d_gates_s, TN)
    d_gates_sum = jnp.sum(d_gates_cat, axis=0, keepdims=True)
    for k in range(4):
        pack[R_LSTM + k * 256 : R_LSTM + (k + 1) * 256, :] = grad_lstm[:, k * H : (k + 1) * H]
        pack[R_MISC + 6 + k : R_MISC + 7 + k, :] = d_gates_sum[:, k * H : (k + 1) * H]
    left = jnp.concatenate(d_reads + [saved[s][7] for s in range(STEPS)], axis=0)
    left_s = split(left)

    def spread(k, carry):
        c = columns(k * LB, LB)
        right = split(jnp.concatenate([w_all[:, c], ds_all[:, c]], axis=0))
        dst_acc[:, c] = mm3(left_s, right, TN)
        return carry

    lax.fori_loop(0, chunks, spread, 0)

    pack[R_GRU:R_SECOND, :] = jnp.zeros((6 * H, 128), f32)
    for layer in reversed(range(LAYERS)):

        def back(k, carry, layer=layer):
            c = columns(k * LB, LB)
            d_state = dst_acc[:, c]
            reset, upd = keep[layer, 0, :, c], keep[layer, 1, :, c]
            fresh, from_st = keep[layer, 2, :, c], keep[layer, 3, :, c]
            d_upd = d_state * (st[layer, :, c] - fresh) * upd * (1.0 - upd)
            d_fresh = d_state * (1.0 - upd) * (1.0 - fresh * fresh)
            d_reset = d_fresh * from_st * reset * (1.0 - reset)
            d_from_in = jnp.concatenate([d_reset, d_upd, d_fresh], axis=0)
            d_from_st = jnp.concatenate([d_reset, d_upd, d_fresh * reset], axis=0)
            in_s, st_s = split(d_from_in), split(d_from_st)
            gm[:, c] = (mm(gru_n[0], in_s[0]) + mm(gru_n[0], in_s[1])).astype(bf16)
            if layer > 0:
                dst_acc[:, c] = d_state * upd + (mm(gru_n[1], st_s[0]) + mm(gru_n[1], st_s[1]))
            ones = jnp.ones((8, LB), bf16)
            message, state_low = msg[layer, :, c], low[layer, :, c]
            for half, left_m, right_m in ((0, message, in_s), (1, state_low, st_s)):
                grad = mm(left_m, right_m[0], NTR) + mm(left_m, right_m[1], NTR)
                sums = (mm(ones, right_m[0], NTR) + mm(ones, right_m[1], NTR))[:1]
                for q in range(3):
                    r = R_GRU + (half * 3 + q) * H
                    pack[r : r + H, :] += grad[:, q * H : (q + 1) * H]
                    m = R_MISC + half * 3 + q
                    pack[m : m + 1, :] += sums[:, q * H : (q + 1) * H]
            return carry

        lax.fori_loop(0, chunks, back, 0)
        if layer > 0:
            bt_high, bt_low = split(jnp.transpose(ebias[...]))

            def pull(b, carry, layer=layer):
                c = columns(b * LB, LB)
                grad = mm(gm[...], hot_dst[:, c])
                grad_low = grad.astype(bf16)
                g_o[layer, :, c] = grad_low
                hid = hid_o[:, c]
                for i in range(H):
                    z[i * EH : (i + 1) * EH, :] = g_o[layer, pl.ds(i, 1), c] * hid
                pulled = mm(w_back[...], z[...])
                pulled = pulled + (mm(bt_high, grad_low) + mm(bt_low, grad_low))
                dst_acc[...] += mm2(pulled, hot_src[:, c], NTR)
                return carry

            lax.fori_loop(0, blocks, pull, 0)
        else:

            def take(b, carry, layer=layer):
                c = columns(b * LB, LB)
                g_o[layer, :, c] = mm(gm[...], hot_dst[:, c]).astype(bf16)
                return carry

            lax.fori_loop(0, blocks, take, 0)
    acc_b = acc.at[:, :H]
    acc_b[...] = jnp.zeros((H, H), f32)

    def bias_sum(b, carry):
        c = columns(b * LB, LB)
        acc_b[...] += mm(g_o[0, :, c], src_o[0, :, c], NTR) + mm(
            g_o[1, :, c], src_o[1, :, c], NTR
        )
        return carry

    lax.fori_loop(0, blocks, bias_sum, 0)
    pack[R_EBIAS:R_END, :] = acc_b[...]


def body_edges(mols, counts_s, w, src, g, hid, before, feat, out, grad_in, grid_z, grad_hid, acc):
    part = pl.program_id(0)
    total = jnp.int32(0)
    for m in range(mols):
        total = total + 2 * (counts_s[m] - 1)
    blocks = lax.div(total + (LB - 1), jnp.int32(LB))
    rows = w.shape[2] // H

    def edges(b, carry):
        c = columns(b * LB, LB)
        base = part * rows
        g0 = g[0, pl.ds(pl.multiple_of(base, rows), rows), c].astype(f32)
        g1 = g[1, pl.ds(pl.multiple_of(base, rows), rows), c].astype(f32)
        s0, s1 = src[0, :, c].astype(f32), src[1, :, c].astype(f32)
        for i in range(rows):
            grid_z[i * H : (i + 1) * H, :] = (g0[i : i + 1] * s0 + g1[i : i + 1] * s1).astype(bf16)
        pulled = mm(w[0], grid_z[...])

        @pl.when(part == 0)
        def _():
            grad_hid[:, c] = pulled

        @pl.when(part > 0)
        def _():
            grad_hid[:, c] += pulled

        product = mm(hid[:, c], grid_z[...], NTR)

        @pl.when(b == 0)
        def _():
            acc[...] = product

        @pl.when(b > 0)
        def _():
            acc[...] += product

        return carry

    lax.fori_loop(0, blocks, edges, 0)
    out[0] = acc[...].astype(out.dtype)

    @pl.when(part == pl.num_programs(0) - 1)
    def _():
        grad_in[...] = jnp.zeros_like(grad_in)

        def finish(b, carry):
            c = columns(b * LB, LB)
            ahead = before[:, c]
            sig = sigmoid(ahead)
            grad = split(grad_hid[:, c] * sig * (1.0 + ahead * (1.0 - sig)))
            rows_low = feat[:, c].astype(bf16)
            grad_in[...] += mm(rows_low, grad[0], NTR) + mm(rows_low, grad[1], NTR)
            return carry

        lax.fori_loop(0, blocks, finish, 0)


def split_biases(biases):
    start = 0
    pieces = []
    for width in (EH, 6 * H, 4 * H, H, NT, 2 * NT):
        pieces.append(biases[start : start + width])
        start = start + width
    return pieces


def adamw(weight, grad, moment, second):
    moment_new = beta_one * moment + (1.0 - beta_one) * grad
    second_new = beta_two * second + (1.0 - beta_two) * grad * grad
    mean_hat = moment_new / (1.0 - beta_one**STEP_COUNT)
    square_hat = second_new / (1.0 - beta_two**STEP_COUNT)
    return (
        weight - rate * (mean_hat / (jnp.sqrt(square_hat) + epsilon) + decay * weight),
        moment_new,
        second_new,
    )


VM = pl.BlockSpec(memory_space=pltpu.VMEM)
SM = pl.BlockSpec(memory_space=pltpu.SMEM)


def per_device(
    node_feats,
    edge_feats,
    edge_ends,
    atom_counts,
    dataset_flags,
    targets,
    present,
    edge_in,
    edge_out,
    edge_bias,
    gru_weights,
    lstm_weights,
    head_first,
    head_second,
    biases,
    *moments_seconds,
):
    row = lax.axis_index("row")
    row_count = lax.axis_size("row")
    mols = node_feats.shape[0]
    own_rows = edge_out.shape[1] // H
    atoms = mols * PAD
    space = -(-mols * LIVE // LB) * LB
    b_in, b_gru, c_lstm, c_head, c_out, offsets = split_biases(biases)

    out_low = edge_out.astype(bf16)
    w_all = lax.all_gather(out_low, "row", axis=0)
    ebias = lax.all_gather(edge_bias, "row", axis=0).reshape(H, H)
    w4 = w_all.reshape(row_count, EH, own_rows, H)
    w_fwd = w4.transpose(0, 2, 1, 3).reshape(H, EH * H)
    w_back = w4.transpose(3, 0, 2, 1).reshape(H, H * EH)

    ends = lax.dynamic_slice_in_dim(edge_ends, row * mols, mols, 1)
    feats = lax.dynamic_slice_in_dim(edge_feats, row * mols * EM, mols * EM, 1)
    tab = jnp.concatenate(
        [
            feats.reshape(EIN, mols, EM),
            ends.astype(bf16),
            jnp.zeros((1, mols, EM), bf16),
        ],
        axis=0,
    )
    tab = tab.transpose(0, 2, 1).reshape(8 * EM, mols)
    nodes = jnp.pad(node_feats, ((0, 0), (0, PAD - ATOMS), (0, 0))).reshape(atoms, H).T
    gru_low = gru_weights.astype(bf16)
    lstm = jnp.concatenate([lstm_weights[:H] + lstm_weights[2 * H :], lstm_weights[H : 2 * H]], 0)
    edge_in_t = jnp.pad(edge_in, ((0, 3), (0, 0))).T

    sds = jax.ShapeDtypeStruct
    pack, src, g, hid, before, feat = pl.pallas_call(
        functools.partial(body_main, mols),
        out_shape=(
            sds((R_END, 128), f32),
            sds((LAYERS, H, space), bf16),
            sds((LAYERS, H, space), bf16),
            sds((EH, space), bf16),
            sds((EH, space), f32),
            sds((8, space), f32),
        ),
        in_specs=[SM] + [VM] * 21,
        out_specs=(VM,) * 6,
        scratch_shapes=[
            pltpu.VMEM((H * EH, LB), bf16),
            pltpu.VMEM((atoms, space), bf16),
            pltpu.VMEM((atoms, space), bf16),
            pltpu.VMEM((LAYERS + 1, H, atoms), f32),
            pltpu.VMEM((LAYERS, H, atoms), bf16),
            pltpu.VMEM((LAYERS, H, atoms), bf16),
            pltpu.VMEM((LAYERS, 4, H, atoms), f32),
            pltpu.VMEM((H, atoms), f32),
            pltpu.VMEM((H, atoms), f32),
            pltpu.VMEM((H, atoms), bf16),
            pltpu.VMEM((STEPS * mols, atoms), f32),
            pltpu.VMEM((STEPS * mols, atoms), f32),
        ],
        compiler_params=pltpu.CompilerParams(vmem_limit_bytes=60 * MIB),
    )(
        atom_counts,
        atom_counts.reshape(mols, 1),
        dataset_flags.reshape(mols, 1),
        targets,
        present,
        tab,
        nodes,
        edge_in_t,
        b_in.reshape(EH, 1),
        w_fwd,
        w_back,
        ebias,
        gru_low.transpose(0, 2, 1),
        gru_low,
        b_gru.reshape(2, 3 * H, 1),
        lstm,
        c_lstm.reshape(1, 4 * H),
        head_first,
        c_head.reshape(1, H),
        head_second,
        c_out.reshape(1, NT),
        offsets.reshape(2, NT),
    )
    shared = lax.psum(pack, ("mol", "row"))

    grad_out, grad_in = pl.pallas_call(
        functools.partial(body_edges, mols),
        out_shape=(sds((row_count, EH, own_rows * H), bf16), sds((8, EH), f32)),
        grid=(row_count,),
        in_specs=[SM, pl.BlockSpec((1, EH, own_rows * H), lambda q: (q, 0, 0))] + [VM] * 5,
        out_specs=(pl.BlockSpec((1, EH, own_rows * H), lambda q: (q, 0, 0)), VM),
        scratch_shapes=[
            pltpu.VMEM((own_rows * H, LB), bf16),
            pltpu.VMEM((EH, space), f32),
            pltpu.VMEM((EH, own_rows * H), f32),
        ],
        compiler_params=pltpu.CompilerParams(vmem_limit_bytes=56 * MIB),
    )(atom_counts, w_all, src, g, hid, before, feat)
    own = lax.psum_scatter(grad_out, "row", scatter_dimension=0, tiled=False)
    own = lax.psum(own.astype(f32), "mol")
    grad_in = lax.psum(grad_in, ("mol", "row"))

    misc = shared[R_MISC:R_EBIAS]
    loss, total_count = misc[14, 0], misc[14, 1]
    lstm_rows = shared[R_LSTM:R_FIRST].reshape(4, 2 * H, H).transpose(1, 0, 2).reshape(2 * H, 4 * H)
    grad_lstm = jnp.concatenate([lstm_rows, lstm_rows[:H]], axis=0)
    grad_gru = (
        shared[R_GRU:R_SECOND].reshape(2, 3, H, H).transpose(0, 2, 1, 3).reshape(2, H, 3 * H)
    )
    grad_bias = jnp.concatenate(
        [
            grad_in[EIN],
            misc[:11].reshape(11 * H),
            misc[11, :NT],
            misc[12, :NT],
            misc[13, :NT],
        ]
    )
    ebias_rows = lax.dynamic_slice_in_dim(shared[R_EBIAS:R_END], row * own_rows, own_rows, 0)
    sums = [
        grad_in[:EIN],
        own,
        ebias_rows.reshape(own_rows * H),
        grad_gru,
        grad_lstm,
        shared[R_FIRST:R_GRU],
        shared[R_SECOND:R_MISC, :NT],
        grad_bias,
    ]
    grads = [grad / total_count for grad in sums]
    edge_squares = lax.psum(jnp.sum(grads[1] * grads[1]) + jnp.sum(grads[2] * grads[2]), "row")
    replicated = grads[0:1] + grads[3:]
    norm = jnp.sqrt(edge_squares + sum((jnp.sum(grad * grad) for grad in replicated)))
    factor = jnp.minimum(1.0, clip_norm / norm)
    params = (
        edge_in,
        edge_out,
        edge_bias,
        gru_weights,
        lstm_weights,
        head_first,
        head_second,
        biases,
    )
    moments, seconds = moments_seconds[:8], moments_seconds[8:]
    result = [
        adamw(params[index], grads[index] * factor, moments[index], seconds[index])
        for index in range(8)
    ]
    return (
        tuple(item[0] for item in result)
        + tuple(item[1] for item in result)
        + tuple(item[2] for item in result)
        + (loss, total_count, norm)
    )


def solution(mesh):
    weights = (P(), P(None, "row"), P("row"), P(), P(), P(), P(), P())
    in_specs = (
        P(("mol", "row"), None, None),
        P(None, "mol"),
        P(None, "mol", None),
        P(("mol", "row")),
        P(("mol", "row")),
        P(("mol", "row"), None),
        P(("mol", "row"), None),
    ) + weights * 3
    out_specs = weights * 3 + (P(), P(), P())
    return jax.shard_map(
        per_device, mesh=mesh, in_specs=in_specs, out_specs=out_specs, check_vma=False
    )
```

```python
import functools
import math

import jax
import jax.numpy as jnp
from jax import lax
from jax.experimental import pallas as pl
from jax.experimental.pallas import tpu as pltpu
from jax.sharding import PartitionSpec as P

H = 128
EH = 128
EIN = 5
NT = 12
STEPS = 6
ATOMS = 29
EM = 64
LAYERS = 2
STEP_COUNT = 10

PAD = 32
LIVE = 2 * (ATOMS - 1)
LB = 256
MIB = 2**20

f32 = jnp.float32
bf16 = jnp.bfloat16
highest = lax.Precision.HIGHEST
beta_one = 0.9
beta_two = 0.999
rate = 0.05
epsilon = 1e-08
decay = 0.01
clip_norm = 0.1

R_LSTM, R_FIRST, R_GRU, R_SECOND, R_MISC, R_EBIAS, R_END = 0, 1024, 1280, 2048, 2176, 2192, 2320
R_PACK = 2560
M_INPUT, M_STATE, M_LSTM, M_HEAD, M_OUT, M_SUMS = 1, 4, 7, 11, 12, 13

NN = ((1,), (0,))
NTR = ((1,), (1,))
TN = ((0,), (0,))


def mm(a, b, dims=NN):
    return lax.dot_general(a, b, (dims, ((), ())), preferred_element_type=f32)


def split(x):
    high = x.astype(bf16)
    return high, (x - high.astype(f32)).astype(bf16)


def mm3(a, b, dims=NN):
    return mm(a[0], b[0], dims) + (mm(a[0], b[1], dims) + mm(a[1], b[0], dims))


def mm2(a, b, dims=NN):
    high, low = split(a)
    return mm(high, b, dims) + mm(low, b, dims)


def columns(start, size):
    return pl.ds(pl.multiple_of(start, size), size)


def sigmoid(v):
    return jax.nn.sigmoid(v)


def body_main(
    mols,
    own_rows,
    counts_s,
    places,
    counts_col,
    flags_col,
    targets,
    present,
    tab,
    nodes,
    edge_in_t,
    b_in_col,
    w_fwd,
    w_nat,
    ebias_parts,
    gru_t,
    gru_n,
    gbias_col,
    lstm,
    c_lstm,
    first,
    c_head,
    second,
    c_out,
    offsets,
    pack,
    src_o,
    g_o,
    hid_o,
    before_o,
    feat_o,
    z,
    hot_src,
    hot_dst,
    st,
    low,
    msg,
    keep,
    acc,
    dst_acc,
    gm,
    gm_rel,
    w_back,
    w_all,
    ds_all,
):
    atoms = mols * PAD
    parts = len(w_fwd)
    total = jnp.int32(0)
    for m in range(mols):
        total = total + 2 * (counts_s[m] - 1)
    blocks = lax.div(total + (LB - 1), jnp.int32(LB))

    def place(k):
        return pl.ds(pl.multiple_of(places[k], own_rows), own_rows)

    live_col = 2.0 * (counts_col[...].astype(f32) - 1.0)
    below = (
        lax.broadcasted_iota(jnp.int32, (mols, mols), 1)
        < lax.broadcasted_iota(jnp.int32, (mols, mols), 0)
    ).astype(bf16)
    start_col = mm(below, jnp.broadcast_to(live_col, (mols, 128)).astype(bf16))[:, :1]
    e_high, e_low = split(edge_in_t[...])
    e_rest = (edge_in_t[...] - e_high.astype(f32) - e_low.astype(f32)).astype(bf16)

    def prepare(b, carry):
        c = columns(b * LB, LB)
        spot = (lax.broadcasted_iota(jnp.int32, (mols, LB), 1) + b * LB).astype(f32)
        mol_hot = ((spot >= start_col) & (spot < start_col + live_col)).astype(f32)
        rows = mm(tab[...], mol_hot.astype(bf16))
        start_row = jnp.sum(mol_hot * start_col, axis=0, keepdims=True)
        mol_row = jnp.sum(
            mol_hot * lax.broadcasted_iota(jnp.int32, (mols, LB), 0).astype(f32),
            axis=0,
            keepdims=True,
        )
        valid = jnp.sum(mol_hot, axis=0, keepdims=True)
        slot = spot[:1] - start_row
        slot_hot = (lax.broadcasted_iota(jnp.int32, (EM, LB), 0).astype(f32) == slot).astype(f32)
        picked = [
            jnp.sum(rows[r * EM : (r + 1) * EM] * slot_hot, axis=0, keepdims=True)
            for r in range(EIN + 2)
        ]
        feat = jnp.concatenate(
            picked[:EIN] + [valid, jnp.zeros((2, LB), f32)], axis=0
        )
        feat_o[:, c] = feat
        feat_low = feat.astype(bf16)
        before = (
            mm(e_high, feat_low) + mm(e_low, feat_low) + mm(e_rest, feat_low) + b_in_col[...]
        )
        before_o[:, c] = before
        hid_o[:, c] = (before * sigmoid(before)).astype(bf16)
        atom = lax.broadcasted_iota(jnp.int32, (atoms, LB), 0)
        base = mol_row * PAD
        src = jnp.where(valid > 0.5, base + picked[EIN], -1.0).astype(jnp.int32)
        dst = jnp.where(valid > 0.5, base + picked[EIN + 1], -1.0).astype(jnp.int32)
        hot_src[:, c] = (atom == src).astype(f32).astype(bf16)
        hot_dst[:, c] = (atom == dst).astype(f32).astype(bf16)
        return carry

    lax.fori_loop(0, blocks, prepare, 0)

    ebias = jnp.concatenate([part[...] for part in ebias_parts], axis=0)
    b_high, b_low = split(ebias)

    def turn(i, carry):
        for k in range(parts):
            w_back[:, pl.ds(pl.multiple_of(k * own_rows * H + i * H, H), H)] = jnp.transpose(
                w_nat[k][:, columns(i * H, H)]
            )
        return carry

    lax.fori_loop(0, own_rows, turn, 0)
    chunks = atoms // LB

    low[0] = nodes[...]
    st[0] = nodes[...].astype(f32)
    for layer in range(LAYERS):
        acc[...] = jnp.zeros_like(acc)

        def move(b, carry, layer=layer):
            c = columns(b * LB, LB)
            source = mm(low[layer], hot_src[:, c]).astype(bf16)
            src_o[layer, :, c] = source
            for h in range(EH):
                z[h * H : (h + 1) * H, :] = hid_o[pl.ds(h, 1), c] * source
            moved = mm(jnp.concatenate([part[...] for part in w_fwd], axis=0), z[...])
            moved = moved + (mm(b_high, source) + mm(b_low, source))
            acc[...] += mm2(moved, hot_dst[:, c], NTR)
            return carry

        lax.fori_loop(0, blocks, move, 0)
        for k in range(parts):
            msg[layer, place(k), :] = acc[k * own_rows : (k + 1) * own_rows, :].astype(bf16)

        def update(k, carry, layer=layer):
            c = columns(k * LB, LB)
            from_in = mm(gru_t[0], msg[layer, :, c]) + gbias_col[0]
            from_st = mm(gru_t[1], low[layer, :, c]) + gbias_col[1]
            reset = sigmoid(from_in[:H] + from_st[:H])
            upd = sigmoid(from_in[H : 2 * H] + from_st[H : 2 * H])
            fresh = jnp.tanh(from_in[2 * H :] + reset * from_st[2 * H :])
            new = (1.0 - upd) * fresh + upd * st[layer, :, c]
            st[layer + 1, :, c] = new
            if layer + 1 < LAYERS:
                low[layer + 1, :, c] = new.astype(bf16)
            keep[layer, 0, :, c] = reset
            keep[layer, 1, :, c] = upd
            keep[layer, 2, :, c] = fresh
            keep[layer, 3, :, c] = from_st[2 * H :]
            return carry

        lax.fori_loop(0, chunks, update, 0)

    lane = lax.broadcasted_iota(jnp.int32, (mols, atoms), 1)
    own = lax.broadcasted_iota(jnp.int32, (mols, atoms), 0)
    slot_of = lane - own * PAD
    alive = (slot_of >= 0) & (slot_of < counts_col[...])
    x = split(st[LAYERS])
    lstm_w = split(lstm[...])
    zeros = jnp.zeros((mols, H), f32)
    hidden, read, cell = zeros, zeros, zeros
    saved = []
    for step in range(STEPS):
        query = jnp.concatenate([hidden, read], axis=1)
        if step == 0:
            gates = jnp.broadcast_to(c_lstm[...], (mols, 4 * H))
        else:
            gates = mm3(split(query), lstm_w) + c_lstm[...]
        in_gate = sigmoid(gates[:, :H])
        forget = sigmoid(gates[:, H : 2 * H])
        part = jnp.tanh(gates[:, 2 * H : 3 * H])
        out_gate = sigmoid(gates[:, 3 * H :])
        before_cell = cell
        cell = forget * cell + in_gate * part
        squashed = jnp.tanh(cell)
        hidden = out_gate * squashed
        scores = jnp.where(alive, mm3(split(hidden), x), -1e30)
        weights = jnp.where(alive, jnp.exp(scores - jnp.max(scores, axis=1, keepdims=True)), 0.0)
        weights = weights / jnp.sum(weights, axis=1, keepdims=True)
        w_all[step * mols : (step + 1) * mols, :] = weights
        read = mm3(split(weights), x, NTR)
        saved.append((query, in_gate, forget, part, out_gate, before_cell, squashed, hidden))
    query = jnp.concatenate([hidden, read], axis=1)
    first_w = split(first[...])
    second_w = split(second[...])
    query_s = split(query)
    inner_pre = mm3(query_s, first_w) + c_head[...]
    inner_sig = sigmoid(inner_pre)
    inner = inner_pre * inner_sig
    inner_s = split(inner)
    is_one = flags_col[...] == 1
    predicted = (
        mm3(inner_s, second_w)
        + c_out[...]
        + jnp.where(is_one, offsets[1:2, :], offsets[0:1, :])
    )
    there = present[...].astype(f32)
    diff = predicted - targets[...]
    loss = jnp.sum(jnp.sum(there * diff * diff, axis=1, keepdims=True), axis=0, keepdims=True)
    count = jnp.sum(jnp.sum(there, axis=1, keepdims=True), axis=0, keepdims=True)

    d_pred = 2.0 * there * diff
    d_pred_s = split(d_pred)
    pack[R_SECOND:R_MISC, :] = jnp.zeros((H, 128), f32)
    pack[R_SECOND:R_MISC, :NT] = mm3(inner_s, d_pred_s, TN)
    misc = jnp.zeros((16, 128), f32)
    pack[R_MISC:R_EBIAS, :] = misc
    pack[R_MISC + M_OUT : R_MISC + M_OUT + 1, :NT] = jnp.sum(d_pred, axis=0, keepdims=True)
    pack[R_MISC + M_OUT : R_MISC + M_OUT + 1, NT : 2 * NT] = jnp.sum(
        jnp.where(is_one, 0.0, d_pred), axis=0, keepdims=True
    )
    pack[R_MISC + M_OUT : R_MISC + M_OUT + 1, 2 * NT : 3 * NT] = jnp.sum(
        jnp.where(is_one, d_pred, 0.0), axis=0, keepdims=True
    )
    pack[R_MISC + M_SUMS : R_MISC + M_SUMS + 1, 0:1] = loss
    pack[R_MISC + M_SUMS : R_MISC + M_SUMS + 1, 1:2] = count
    d_inner = mm3(d_pred_s, second_w, NTR)
    d_pre = d_inner * inner_sig * (1.0 + inner_pre * (1.0 - inner_sig))
    d_pre_s = split(d_pre)
    pack[R_FIRST:R_GRU, :] = mm3(query_s, d_pre_s, TN)
    pack[R_MISC + M_HEAD : R_MISC + M_HEAD + 1, :] = jnp.sum(d_pre, axis=0, keepdims=True)
    d_query = mm3(d_pre_s, first_w, NTR)
    d_hidden, d_read = d_query[:, :H], d_query[:, H:]
    d_cell = zeros
    d_gates_all = [None] * STEPS
    d_reads = [None] * STEPS
    for step in reversed(range(STEPS)):
        query, in_gate, forget, part, out_gate, before_cell, squashed, hid_t = saved[step]
        weights = w_all[step * mols : (step + 1) * mols, :]
        d_read_s = split(d_read)
        d_reads[step] = d_read
        d_weights = mm3(d_read_s, x)
        d_scores = weights * (d_weights - jnp.sum(weights * d_weights, axis=1, keepdims=True))
        ds_all[step * mols : (step + 1) * mols, :] = d_scores
        d_hidden = d_hidden + mm3(split(d_scores), x, NTR)
        d_out = d_hidden * squashed * out_gate * (1.0 - out_gate)
        d_cell = d_cell + d_hidden * out_gate * (1.0 - squashed * squashed)
        d_forget = d_cell * before_cell * forget * (1.0 - forget)
        d_in = d_cell * part * in_gate * (1.0 - in_gate)
        d_part = d_cell * in_gate * (1.0 - part * part)
        d_cell = d_cell * forget
        d_gates = jnp.concatenate([d_in, d_forget, d_part, d_out], axis=1)
        d_gates_all[step] = d_gates
        if step > 0:
            d_query = mm3(split(d_gates), lstm_w, NTR)
            d_hidden, d_read = d_query[:, :H], d_query[:, H:]
    queries = split(jnp.concatenate([saved[s][0] for s in range(STEPS)], axis=0))
    d_gates_cat = jnp.concatenate(d_gates_all, axis=0)
    d_gates_s = split(d_gates_cat)
    grad_lstm = mm3(queries, d_gates_s, TN)
    d_gates_sum = jnp.sum(d_gates_cat, axis=0, keepdims=True)
    for k in range(4):
        pack[R_LSTM + k * 256 : R_LSTM + (k + 1) * 256, :] = grad_lstm[:, k * H : (k + 1) * H]
        pack[R_MISC + M_LSTM + k : R_MISC + M_LSTM + k + 1, :] = d_gates_sum[:, k * H : (k + 1) * H]
    left = jnp.concatenate(d_reads + [saved[s][7] for s in range(STEPS)], axis=0)
    left_s = split(left)

    def spread(k, carry):
        c = columns(k * LB, LB)
        right = split(jnp.concatenate([w_all[:, c], ds_all[:, c]], axis=0))
        dst_acc[:, c] = mm3(left_s, right, TN)
        return carry

    lax.fori_loop(0, chunks, spread, 0)

    pack[R_GRU:R_SECOND, :] = jnp.zeros((6 * H, 128), f32)
    for layer in reversed(range(LAYERS)):

        def back(k, carry, layer=layer):
            c = columns(k * LB, LB)
            d_state = dst_acc[:, c]
            reset, upd = keep[layer, 0, :, c], keep[layer, 1, :, c]
            fresh, from_st = keep[layer, 2, :, c], keep[layer, 3, :, c]
            d_upd = d_state * (st[layer, :, c] - fresh) * upd * (1.0 - upd)
            d_fresh = d_state * (1.0 - upd) * (1.0 - fresh * fresh)
            d_reset = d_fresh * from_st * reset * (1.0 - reset)
            d_from_in = jnp.concatenate([d_reset, d_upd, d_fresh], axis=0)
            d_from_st = jnp.concatenate([d_reset, d_upd, d_fresh * reset], axis=0)
            in_s, st_s = split(d_from_in), split(d_from_st)
            gm[:, c] = (mm(gru_n[0], in_s[0]) + mm(gru_n[0], in_s[1])).astype(bf16)
            if layer > 0:
                dst_acc[:, c] = d_state * upd + (mm(gru_n[1], st_s[0]) + mm(gru_n[1], st_s[1]))
            ones = jnp.ones((8, LB), bf16)
            message, state_low = msg[layer, :, c], low[layer, :, c]
            for half, left_m, right_m in ((0, message, in_s), (1, state_low, st_s)):
                grad = mm(left_m, right_m[0], NTR) + mm(left_m, right_m[1], NTR)
                sums = (mm(ones, right_m[0], NTR) + mm(ones, right_m[1], NTR))[:1]
                for q in range(3):
                    r = R_GRU + (half * 3 + q) * H
                    pack[r : r + H, :] += grad[:, q * H : (q + 1) * H]
                    m = R_MISC + M_INPUT + half * 3 + q
                    pack[m : m + 1, :] += sums[:, q * H : (q + 1) * H]
            return carry

        lax.fori_loop(0, chunks, back, 0)
        for k in range(parts):
            gm_rel[k * own_rows : (k + 1) * own_rows, :] = gm[place(k), :]
        if layer > 0:
            bt_high, bt_low = split(jnp.transpose(ebias))

            def pull(b, carry, layer=layer):
                c = columns(b * LB, LB)
                grad = mm(gm_rel[...], hot_dst[:, c])
                grad_low = grad.astype(bf16)
                g_o[layer, :, c] = grad_low
                hid = hid_o[:, c]
                for i in range(H):
                    z[i * EH : (i + 1) * EH, :] = g_o[layer, pl.ds(i, 1), c] * hid
                pulled = mm(w_back[...], z[...])
                pulled = pulled + (mm(bt_high, grad_low) + mm(bt_low, grad_low))
                dst_acc[...] += mm2(pulled, hot_src[:, c], NTR)
                return carry

            lax.fori_loop(0, blocks, pull, 0)
        else:

            def take(b, carry, layer=layer):
                c = columns(b * LB, LB)
                g_o[layer, :, c] = mm(gm_rel[...], hot_dst[:, c]).astype(bf16)
                return carry

            lax.fori_loop(0, blocks, take, 0)
    acc_b = acc.at[:, :H]
    acc_b[...] = jnp.zeros((H, H), f32)

    def bias_sum(b, carry):
        c = columns(b * LB, LB)
        acc_b[...] += mm(g_o[0, :, c], src_o[0, :, c], NTR) + mm(
            g_o[1, :, c], src_o[1, :, c], NTR
        )
        return carry

    lax.fori_loop(0, blocks, bias_sum, 0)
    for k in range(parts):
        row = pl.multiple_of(R_EBIAS + places[k], 8)
        pack[pl.ds(row, own_rows), :] = acc_b[k * own_rows : (k + 1) * own_rows, :]
    pack[R_END:R_PACK, :] = jnp.zeros((R_PACK - R_END, 128), f32)


def body_edges(mols, rels, last, counts_s, *refs):
    n = len(rels)
    ws, (src, g, hid) = refs[:n], refs[n : n + 3]
    if last:
        hid_before, before, feat = refs[n + 3 : n + 6]
        outs, grad_in = refs[n + 6 : 2 * n + 6], refs[2 * n + 6]
        built, acc, grad_hid = refs[2 * n + 7 :]
    else:
        outs, grad_hid = refs[n + 3 : 2 * n + 3], refs[2 * n + 3]
        built, acc = refs[2 * n + 4 :]
    total = jnp.int32(0)
    for m in range(mols):
        total = total + 2 * (counts_s[m] - 1)
    blocks = lax.div(total + (LB - 1), jnp.int32(LB))
    rows = ws[0].shape[1] // H

    for q, rel in enumerate(rels):
        acc[...] = jnp.zeros_like(acc)

        def edges(b, carry, q=q, rel=rel):
            c = columns(b * LB, LB)
            g0 = g[0, rel * rows : (rel + 1) * rows, c].astype(f32)
            g1 = g[1, rel * rows : (rel + 1) * rows, c].astype(f32)
            s0, s1 = src[0, :, c].astype(f32), src[1, :, c].astype(f32)
            for i in range(rows):
                built[i * H : (i + 1) * H, :] = (g0[i : i + 1] * s0 + g1[i : i + 1] * s1).astype(
                    bf16
                )
            pulled = mm(ws[q][...], built[...])
            if q > 0:
                grad_hid[:, c] += pulled
            elif last:
                grad_hid[:, c] = hid_before[:, c] + pulled
            else:
                grad_hid[:, c] = pulled
            acc[...] += mm(hid[:, c], built[...], NTR)
            return carry

        lax.fori_loop(0, blocks, edges, 0)
        outs[q][...] = acc[...].astype(outs[q].dtype)

    if last:
        grad_in[...] = jnp.zeros_like(grad_in)

        def finish(b, carry):
            c = columns(b * LB, LB)
            ahead = before[:, c]
            sig = sigmoid(ahead)
            grad = split(grad_hid[:, c] * sig * (1.0 + ahead * (1.0 - sig)))
            rows_low = feat[:, c].astype(bf16)
            grad_in[...] += mm(rows_low, grad[0], NTR) + mm(rows_low, grad[1], NTR)
            return carry

        lax.fori_loop(0, blocks, finish, 0)


def adamw(weight, grad, moment, second):
    moment_new = beta_one * moment + (1.0 - beta_one) * grad
    second_new = beta_two * second + (1.0 - beta_two) * grad * grad
    mean_hat = moment_new / (1.0 - beta_one**STEP_COUNT)
    square_hat = second_new / (1.0 - beta_two**STEP_COUNT)
    return (
        weight - rate * (mean_hat / (jnp.sqrt(square_hat) + epsilon) + decay * weight),
        moment_new,
        second_new,
    )


def squares(x):
    return jnp.sum(jnp.sum(x * x, axis=1, keepdims=True), axis=0, keepdims=True)


def body_adamw(own_rows, place, own, pack, grad_in, edge_squares, *refs):
    params, moments, seconds = refs[0:8], refs[8:16], refs[16:24]
    outs = refs[24:48]
    loss, count, norm, scale = refs[48:52]

    def step(index, grad, at=...):
        new = adamw(params[index][at], grad, moments[index][at], seconds[index][at])
        for kind in range(3):
            outs[kind * 8 + index][at] = new[kind]

    @pl.when(pl.program_id(0) == 0)
    def _():
        sums = pack[R_MISC + M_SUMS : R_MISC + M_SUMS + 1, :]
        total = (
            edge_squares[:, 0:1]
            + squares(grad_in[: EIN + 1, :])
            + squares(pack[: R_MISC + M_SUMS, :])
            + squares(pack[R_EBIAS:R_END, :])
        )
        for k in range(4):
            total = total + squares(pack[R_LSTM + k * 2 * H : R_LSTM + k * 2 * H + H, :])
        loss[...] = sums[:, 0:1]
        count[...] = sums[:, 1:2]
        grad_norm = jnp.sqrt(total) / sums[:, 1:2]
        norm[...] = grad_norm
        factor = jnp.minimum(1.0, clip_norm / grad_norm) / sums[:, 1:2]
        scale[...] = jnp.broadcast_to(factor, scale.shape)
        step(0, grad_in[:EIN, :] * factor)
        step(2, pack[pl.ds(pl.multiple_of(R_EBIAS + place[0], 8), own_rows), :] * factor)
        for half in range(2):
            for q in range(3):
                r = R_GRU + (half * 3 + q) * H
                step(3, pack[r : r + H, :] * factor, (half, slice(None), slice(q * H, (q + 1) * H)))
        for k in range(4):
            r = R_LSTM + k * 2 * H
            for block, start in ((0, 0), (1, H), (2, 0)):
                step(
                    4,
                    pack[r + start : r + start + H, :] * factor,
                    (slice(block * H, (block + 1) * H), slice(k * H, (k + 1) * H)),
                )
        step(5, pack[R_FIRST:R_GRU, :] * factor)
        step(6, pack[R_SECOND:R_MISC, :NT] * factor)
        bias = jnp.concatenate([grad_in[EIN : EIN + 1, :], pack[R_MISC + 1 : R_EBIAS, :]], axis=0)
        step(7, bias * factor)

    step(1, own[...] * scale[0:1, 0:1])


def split_biases(biases):
    start = 0
    pieces = []
    for width in (EH, 6 * H, 4 * H, H, NT, 2 * NT):
        pieces.append(biases[start : start + width])
        start = start + width
    return pieces


VM = pl.BlockSpec(memory_space=pltpu.VMEM)
SM = pl.BlockSpec(memory_space=pltpu.SMEM)


def per_device(
    node_feats,
    edge_feats,
    edge_ends,
    atom_counts,
    dataset_flags,
    targets,
    present,
    edge_in,
    edge_out,
    edge_bias,
    gru_weights,
    lstm_weights,
    head_first,
    head_second,
    biases,
    *moments_seconds,
):
    row = lax.axis_index("row")
    row_count = lax.axis_size("row")
    mol = lax.axis_index("mol")
    mol_bits = lax.axis_size("mol").bit_length() - 1
    row_bits = row_count.bit_length() - 1
    mols = node_feats.shape[0]
    own_rows = edge_out.shape[1] // H
    atoms = mols * PAD
    space = -(-mols * LIVE // LB) * LB
    b_in, b_gru, c_lstm, c_head, c_out, offsets = split_biases(biases)

    def row_swap(x, k):
        return lax.ppermute(x, "row", [(i, i ^ k) for i in range(row_count)])

    def mol_swap(x, bit):
        return lax.ppermute(x, "mol", [(i, i ^ (1 << bit)) for i in range(2**mol_bits)])

    def halve(x, swap, bit, send_type):
        halves = x.reshape((2, x.shape[0] // 2) + x.shape[1:])
        sent = lax.dynamic_index_in_dim(halves, 1 - bit, 0, False).astype(send_type)
        kept = lax.dynamic_index_in_dim(halves, bit, 0, False)
        return kept + swap(sent).astype(f32)

    def double(x, swap, bit):
        other = swap(x)
        return jnp.concatenate(
            [jnp.where(bit == 0, x, other), jnp.where(bit == 0, other, x)], axis=0
        )

    out_low = edge_out.astype(bf16)
    parts, bias_parts = [out_low], [edge_bias.reshape(own_rows, H)]
    for bit in range(row_bits):
        for k in range(1 << bit):
            parts.append(row_swap(parts[k], 1 << bit))
            bias_parts.append(row_swap(bias_parts[k], 1 << bit))
    places = jnp.stack([(row ^ k) * own_rows for k in range(row_count)]).astype(jnp.int32)
    w_fwd = [
        part.reshape(EH, own_rows, H).transpose(1, 0, 2).reshape(own_rows, EH * H)
        for part in parts
    ]

    ends = lax.dynamic_slice_in_dim(edge_ends, row * mols, mols, 1)
    feats = lax.dynamic_slice_in_dim(edge_feats, row * mols * EM, mols * EM, 1)
    tab = jnp.concatenate(
        [
            feats.reshape(EIN, mols, EM),
            ends.astype(bf16),
            jnp.zeros((1, mols, EM), bf16),
        ],
        axis=0,
    )
    tab = tab.transpose(0, 2, 1).reshape(8 * EM, mols)
    nodes = jnp.pad(node_feats, ((0, 0), (0, PAD - ATOMS), (0, 0))).reshape(atoms, H).T
    gru_low = gru_weights.astype(bf16)
    lstm = jnp.concatenate([lstm_weights[:H] + lstm_weights[2 * H :], lstm_weights[H : 2 * H]], 0)
    edge_in_t = jnp.pad(edge_in, ((0, 3), (0, 0))).T

    sds = jax.ShapeDtypeStruct
    n = row_count

    def main(*refs):
        at = 10
        body_main(
            mols,
            own_rows,
            *refs[:at],
            refs[at : at + n],
            refs[at + n : at + 2 * n],
            refs[at + 2 * n : at + 3 * n],
            *refs[at + 3 * n :],
        )

    pack, src, g, hid, before, feat = pl.pallas_call(
        main,
        out_shape=(
            sds((R_PACK, 128), f32),
            sds((LAYERS, H, space), bf16),
            sds((LAYERS, H, space), bf16),
            sds((EH, space), bf16),
            sds((EH, space), f32),
            sds((8, space), f32),
        ),
        in_specs=[SM, SM] + [VM] * (18 + 3 * n),
        out_specs=(VM,) * 6,
        scratch_shapes=[
            pltpu.VMEM((H * EH, LB), bf16),
            pltpu.VMEM((atoms, space), bf16),
            pltpu.VMEM((atoms, space), bf16),
            pltpu.VMEM((LAYERS + 1, H, atoms), f32),
            pltpu.VMEM((LAYERS, H, atoms), bf16),
            pltpu.VMEM((LAYERS, H, atoms), bf16),
            pltpu.VMEM((LAYERS, 4, H, atoms), f32),
            pltpu.VMEM((H, atoms), f32),
            pltpu.VMEM((H, atoms), f32),
            pltpu.VMEM((H, atoms), bf16),
            pltpu.VMEM((H, atoms), bf16),
            pltpu.VMEM((H, H * EH), bf16),
            pltpu.VMEM((STEPS * mols, atoms), f32),
            pltpu.VMEM((STEPS * mols, atoms), f32),
        ],
        compiler_params=pltpu.CompilerParams(vmem_limit_bytes=60 * MIB),
    )(
        atom_counts,
        places,
        atom_counts.reshape(mols, 1),
        dataset_flags.reshape(mols, 1),
        targets,
        present,
        tab,
        nodes,
        edge_in_t,
        b_in.reshape(EH, 1),
        *w_fwd,
        *parts,
        *bias_parts,
        gru_low.transpose(0, 2, 1),
        gru_low,
        b_gru.reshape(2, 3 * H, 1),
        lstm,
        c_lstm.reshape(1, 4 * H),
        head_first,
        c_head.reshape(1, H),
        head_second,
        c_out.reshape(1, NT),
        offsets.reshape(2, NT),
    )

    far, near = tuple(range(n // 2, n)), tuple(range(n // 2))
    part_scratch = [pltpu.VMEM((own_rows * H, LB), bf16), pltpu.VMEM((EH, own_rows * H), f32)]
    params = pltpu.CompilerParams(vmem_limit_bytes=56 * MIB)
    part_shape = sds((EH, own_rows * H), bf16)
    *far_parts, grad_hid = pl.pallas_call(
        functools.partial(body_edges, mols, far, False),
        out_shape=(part_shape,) * len(far) + (sds((EH, space), f32),),
        in_specs=[SM] + [VM] * (len(far) + 3),
        out_specs=(VM,) * (len(far) + 1),
        scratch_shapes=part_scratch,
        compiler_params=params,
    )(atom_counts, *(parts[k] for k in far), src, g, hid)
    *near_parts, grad_in = pl.pallas_call(
        functools.partial(body_edges, mols, near, True),
        out_shape=(part_shape,) * len(near) + (sds((8, EH), f32),),
        in_specs=[SM] + [VM] * (len(near) + 6),
        out_specs=(VM,) * (len(near) + 1),
        scratch_shapes=part_scratch + [pltpu.VMEM((EH, space), f32)],
        compiler_params=params,
    )(atom_counts, *(parts[k] for k in near), src, g, hid, grad_hid, before, feat)

    row_bit = [(row >> bit) & 1 for bit in range(row_bits)]
    mol_bit = [(mol >> bit) & 1 for bit in range(mol_bits)]
    steps = [
        (functools.partial(row_swap, k=1 << bit), row_bit[bit]) for bit in range(row_bits)
    ] + [(functools.partial(mol_swap, bit=bit), mol_bit[bit]) for bit in range(mol_bits)]
    for swap, bit in steps:
        pack = halve(pack, swap, bit, f32)
    for swap, bit in reversed(steps):
        pack = double(pack, swap, bit)
    for swap, bit in steps:
        grad_in = grad_in + swap(grad_in)

    slots = near_parts + far_parts
    for bit in reversed(range(row_bits)):
        k = 1 << bit
        slots = [
            slots[i].astype(f32) + row_swap(slots[i + k].astype(bf16), k).astype(f32)
            for i in range(k)
        ]
    own = slots[0]
    mol_steps = steps[row_bits:]
    for swap, bit in mol_steps:
        own = halve(own, swap, bit, bf16)
    largest = jnp.maximum(jnp.max(jnp.abs(own)), 1e-30)
    note = jnp.concatenate(
        [jnp.sum(own * own).reshape(1, 1), largest.reshape(1, 1), jnp.zeros((1, 126), f32)], axis=1
    )
    own = (own * (16384.0 / largest)).astype(jnp.float16)
    for swap, bit in reversed(mol_steps):
        own = double(own, swap, bit)
        note = double(note, swap, bit)
    pieces = note.shape[0]
    own = own.astype(f32).reshape(pieces, -1) * (note[:, 1:2] * (1.0 / 16384.0))
    own = own.reshape(EH, own_rows * H)
    edge_squares = jnp.broadcast_to(jnp.sum(note[:, 0]), (1, 128))
    for swap, bit in steps[:row_bits]:
        edge_squares = edge_squares + swap(edge_squares)

    weights = [
        edge_in,
        edge_out,
        edge_bias,
        gru_weights,
        lstm_weights,
        head_first,
        head_second,
        biases,
    ]
    states = []
    for group in (weights, moments_seconds[:8], moments_seconds[8:]):
        group = list(group)
        group[2] = group[2].reshape(own_rows, H)
        group[7] = jnp.pad(group[7], (0, 16 * 128 - group[7].shape[0])).reshape(16, 128)
        states += group
    grid = 4
    block = pl.BlockSpec((EH // grid, own_rows * H), lambda i: (i, 0))

    def state_specs():
        return [block if index == 1 else VM for index in range(8)] * 3

    shapes = [sds(state.shape, f32) for state in states]
    results = pl.pallas_call(
        functools.partial(body_adamw, own_rows),
        grid=(grid,),
        out_shape=tuple(shapes) + (sds((1, 1), f32),) * 3,
        in_specs=[SM, block, VM, VM, VM] + state_specs(),
        out_specs=tuple(state_specs()) + (VM,) * 3,
        scratch_shapes=[pltpu.VMEM((8, 128), f32)],
        compiler_params=params,
    )(places, own, pack, grad_in, edge_squares, *states)
    results = list(results)
    for kind in range(3):
        results[kind * 8 + 2] = results[kind * 8 + 2].reshape(own_rows * H)
        results[kind * 8 + 7] = results[kind * 8 + 7].reshape(-1)[: biases.shape[0]]
    for index in range(24, 27):
        results[index] = results[index].reshape(())
    return tuple(results)


def solution(mesh):
    weights = (P(), P(None, "row"), P("row"), P(), P(), P(), P(), P())
    in_specs = (
        P(("mol", "row"), None, None),
        P(None, "mol"),
        P(None, "mol", None),
        P(("mol", "row")),
        P(("mol", "row")),
        P(("mol", "row"), None),
        P(("mol", "row"), None),
    ) + weights * 3
    out_specs = weights * 3 + (P(), P(), P())
    return jax.shard_map(
        per_device, mesh=mesh, in_specs=in_specs, out_specs=out_specs, check_vma=False
    )
```

```python
import functools
import math

import jax
import jax.numpy as jnp
from jax import lax
from jax.experimental import pallas as pl
from jax.experimental.pallas import tpu as pltpu
from jax.sharding import PartitionSpec as P

H = 128
EH = 128
EIN = 5
NT = 12
STEPS = 6
ATOMS = 29
EM = 64
LAYERS = 2
STEP_COUNT = 10

PAD = 32
LIVE = 2 * (ATOMS - 1)
LB = 256
MIB = 2**20

f32 = jnp.float32
bf16 = jnp.bfloat16
highest = lax.Precision.HIGHEST
beta_one = 0.9
beta_two = 0.999
rate = 0.05
epsilon = 1e-08
decay = 0.01
clip_norm = 0.1

R_LSTM, R_FIRST, R_GRU, R_SECOND, R_MISC, R_EBIAS, R_END = 0, 1024, 1280, 2048, 2064, 2080, 2208
R_PACK = 2560
M_INPUT, M_LSTM, M_HEAD, M_OUT = 1, 7, 11, 12
G_BIAS, G_SUMS = EIN, EIN + 1
WINDOW = 384
CHUNKS = 2

NN = ((1,), (0,))
NTR = ((1,), (1,))
TN = ((0,), (0,))


def mm(a, b, dims=NN):
    return lax.dot_general(a, b, (dims, ((), ())), preferred_element_type=f32)


def split(x):
    high = x.astype(bf16)
    return high, (x - high.astype(f32)).astype(bf16)


def mm3(a, b, dims=NN):
    return mm(a[0], b[0], dims) + (mm(a[0], b[1], dims) + mm(a[1], b[0], dims))


def mm2(a, b, dims=NN):
    high, low = split(a)
    return mm(high, b, dims) + mm(low, b, dims)


def total_of(x):
    return jnp.sum(jnp.sum(x, axis=1, keepdims=True), axis=0, keepdims=True)


def columns(start, size):
    return pl.ds(pl.multiple_of(start, size), size)


def sigmoid(v):
    return jax.nn.sigmoid(v)


def column_of(values, size):
    at = lax.broadcasted_iota(jnp.int32, (size, 1), 0)
    found = jnp.zeros((size, 1), jnp.int32)
    for m in range(size):
        found = jnp.where(at == m, values[m], found)
    return found


def row_of(values, size):
    at = lax.broadcasted_iota(jnp.int32, (1, size), 1)
    found = jnp.zeros((1, size), jnp.int32)
    for m in range(size):
        found = jnp.where(at == m, values[m], found)
    return found


def starts_of(column, size):
    below = (
        lax.broadcasted_iota(jnp.int32, (size, size), 1)
        < lax.broadcasted_iota(jnp.int32, (size, size), 0)
    ).astype(bf16)
    return mm(below, jnp.broadcast_to(column, (size, 128)).astype(bf16))[:, :1]


def body_prepare(
    mols,
    counts_s,
    table,
    node_feats,
    edge_in,
    bias_rows,
    meta,
    nodes_o,
    hid_o,
    before_o,
    feat_o,
    hot_src,
    hot_dst,
    square,
    flat,
):
    lanes = nodes_o.shape[1]
    space = hid_o.shape[1]
    for b in range(space // LB):
        meta[2 + b] = jnp.int32(0)
    edges, atoms = jnp.int32(0), jnp.int32(0)
    for m in range(mols):
        live = 2 * (counts_s[m] - 1)
        block = lax.div(edges + (LB - 1), jnp.int32(LB))

        @pl.when(block * LB < edges + live)
        def _(block=block, atoms=atoms):
            meta[2 + block] = lax.div(atoms, jnp.int32(128)) * 128

        edges = edges + live
        atoms = atoms + counts_s[m]
    blocks = lax.div(edges + (LB - 1), jnp.int32(LB))
    meta[0] = blocks
    meta[1] = lax.div(atoms + (LB - 1), jnp.int32(LB))

    count_col = column_of(counts_s, mols).astype(f32)
    live_col = 2.0 * (count_col - 1.0)
    start_col = starts_of(live_col, mols)
    atom_col = starts_of(count_col, mols)

    square[...] = jnp.zeros_like(square)
    square[0:EIN, :] = edge_in[...]
    square[8:24, :] = bias_rows[...]
    turned = jnp.transpose(square[...])
    in_t, b_in_col = turned[:, :8], turned[:, 8:9]
    e_high, e_low = split(in_t)
    e_rest = (in_t - e_high.astype(f32) - e_low.astype(f32)).astype(bf16)

    flat[...] = jnp.zeros_like(flat)
    for m in range(mols):
        flat[m * PAD : m * PAD + ATOMS, :] = node_feats[m].astype(f32)
    flat_low = flat[...].astype(bf16)
    nodes_o[...] = jnp.zeros_like(nodes_o)
    atom_at = lax.broadcasted_iota(jnp.int32, (mols * PAD, 1), 0)
    spread = (
        lax.broadcasted_iota(jnp.int32, (mols * PAD, mols), 0) // PAD
        == lax.broadcasted_iota(jnp.int32, (mols * PAD, mols), 1)
    ).astype(bf16)
    goal_high = jnp.floor(atom_col * (1.0 / 8.0))
    goal_parts = jnp.concatenate([goal_high, atom_col - 8.0 * goal_high, count_col], axis=1)
    goal = mm(
        spread,
        jnp.concatenate([goal_parts, jnp.zeros((mols, 125), f32)], axis=1).astype(bf16),
    )
    within = lax.rem(atom_at, jnp.int32(PAD)).astype(f32)
    target = jnp.where(
        within < goal[:, 2:3], 8.0 * goal[:, 0:1] + goal[:, 1:2] + within, -1.0
    ).astype(jnp.int32)

    def pack_atoms(k, carry):
        c = columns(k * LB, LB)
        at = lax.broadcasted_iota(jnp.int32, (mols * PAD, LB), 1) + k * LB
        hot = (at == target).astype(f32).astype(bf16)
        nodes_o[:, c] = mm(flat_low, hot, TN).astype(bf16)
        return carry

    lax.fori_loop(0, meta[1], pack_atoms, 0)

    def prepare(b, carry):
        c = columns(b * LB, LB)
        spot = (lax.broadcasted_iota(jnp.int32, (mols, LB), 1) + b * LB).astype(f32)
        mol_hot = ((spot >= start_col) & (spot < start_col + live_col)).astype(f32)
        rows = mm(table[...], mol_hot.astype(bf16), TN)
        start_row = jnp.sum(mol_hot * start_col, axis=0, keepdims=True)
        base = jnp.sum(mol_hot * atom_col, axis=0, keepdims=True)
        valid = jnp.sum(mol_hot, axis=0, keepdims=True)
        slot = spot[:1] - start_row
        slot_hot = (lax.broadcasted_iota(jnp.int32, (EM, LB), 0).astype(f32) == slot).astype(f32)
        picked = [
            jnp.sum(rows[r * EM : (r + 1) * EM] * slot_hot, axis=0, keepdims=True)
            for r in range(EIN + 2)
        ]
        feat = jnp.concatenate(picked[:EIN] + [valid, jnp.zeros((2, LB), f32)], axis=0)
        feat_o[:, c] = feat
        feat_low = feat.astype(bf16)
        before = mm(e_high, feat_low) + mm(e_low, feat_low) + mm(e_rest, feat_low) + b_in_col
        before_o[:, c] = before
        hid_o[:, c] = (before * sigmoid(before)).astype(bf16)
        atom = lax.broadcasted_iota(jnp.int32, (WINDOW, LB), 0)
        base = base - meta[2 + b].astype(f32)
        src = jnp.where(valid > 0.5, base + picked[EIN], -1.0).astype(jnp.int32)
        dst = jnp.where(valid > 0.5, base + picked[EIN + 1], -1.0).astype(jnp.int32)
        hot_src[:, c] = (atom == src).astype(f32).astype(bf16)
        hot_dst[:, c] = (atom == dst).astype(f32).astype(bf16)
        return carry

    lax.fori_loop(0, blocks, prepare, 0)


def body_main(
    mols,
    own_rows,
    counts_s,
    flags_s,
    places,
    meta,
    targets,
    present,
    nodes,
    hid_i,
    hot_src,
    hot_dst,
    w_fwd,
    w_nat,
    ebias_parts,
    gru,
    bias_rows,
    lstm_rows,
    first,
    second,
    pack,
    sums_o,
    src_o,
    g_o,
    z,
    st,
    low,
    msg,
    keep,
    acc,
    dst_acc,
    gm,
    gm_rel,
    w_back,
    w_all,
    ds_all,
    gru_n,
    gru_t,
    square,
):
    parts = len(w_fwd)
    blocks, chunks = meta[0], meta[1]
    atoms = w_all.shape[1]

    def place(k):
        return pl.ds(pl.multiple_of(places[k], own_rows), own_rows)

    def window(b):
        return pl.ds(pl.multiple_of(meta[2 + b], 128), WINDOW)

    square[...] = jnp.zeros_like(square)
    square[0:16, :] = bias_rows[...]
    turned = jnp.transpose(square[...])
    gbias_col = [
        jnp.concatenate([turned[:, r + q : r + q + 1] for q in range(3)], axis=0)
        for r in (M_INPUT, M_INPUT + 3)
    ]
    c_lstm = jnp.concatenate(
        [bias_rows[M_LSTM + k : M_LSTM + k + 1, :] for k in range(4)], axis=1
    )
    c_head = bias_rows[M_HEAD : M_HEAD + 1, :]
    out_cols = [turned[k * NT : (k + 1) * NT, M_OUT : M_OUT + 1] for k in range(3)]
    gru_n[...] = gru[...].astype(bf16)
    for half in range(2):
        for q in range(3):
            gru_t[half, q * H : (q + 1) * H, :] = jnp.transpose(
                gru_n[half, :, q * H : (q + 1) * H]
            )
    ebias = jnp.concatenate([part[...] for part in ebias_parts], axis=0)
    b_high, b_low = split(ebias)

    def turn(i, carry):
        for k in range(parts):
            w_back[:, pl.ds(pl.multiple_of(k * own_rows * H + i * H, H), H)] = jnp.transpose(
                w_nat[k][:, columns(i * H, H)]
            )
        return carry

    lax.fori_loop(0, own_rows, turn, 0)

    for layer in range(LAYERS):
        low[layer] = jnp.zeros_like(low[layer])
    low[0, :, :atoms] = nodes[...]
    st[0] = nodes[...].astype(f32)
    st[LAYERS] = jnp.zeros_like(st[LAYERS])
    gm_rel[...] = jnp.zeros_like(gm_rel)
    for layer in range(LAYERS):
        acc[...] = jnp.zeros_like(acc)

        def move(b, carry, layer=layer):
            c, w = columns(b * LB, LB), window(b)
            source = mm(low[layer, :, w], hot_src[:, c]).astype(bf16)
            src_o[layer, :, c] = source
            for h in range(EH):
                z[h * H : (h + 1) * H, :] = hid_i[pl.ds(h, 1), c] * source
            moved = mm(jnp.concatenate([part[...] for part in w_fwd], axis=0), z[...])
            moved = moved + (mm(b_high, source) + mm(b_low, source))
            acc[:, w] += mm2(moved, hot_dst[:, c], NTR)
            return carry

        lax.fori_loop(0, blocks, move, 0)
        for k in range(parts):
            msg[layer, place(k), :] = acc[k * own_rows : (k + 1) * own_rows, :atoms].astype(bf16)

        def update(k, carry, layer=layer):
            c = columns(k * LB, LB)
            from_in = mm(gru_t[0], msg[layer, :, c]) + gbias_col[0]
            from_st = mm(gru_t[1], low[layer, :, c]) + gbias_col[1]
            reset = sigmoid(from_in[:H] + from_st[:H])
            upd = sigmoid(from_in[H : 2 * H] + from_st[H : 2 * H])
            fresh = jnp.tanh(from_in[2 * H :] + reset * from_st[2 * H :])
            new = (1.0 - upd) * fresh + upd * st[layer, :, c]
            st[layer + 1, :, c] = new
            if layer + 1 < LAYERS:
                low[layer + 1, :, c] = new.astype(bf16)
            keep[layer, 0, :, c] = reset
            keep[layer, 1, :, c] = upd
            keep[layer, 2, :, c] = fresh
            keep[layer, 3, :, c] = from_st[2 * H :]
            return carry

        lax.fori_loop(0, chunks, update, 0)

    lane = lax.broadcasted_iota(jnp.int32, (mols, atoms), 1).astype(f32)
    count_col = column_of(counts_s, mols).astype(f32)
    slot_of = lane - starts_of(count_col, mols)
    alive = (slot_of >= 0.0) & (slot_of < count_col)
    x = split(st[LAYERS])
    lstm = jnp.concatenate(
        [lstm_rows[0:H, :] + lstm_rows[2 * H : 3 * H, :], lstm_rows[H : 2 * H, :]], axis=0
    )
    lstm_w = split(lstm)
    zeros = jnp.zeros((mols, H), f32)
    hidden, read, cell = zeros, zeros, zeros
    saved = []
    for step in range(STEPS):
        query = jnp.concatenate([hidden, read], axis=1)
        if step == 0:
            gates = jnp.broadcast_to(c_lstm, (mols, 4 * H))
        else:
            gates = mm3(split(query), lstm_w) + c_lstm
        in_gate = sigmoid(gates[:, :H])
        forget = sigmoid(gates[:, H : 2 * H])
        part = jnp.tanh(gates[:, 2 * H : 3 * H])
        out_gate = sigmoid(gates[:, 3 * H :])
        before_cell = cell
        cell = forget * cell + in_gate * part
        squashed = jnp.tanh(cell)
        hidden = out_gate * squashed
        scores = jnp.where(alive, mm3(split(hidden), x), -1e30)
        weights = jnp.where(alive, jnp.exp(scores - jnp.max(scores, axis=1, keepdims=True)), 0.0)
        weights = weights / jnp.sum(weights, axis=1, keepdims=True)
        w_all[step * mols : (step + 1) * mols, :] = weights
        read = mm3(split(weights), x, NTR)
        saved.append((query, in_gate, forget, part, out_gate, before_cell, squashed, hidden))
    query = jnp.concatenate([hidden, read], axis=1)
    first_w = split(first[...])
    second_w = split(second[...])
    query_s = split(query)
    inner_pre = mm3(query_s, first_w) + c_head
    inner_sig = sigmoid(inner_pre)
    inner = inner_pre * inner_sig
    inner_s = split(inner)
    is_one = row_of(flags_s, mols) == 1
    predicted = (
        mm3(second_w, inner_s, NTR)
        + out_cols[0]
        + jnp.where(is_one, out_cols[2], out_cols[1])
    )
    there = present[...].astype(f32)
    diff = predicted - targets[...]
    lanes = lax.broadcasted_iota(jnp.int32, (1, 128), 1)
    loss = total_of(there * diff * diff)
    count = total_of(there)
    sums_o[...] = jnp.zeros_like(sums_o)
    sums_o[G_SUMS : G_SUMS + 1, :] = jnp.where(lanes == 0, loss, jnp.where(lanes == 1, count, 0.0))

    d_pred = 2.0 * there * diff
    d_pred_s = split(d_pred)
    pack[R_SECOND:R_MISC, :] = jnp.zeros((R_MISC - R_SECOND, 128), f32)
    pack[R_SECOND : R_SECOND + NT, :] = mm3(d_pred_s, inner_s)
    pack[R_MISC:R_EBIAS, :] = jnp.zeros((R_EBIAS - R_MISC, 128), f32)
    zero_pred = jnp.where(is_one, 0.0, d_pred)
    out_sums = jnp.concatenate([d_pred, zero_pred, d_pred - zero_pred], axis=0)
    out_high, out_low = split(out_sums)
    out_ones = jnp.ones((8, mols), bf16)
    pack[R_MISC + M_OUT : R_MISC + M_OUT + 1, : 3 * NT] = (
        mm(out_ones, out_high, NTR) + mm(out_ones, out_low, NTR)
    )[:1]
    d_inner = mm3(d_pred_s, second_w, TN)
    d_pre = d_inner * inner_sig * (1.0 + inner_pre * (1.0 - inner_sig))
    d_pre_s = split(d_pre)
    pack[R_FIRST:R_GRU, :] = mm3(query_s, d_pre_s, TN)
    pack[R_MISC + M_HEAD : R_MISC + M_HEAD + 1, :] = jnp.sum(d_pre, axis=0, keepdims=True)
    d_query = mm3(d_pre_s, first_w, NTR)
    d_hidden, d_read = d_query[:, :H], d_query[:, H:]
    d_cell = zeros
    d_gates_all = [None] * STEPS
    d_reads = [None] * STEPS
    for step in reversed(range(STEPS)):
        query, in_gate, forget, part, out_gate, before_cell, squashed, hid_t = saved[step]
        weights = w_all[step * mols : (step + 1) * mols, :]
        d_read_s = split(d_read)
        d_reads[step] = d_read
        d_weights = mm3(d_read_s, x)
        d_scores = weights * (d_weights - jnp.sum(weights * d_weights, axis=1, keepdims=True))
        ds_all[step * mols : (step + 1) * mols, :] = d_scores
        d_hidden = d_hidden + mm3(split(d_scores), x, NTR)
        d_out = d_hidden * squashed * out_gate * (1.0 - out_gate)
        d_cell = d_cell + d_hidden * out_gate * (1.0 - squashed * squashed)
        d_forget = d_cell * before_cell * forget * (1.0 - forget)
        d_in = d_cell * part * in_gate * (1.0 - in_gate)
        d_part = d_cell * in_gate * (1.0 - part * part)
        d_cell = d_cell * forget
        d_gates = jnp.concatenate([d_in, d_forget, d_part, d_out], axis=1)
        d_gates_all[step] = d_gates
        if step > 0:
            d_query = mm3(split(d_gates), lstm_w, NTR)
            d_hidden, d_read = d_query[:, :H], d_query[:, H:]
    queries = split(jnp.concatenate([saved[s][0] for s in range(STEPS)], axis=0))
    d_gates_cat = jnp.concatenate(d_gates_all, axis=0)
    d_gates_s = split(d_gates_cat)
    grad_lstm = mm3(queries, d_gates_s, TN)
    d_gates_sum = jnp.sum(d_gates_cat, axis=0, keepdims=True)
    for k in range(4):
        pack[R_LSTM + k * 256 : R_LSTM + (k + 1) * 256, :] = grad_lstm[:, k * H : (k + 1) * H]
        pack[R_MISC + M_LSTM + k : R_MISC + M_LSTM + k + 1, :] = d_gates_sum[:, k * H : (k + 1) * H]
    left = jnp.concatenate(d_reads + [saved[s][7] for s in range(STEPS)], axis=0)
    left_s = split(left)

    def spread(k, carry):
        c = columns(k * LB, LB)
        right = split(jnp.concatenate([w_all[:, c], ds_all[:, c]], axis=0))
        dst_acc[:, c] = mm3(left_s, right, TN)
        return carry

    dst_acc[...] = jnp.zeros_like(dst_acc)
    lax.fori_loop(0, chunks, spread, 0)

    pack[R_GRU:R_SECOND, :] = jnp.zeros((6 * H, 128), f32)
    gm[...] = jnp.zeros_like(gm)
    for layer in reversed(range(LAYERS)):

        def back(k, carry, layer=layer):
            c = columns(k * LB, LB)
            d_state = dst_acc[:, c]
            reset, upd = keep[layer, 0, :, c], keep[layer, 1, :, c]
            fresh, from_st = keep[layer, 2, :, c], keep[layer, 3, :, c]
            d_upd = d_state * (st[layer, :, c] - fresh) * upd * (1.0 - upd)
            d_fresh = d_state * (1.0 - upd) * (1.0 - fresh * fresh)
            d_reset = d_fresh * from_st * reset * (1.0 - reset)
            d_from_in = jnp.concatenate([d_reset, d_upd, d_fresh], axis=0)
            d_from_st = jnp.concatenate([d_reset, d_upd, d_fresh * reset], axis=0)
            in_s, st_s = split(d_from_in), split(d_from_st)
            gm[:, c] = (mm(gru_n[0], in_s[0]) + mm(gru_n[0], in_s[1])).astype(bf16)
            if layer > 0:
                dst_acc[:, c] = d_state * upd + (mm(gru_n[1], st_s[0]) + mm(gru_n[1], st_s[1]))
            ones = jnp.ones((8, LB), bf16)
            message, state_low = msg[layer, :, c], low[layer, :, c]
            for half, left_m, right_m in ((0, message, in_s), (1, state_low, st_s)):
                grad = mm(left_m, right_m[0], NTR) + mm(left_m, right_m[1], NTR)
                sums = (mm(ones, right_m[0], NTR) + mm(ones, right_m[1], NTR))[:1]
                for q in range(3):
                    r = R_GRU + (half * 3 + q) * H
                    pack[r : r + H, :] += grad[:, q * H : (q + 1) * H]
                    m = R_MISC + M_INPUT + half * 3 + q
                    pack[m : m + 1, :] += sums[:, q * H : (q + 1) * H]
            return carry

        lax.fori_loop(0, chunks, back, 0)
        for k in range(parts):
            gm_rel[k * own_rows : (k + 1) * own_rows, :atoms] = gm[place(k), :]
        if layer > 0:
            bt_high, bt_low = split(jnp.transpose(ebias))

            def pull(b, carry, layer=layer):
                c = columns(b * LB, LB)
                w = window(b)
                grad = mm(gm_rel[:, w], hot_dst[:, c])
                grad_low = grad.astype(bf16)
                g_o[layer, :, c] = grad_low
                hid = hid_i[:, c]
                for i in range(H):
                    z[i * EH : (i + 1) * EH, :] = g_o[layer, pl.ds(i, 1), c] * hid
                pulled = mm(w_back[...], z[...])
                pulled = pulled + (mm(bt_high, grad_low) + mm(bt_low, grad_low))
                dst_acc[:, w] += mm2(pulled, hot_src[:, c], NTR)
                return carry

            lax.fori_loop(0, blocks, pull, 0)
        else:

            def take(b, carry, layer=layer):
                c = columns(b * LB, LB)
                g_o[layer, :, c] = mm(gm_rel[:, window(b)], hot_dst[:, c]).astype(bf16)
                return carry

            lax.fori_loop(0, blocks, take, 0)
    acc_b = acc.at[:, :H]
    acc_b[...] = jnp.zeros((H, H), f32)

    def bias_sum(b, carry):
        c = columns(b * LB, LB)
        acc_b[...] += mm(g_o[0, :, c], src_o[0, :, c], NTR) + mm(
            g_o[1, :, c], src_o[1, :, c], NTR
        )
        return carry

    lax.fori_loop(0, blocks, bias_sum, 0)
    for k in range(parts):
        row = pl.multiple_of(R_EBIAS + places[k], 8)
        pack[pl.ds(row, own_rows), :] = acc_b[k * own_rows : (k + 1) * own_rows, :]
    pack[R_END:R_PACK, :] = jnp.zeros((R_PACK - R_END, 128), f32)


def body_edges(jobs, start, last, meta, *refs):
    n = len(jobs)
    ws, (src, g, hid), refs = refs[:n], refs[n : n + 3], refs[n + 3 :]
    if not start:
        hid_before, refs = refs[0], refs[1:]
    if last:
        (before, feat, sums), refs = refs[:3], refs[3:]
    outs, result, built, acc = refs[:n], refs[n], refs[n + 1], refs[n + 2]
    grad_hid = refs[n + 3] if last else result
    blocks = meta[0]
    rows = ws[0].shape[1] // H

    acc[...] = jnp.zeros_like(acc)

    def edges(b, carry):
        c = columns(b * LB, LB)
        s0, s1 = src[0, :, c].astype(f32), src[1, :, c].astype(f32)
        pulled = None if start else hid_before[:, c]
        for q, (rel, chunk) in enumerate(jobs):
            at = (rel * CHUNKS + chunk) * rows
            g0 = g[0, at : at + rows, c].astype(f32)
            g1 = g[1, at : at + rows, c].astype(f32)
            for i in range(rows):
                built[q % 2, i * H : (i + 1) * H, :] = (
                    g0[i : i + 1] * s0 + g1[i : i + 1] * s1
                ).astype(bf16)
            part = mm(ws[q][...], built[q % 2])
            pulled = part if pulled is None else pulled + part
            acc[q] += mm(hid[:, c], built[q % 2], NTR)
        grad_hid[:, c] = pulled
        return carry

    lax.fori_loop(0, blocks, edges, 0)
    for q in range(n):
        for i in range(rows):
            outs[q][i * EH : (i + 1) * EH, :] = acc[q, :, i * H : (i + 1) * H].astype(
                outs[q].dtype
            )

    if last:
        result[...] = sums[...]

        def finish(b, carry):
            c = columns(b * LB, LB)
            ahead = before[:, c]
            sig = sigmoid(ahead)
            grad = split(grad_hid[:, c] * sig * (1.0 + ahead * (1.0 - sig)))
            rows_low = feat[:, c].astype(bf16)
            result[...] += mm(rows_low, grad[0], NTR) + mm(rows_low, grad[1], NTR)
            return carry

        lax.fori_loop(0, blocks, finish, 0)


def adamw(weight, grad, moment, second):
    moment_new = beta_one * moment + (1.0 - beta_one) * grad
    second_new = beta_two * second + (1.0 - beta_two) * grad * grad
    mean_hat = moment_new / (1.0 - beta_one**STEP_COUNT)
    square_hat = second_new / (1.0 - beta_two**STEP_COUNT)
    return (
        weight - rate * (mean_hat / (jnp.sqrt(square_hat) + epsilon) + decay * weight),
        moment_new,
        second_new,
    )


def body_adamw(own_rows, place, *refs):
    owns, refs = refs[:CHUNKS], refs[CHUNKS:]
    (pack, grad_in, squares), refs = refs[:3], refs[3:]
    params, moments, seconds = refs[0:8], refs[8:16], refs[16:24]
    outs = refs[24:48]
    loss, count, norm, scale = refs[48:52]

    def step(index, grad, at=...):
        new = adamw(params[index][at], grad, moments[index][at], seconds[index][at])
        for kind in range(3):
            outs[kind * 8 + index][at] = new[kind]

    @pl.when(pl.program_id(0) == 0)
    def _():
        total = squares[0:1, 0:1] + total_of(jnp.square(grad_in[: G_BIAS + 1, :]))
        for k in range(4):
            total = total + total_of(jnp.square(pack[R_LSTM + k * 2 * H : R_LSTM + k * 2 * H + H, :]))
        loss[...] = grad_in[G_SUMS : G_SUMS + 1, 0:1]
        number = grad_in[G_SUMS : G_SUMS + 1, 1:2]
        count[...] = number
        grad_norm = jnp.sqrt(total) / number
        norm[...] = grad_norm
        factor = jnp.minimum(1.0, clip_norm / grad_norm) / number
        scale[...] = jnp.broadcast_to(factor, scale.shape)
        step(0, grad_in[:EIN, :] * factor)
        step(2, pack[pl.ds(pl.multiple_of(R_EBIAS + place[0], 8), own_rows), :] * factor)
        for half in range(2):
            for q in range(3):
                r = R_GRU + (half * 3 + q) * H
                step(3, pack[r : r + H, :] * factor, (half, slice(None), slice(q * H, (q + 1) * H)))
        for k in range(4):
            r = R_LSTM + k * 2 * H
            for block, start in ((0, 0), (1, H), (2, 0)):
                step(
                    4,
                    pack[r + start : r + start + H, :] * factor,
                    (slice(block * H, (block + 1) * H), slice(k * H, (k + 1) * H)),
                )
        step(5, pack[R_FIRST:R_GRU, :] * factor)
        step(6, pack[R_SECOND : R_SECOND + NT, :] * factor)
        bias = jnp.concatenate(
            [grad_in[G_BIAS : G_BIAS + 1, :], pack[R_MISC + 1 : R_EBIAS, :]], axis=0
        )
        step(7, bias * factor)

    per = pl.num_programs(0) // CHUNKS
    for c in range(CHUNKS):

        @pl.when(pl.program_id(0) // per == c)
        def _(c=c):
            for i in range(params[1].shape[1] // H):
                step(
                    1,
                    owns[c][i * EH : (i + 1) * EH, :] * scale[0:1, 0:1],
                    (slice(None), slice(i * H, (i + 1) * H)),
                )


VM = pl.BlockSpec(memory_space=pltpu.VMEM)
SM = pl.BlockSpec(memory_space=pltpu.SMEM)


def per_device(
    node_feats,
    edge_feats,
    edge_ends,
    atom_counts,
    dataset_flags,
    targets,
    present,
    edge_in,
    edge_out,
    edge_bias,
    gru_weights,
    lstm_weights,
    head_first,
    head_second,
    biases,
    *moments_seconds,
):
    row = lax.axis_index("row")
    row_count = lax.axis_size("row")
    mol = lax.axis_index("mol")
    mol_bits = lax.axis_size("mol").bit_length() - 1
    row_bits = row_count.bit_length() - 1
    mols = node_feats.shape[0]
    own_rows = edge_out.shape[1] // H
    atoms = -(-mols * ATOMS // LB) * LB
    space = -(-mols * LIVE // LB) * LB

    def row_swap(x, k):
        return lax.ppermute(x, "row", [(i, i ^ k) for i in range(row_count)])

    def mol_swap(x, bit):
        return lax.ppermute(x, "mol", [(i, i ^ (1 << bit)) for i in range(2**mol_bits)])

    def double(x, swap, bit):
        other = swap(x)
        return jnp.concatenate(
            [jnp.where(bit == 0, x, other), jnp.where(bit == 0, other, x)], axis=0
        )

    sds = jax.ShapeDtypeStruct
    n = row_count
    al = atoms + WINDOW - 128
    params = pltpu.CompilerParams(vmem_limit_bytes=56 * MIB)

    sent = edge_out.astype(bf16)
    bias_sent = edge_bias.reshape(own_rows, H)

    def forward_order(part):
        part = part.reshape(EH, own_rows, H)
        return part.transpose(1, 0, 2).reshape(own_rows, EH * H)

    parts, bias_parts = {0: sent}, {0: bias_sent}
    for bit in reversed(range(row_bits)):
        parts[1 << bit] = row_swap(sent, 1 << bit)
        bias_parts[1 << bit] = row_swap(bias_sent, 1 << bit)

    ends = lax.dynamic_slice_in_dim(edge_ends, row * mols, mols, 1)
    feats = lax.dynamic_slice_in_dim(edge_feats, row * mols * EM, mols * EM, 1)
    table = jnp.concatenate([feats.reshape(EIN, mols, EM), ends.astype(bf16)], axis=0)
    table = table.transpose(1, 0, 2).reshape(mols, (EIN + 2) * EM)
    places = jnp.stack([(row ^ k) * own_rows for k in range(row_count)]).astype(jnp.int32)
    bias_rows = jnp.pad(biases, (0, 16 * 128 - biases.shape[0])).reshape(16, 128)

    prepared = pl.pallas_call(
        functools.partial(body_prepare, mols),
        out_shape=(
            sds((2 + space // LB,), jnp.int32),
            sds((H, atoms), bf16),
            sds((EH, space), bf16),
            sds((EH, space), f32),
            sds((8, space), f32),
            sds((WINDOW, space), bf16),
            sds((WINDOW, space), bf16),
        ),
        in_specs=[SM] + [VM] * 4,
        out_specs=(SM,) + (VM,) * 6,
        scratch_shapes=[pltpu.VMEM((128, 128), f32), pltpu.VMEM((mols * PAD, H), f32)],
        compiler_params=params,
    )(atom_counts, table, node_feats, edge_in, bias_rows)
    forward = {k: forward_order(part) for k, part in parts.items() if k < n // 2}
    parts, bias_parts, prepared, forward = lax.optimization_barrier(
        (parts, bias_parts, prepared, forward)
    )
    meta, nodes, hid, before, feat, hot_src, hot_dst = prepared
    for bit in reversed(range(row_bits)):
        for k in [k for k in parts if k > 1 << bit and not k & (1 << bit)]:
            parts[k + (1 << bit)] = row_swap(parts[k], 1 << bit)
            bias_parts[k + (1 << bit)] = row_swap(bias_parts[k], 1 << bit)
    parts = [parts[k] for k in range(n)]
    bias_parts = [bias_parts[k] for k in range(n)]
    w_fwd = [forward[k] if k in forward else forward_order(parts[k]) for k in range(n)]

    def main(*refs):
        at = 10
        body_main(
            mols,
            own_rows,
            *refs[:at],
            refs[at : at + n],
            refs[at + n : at + 2 * n],
            refs[at + 2 * n : at + 3 * n],
            *refs[at + 3 * n :],
        )

    pack, sums, src, g = pl.pallas_call(
        main,
        out_shape=(
            sds((R_PACK, 128), f32),
            sds((8, 128), f32),
            sds((LAYERS, H, space), bf16),
            sds((LAYERS, H, space), bf16),
        ),
        in_specs=[SM] * 4 + [VM] * (11 + 3 * n),
        out_specs=(VM,) * 4,
        scratch_shapes=[
            pltpu.VMEM((H * EH, LB), bf16),
            pltpu.VMEM((LAYERS + 1, H, atoms), f32),
            pltpu.VMEM((LAYERS, H, al), bf16),
            pltpu.VMEM((LAYERS, H, atoms), bf16),
            pltpu.VMEM((LAYERS, 4, H, atoms), f32),
            pltpu.VMEM((H, al), f32),
            pltpu.VMEM((H, al), f32),
            pltpu.VMEM((H, atoms), bf16),
            pltpu.VMEM((H, al), bf16),
            pltpu.VMEM((H, H * EH), bf16),
            pltpu.VMEM((STEPS * mols, atoms), f32),
            pltpu.VMEM((STEPS * mols, atoms), f32),
            pltpu.VMEM((2, H, 3 * H), bf16),
            pltpu.VMEM((2, 3 * H, H), bf16),
            pltpu.VMEM((128, 128), f32),
        ],
        compiler_params=pltpu.CompilerParams(vmem_limit_bytes=60 * MIB),
    )(
        atom_counts,
        dataset_flags,
        places,
        meta,
        targets.T,
        present.T,
        nodes,
        hid,
        hot_src,
        hot_dst,
        *w_fwd,
        *parts,
        *bias_parts,
        gru_weights,
        bias_rows,
        lstm_weights,
        head_first,
        head_second.T,
    )

    span = own_rows * H // CHUNKS

    def edge_parts(jobs, before_hid, last):
        start = before_hid is None
        extra = () if start else (before_hid,)
        if last:
            extra = extra + (before, feat, sums)
        *found, result = pl.pallas_call(
            functools.partial(body_edges, jobs, start, last),
            grid=(1,),
            out_shape=(sds((span, EH), bf16),) * len(jobs)
            + (sds((8, EH) if last else (EH, space), f32),),
            in_specs=[SM]
            + [pl.BlockSpec((EH, span), lambda i, c=chunk: (0, c)) for _, chunk in jobs]
            + [VM] * (3 + len(extra)),
            out_specs=(VM,) * (len(jobs) + 1),
            scratch_shapes=[
                pltpu.VMEM((2, span, LB), bf16),
                pltpu.VMEM((len(jobs), EH, span), f32),
            ]
            + ([pltpu.VMEM((EH, space), f32)] if last else []),
            compiler_params=params,
        )(meta, *(parts[k] for k, _ in jobs), src, g, hid, *extra)
        return found, result

    row_steps = [(functools.partial(row_swap, k=1 << b), (row >> b) & 1) for b in range(row_bits)]
    mol_steps = [(functools.partial(mol_swap, bit=b), (mol >> b) & 1) for b in range(mol_bits)]
    tie = lax.optimization_barrier
    (core, core_bit), (cross, cross_bit) = row_steps

    def halves(x, bit):
        both = x.reshape((2, x.shape[0] // 2) + x.shape[1:])
        return (
            lax.dynamic_index_in_dim(both, 1 - bit, 0, False),
            lax.dynamic_index_in_dim(both, bit, 0, False),
        )

    def as_low(x, count):
        found = []
        for _ in range(count):
            high = lax.reduce_precision(x, 8, 7)
            found.append(high)
            x = x - high
        return jnp.concatenate(found, axis=0).astype(bf16)

    def from_low(x, count):
        x = x.astype(f32).reshape(count, -1, 128)
        found = x[count - 1]
        for k in reversed(range(count - 1)):
            found = found + x[k]
        return found

    (far, far_core), carry = edge_parts(((2, 0), (3, 0)), None, False)
    pack_sent, pack = halves(pack, core_bit)
    came = core(jnp.concatenate([far_core, as_low(pack_sent, 2)], axis=0))
    pack_sent, pack = halves(pack + from_low(came[span:], 2), cross_bit)
    sent = (far.astype(f32) + came[:span].astype(f32)).astype(bf16)
    sent = jnp.concatenate([sent, as_low(pack_sent, 2)], axis=0)
    sent, carry = tie((sent, carry))
    arrived = cross(sent)
    (near, near_core, far, far_core), carry = edge_parts(
        ((0, 0), (1, 0), (2, 1), (3, 1)), carry, False
    )
    sent, arrived = tie((jnp.concatenate([near_core, far_core], axis=0), arrived))
    came = core(sent)
    own = near.astype(f32) + came[:span].astype(f32) + arrived[:span].astype(f32)
    pack = pack + from_low(arrived[span:], 2)
    sent = (far.astype(f32) + came[span:].astype(f32)).astype(bf16)

    def first_stage(own, pack, swap, bit):
        own_sent, own = halves(own, bit)
        pack_sent, pack = halves(pack, bit)
        half = own.shape[0]

        def take(came):
            return own + came[:half].astype(f32), pack + from_low(came[half:], 2)

        return jnp.concatenate([own_sent.astype(bf16), as_low(pack_sent, 2)], axis=0), take

    first_sent, take = first_stage(own, pack, *mol_steps[0])
    sent, first_sent, carry = tie((sent, first_sent, carry))
    arrived = cross(sent)
    first_came = mol_steps[0][0](first_sent)
    (near, near_core), grad_in = edge_parts(((0, 1), (1, 1)), carry, True)
    sent = jnp.concatenate([near_core, as_low(grad_in, 3)], axis=0)
    sent, arrived, first_came = tie((sent, arrived, first_came))
    came = core(sent)
    grad_in = grad_in + from_low(came[span:], 3)
    own = near.astype(f32) + came[:span].astype(f32) + arrived.astype(f32)
    first, pack = take(first_came)
    grad_in = grad_in + cross(grad_in)
    grad_in = grad_in + mol_steps[0][0](grad_in)
    for index, (swap, bit) in enumerate(mol_steps):
        if index > 0:
            first_sent, take = first_stage(first, pack, swap, bit)
            first, pack = take(swap(first_sent))
        own_sent, own = halves(own, bit)
        half = own.shape[0]
        sent = own_sent.astype(bf16)
        if index > 0:
            sent = jnp.concatenate([sent, as_low(grad_in, 3)], axis=0)
        came = swap(sent)
        own = own + came[:half].astype(f32)
        if index > 0:
            grad_in = grad_in + from_low(came[half:], 3)
    owns = [first, own]
    own_rest = owns[0].shape[0]
    pieces = [jnp.concatenate([owns[0], pack], axis=0)] + owns[1:]
    squares = jnp.broadcast_to(sum(jnp.sum(piece * piece) for piece in pieces), (8, 128))

    travel = []
    for piece in pieces:
        largest = jnp.maximum(jnp.max(jnp.abs(piece)), 1e-30)
        power = 14.0 - jnp.ceil(jnp.log2(largest))
        travel.append(
            jnp.concatenate(
                [piece * jnp.exp2(power), jnp.broadcast_to(power, (16, 128))], axis=0
            ).astype(jnp.float16)
        )
    squares, travel[-1] = tie((squares, travel[-1]))
    squares = (squares + row_swap(squares, 1)) + (row_swap(squares, 2) + row_swap(squares, 3))
    for swap, bit in reversed(mol_steps):
        squares = squares + swap(squares)
    for swap, bit in reversed(mol_steps):
        travel = [double(sent, swap, bit) for sent in travel]
    owns = []
    for piece, sent in zip(pieces, travel):
        height = piece.shape[0]
        sent = sent.astype(f32).reshape(-1, height + 16, 128)
        owns.append(sent[:, :height] * jnp.exp2(-sent[:, height : height + 1, 0:1]))
    pack = owns[0][:, own_rest:].reshape(-1, 128)
    owns[0] = owns[0][:, :own_rest]
    owns = [own.reshape(-1, 128) for own in owns]
    for swap, bit in reversed(row_steps):
        pack = double(pack, swap, bit)

    weights = [
        edge_in,
        edge_out,
        edge_bias,
        gru_weights,
        lstm_weights,
        head_first,
        head_second,
        biases,
    ]
    states = []
    for group in (weights, moments_seconds[:8], moments_seconds[8:]):
        group = list(group)
        group[2] = group[2].reshape(own_rows, H)
        group[6] = group[6].T
        if group[7] is biases:
            group[7] = bias_rows
        else:
            group[7] = jnp.pad(group[7], (0, 16 * 128 - group[7].shape[0])).reshape(16, 128)
        states += group
    grid = 2 * CHUNKS
    block = pl.BlockSpec((EH, own_rows * H // grid), lambda i: (0, i))
    own_specs = [
        pl.BlockSpec((span // 2, EH), lambda i, c=c: (jnp.clip(i - 2 * c, 0, 1), 0))
        for c in range(CHUNKS)
    ]

    def state_specs():
        return [block if index == 1 else VM for index in range(8)] * 3

    shapes = [sds(state.shape, f32) for state in states]
    results = pl.pallas_call(
        functools.partial(body_adamw, own_rows),
        grid=(grid,),
        out_shape=tuple(shapes) + (sds((1, 1), f32),) * 3,
        in_specs=[SM] + own_specs + [VM, VM, VM] + state_specs(),
        out_specs=tuple(state_specs()) + (VM,) * 3,
        scratch_shapes=[pltpu.VMEM((8, 128), f32)],
        compiler_params=params,
    )(places, *owns, pack, grad_in, squares, *states)
    results = list(results)
    for kind in range(3):
        results[kind * 8 + 2] = results[kind * 8 + 2].reshape(own_rows * H)
        results[kind * 8 + 6] = results[kind * 8 + 6].T
        results[kind * 8 + 7] = results[kind * 8 + 7].reshape(-1)[: biases.shape[0]]
    for index in range(24, 27):
        results[index] = results[index].reshape(())
    return tuple(results)


def solution(mesh):
    weights = (P(), P(None, "row"), P("row"), P(), P(), P(), P(), P())
    in_specs = (
        P(("mol", "row"), None, None),
        P(None, "mol"),
        P(None, "mol", None),
        P(("mol", "row")),
        P(("mol", "row")),
        P(("mol", "row"), None),
        P(("mol", "row"), None),
    ) + weights * 3
    out_specs = weights * 3 + (P(), P(), P())
    return jax.shard_map(
        per_device, mesh=mesh, in_specs=in_specs, out_specs=out_specs, check_vma=False
    )
```

```python
import functools
import math

import jax
import jax.numpy as jnp
from jax import lax
from jax.experimental import pallas as pl
from jax.experimental.pallas import tpu as pltpu
from jax.sharding import PartitionSpec as P

H = 128
EH = 128
EIN = 5
NT = 12
STEPS = 6
ATOMS = 29
EM = 64
LAYERS = 2
STEP_COUNT = 10

PAD = 32
LIVE = 2 * (ATOMS - 1)
LB = 256
MIB = 2**20

f32 = jnp.float32
bf16 = jnp.bfloat16
highest = lax.Precision.HIGHEST
beta_one = 0.9
beta_two = 0.999
rate = 0.05
epsilon = 1e-08
decay = 0.01
clip_norm = 0.1

R_LSTM, R_FIRST, R_GRU, R_SECOND, R_MISC, R_EBIAS, R_END = 0, 1024, 1280, 2048, 2064, 2080, 2208
R_PACK = 2560
M_INPUT, M_LSTM, M_HEAD, M_OUT = 1, 7, 11, 12
G_BIAS, G_SUMS = EIN, EIN + 1
WINDOW = 384
CHUNKS = 2

NN = ((1,), (0,))
NTR = ((1,), (1,))
TN = ((0,), (0,))


def mm(a, b, dims=NN):
    return lax.dot_general(a, b, (dims, ((), ())), preferred_element_type=f32)


def split(x):
    high = x.astype(bf16)
    return high, (x - high.astype(f32)).astype(bf16)


def mm3(a, b, dims=NN):
    return mm(a[0], b[0], dims) + (mm(a[0], b[1], dims) + mm(a[1], b[0], dims))


def mm2(a, b, dims=NN):
    high, low = split(a)
    return mm(high, b, dims) + mm(low, b, dims)


def total_of(x):
    return jnp.sum(jnp.sum(x, axis=1, keepdims=True), axis=0, keepdims=True)


def columns(start, size):
    return pl.ds(pl.multiple_of(start, size), size)


def sigmoid(v):
    return jax.nn.sigmoid(v)


def column_of(values, size):
    at = lax.broadcasted_iota(jnp.int32, (size, 1), 0)
    found = jnp.zeros((size, 1), jnp.int32)
    for m in range(size):
        found = jnp.where(at == m, values[m], found)
    return found


def row_of(values, size):
    at = lax.broadcasted_iota(jnp.int32, (1, size), 1)
    found = jnp.zeros((1, size), jnp.int32)
    for m in range(size):
        found = jnp.where(at == m, values[m], found)
    return found


def starts_of(column, size):
    below = (
        lax.broadcasted_iota(jnp.int32, (size, size), 1)
        < lax.broadcasted_iota(jnp.int32, (size, size), 0)
    ).astype(bf16)
    return mm(below, jnp.broadcast_to(column, (size, 128)).astype(bf16))[:, :1]


def body_prepare(
    mols,
    counts_s,
    table,
    node_feats,
    edge_in,
    bias_rows,
    meta,
    nodes_o,
    hid_o,
    before_o,
    feat_o,
    hot_src,
    hot_dst,
    square,
    flat,
):
    lanes = nodes_o.shape[1]
    space = hid_o.shape[1]
    for b in range(space // LB):
        meta[2 + b] = jnp.int32(0)
    edges, atoms = jnp.int32(0), jnp.int32(0)
    for m in range(mols):
        live = 2 * (counts_s[m] - 1)
        block = lax.div(edges + (LB - 1), jnp.int32(LB))

        @pl.when(block * LB < edges + live)
        def _(block=block, atoms=atoms):
            meta[2 + block] = lax.div(atoms, jnp.int32(128)) * 128

        edges = edges + live
        atoms = atoms + counts_s[m]
    blocks = lax.div(edges + (LB - 1), jnp.int32(LB))
    meta[0] = blocks
    meta[1] = lax.div(atoms + (LB - 1), jnp.int32(LB))

    count_col = column_of(counts_s, mols).astype(f32)
    live_col = 2.0 * (count_col - 1.0)
    start_col = starts_of(live_col, mols)
    atom_col = starts_of(count_col, mols)

    square[...] = jnp.zeros_like(square)
    square[0:EIN, :] = edge_in[...]
    square[8:24, :] = bias_rows[...]
    turned = jnp.transpose(square[...])
    in_t, b_in_col = turned[:, :8], turned[:, 8:9]
    e_high, e_low = split(in_t)
    e_rest = (in_t - e_high.astype(f32) - e_low.astype(f32)).astype(bf16)

    flat[...] = jnp.zeros_like(flat)
    for m in range(mols):
        flat[m * PAD : m * PAD + ATOMS, :] = node_feats[m].astype(f32)
    flat_low = flat[...].astype(bf16)
    nodes_o[...] = jnp.zeros_like(nodes_o)
    atom_at = lax.broadcasted_iota(jnp.int32, (mols * PAD, 1), 0)
    spread = (
        lax.broadcasted_iota(jnp.int32, (mols * PAD, mols), 0) // PAD
        == lax.broadcasted_iota(jnp.int32, (mols * PAD, mols), 1)
    ).astype(bf16)
    goal_high = jnp.floor(atom_col * (1.0 / 8.0))
    goal_parts = jnp.concatenate([goal_high, atom_col - 8.0 * goal_high, count_col], axis=1)
    goal = mm(
        spread,
        jnp.concatenate([goal_parts, jnp.zeros((mols, 125), f32)], axis=1).astype(bf16),
    )
    within = lax.rem(atom_at, jnp.int32(PAD)).astype(f32)
    target = jnp.where(
        within < goal[:, 2:3], 8.0 * goal[:, 0:1] + goal[:, 1:2] + within, -1.0
    ).astype(jnp.int32)

    def pack_atoms(k, carry):
        c = columns(k * LB, LB)
        at = lax.broadcasted_iota(jnp.int32, (mols * PAD, LB), 1) + k * LB
        hot = (at == target).astype(f32).astype(bf16)
        nodes_o[:, c] = mm(flat_low, hot, TN).astype(bf16)
        return carry

    lax.fori_loop(0, meta[1], pack_atoms, 0)

    def prepare(b, carry):
        c = columns(b * LB, LB)
        spot = (lax.broadcasted_iota(jnp.int32, (mols, LB), 1) + b * LB).astype(f32)
        mol_hot = ((spot >= start_col) & (spot < start_col + live_col)).astype(f32)
        rows = mm(table[...], mol_hot.astype(bf16), TN)
        start_row = jnp.sum(mol_hot * start_col, axis=0, keepdims=True)
        base = jnp.sum(mol_hot * atom_col, axis=0, keepdims=True)
        valid = jnp.sum(mol_hot, axis=0, keepdims=True)
        slot = spot[:1] - start_row
        slot_hot = (lax.broadcasted_iota(jnp.int32, (EM, LB), 0).astype(f32) == slot).astype(f32)
        picked = [
            jnp.sum(rows[r * EM : (r + 1) * EM] * slot_hot, axis=0, keepdims=True)
            for r in range(EIN + 2)
        ]
        feat = jnp.concatenate(picked[:EIN] + [valid, jnp.zeros((2, LB), f32)], axis=0)
        feat_o[:, c] = feat
        feat_low = feat.astype(bf16)
        before = mm(e_high, feat_low) + mm(e_low, feat_low) + mm(e_rest, feat_low) + b_in_col
        before_o[:, c] = before
        hid_o[:, c] = (before * sigmoid(before)).astype(bf16)
        atom = lax.broadcasted_iota(jnp.int32, (WINDOW, LB), 0)
        base = base - meta[2 + b].astype(f32)
        src = jnp.where(valid > 0.5, base + picked[EIN], -1.0).astype(jnp.int32)
        dst = jnp.where(valid > 0.5, base + picked[EIN + 1], -1.0).astype(jnp.int32)
        hot_src[:, c] = (atom == src).astype(f32).astype(bf16)
        hot_dst[:, c] = (atom == dst).astype(f32).astype(bf16)
        return carry

    lax.fori_loop(0, blocks, prepare, 0)


def body_main(
    mols,
    own_rows,
    counts_s,
    flags_s,
    places,
    meta,
    targets,
    present,
    nodes,
    hid_i,
    hot_src,
    hot_dst,
    w_fwd,
    w_nat,
    ebias_parts,
    gru,
    bias_rows,
    lstm_rows,
    first,
    second,
    pack,
    sums_o,
    src_o,
    g_o,
    z,
    st,
    low,
    msg,
    keep,
    acc,
    dst_acc,
    gm,
    gm_rel,
    w_back,
    w_all,
    ds_all,
    gru_n,
    gru_t,
    square,
):
    parts = len(w_fwd)
    blocks, chunks = meta[0], meta[1]
    atoms = w_all.shape[1]

    def place(k):
        return pl.ds(pl.multiple_of(places[k], own_rows), own_rows)

    def window(b):
        return pl.ds(pl.multiple_of(meta[2 + b], 128), WINDOW)

    square[...] = jnp.zeros_like(square)
    square[0:16, :] = bias_rows[...]
    turned = jnp.transpose(square[...])
    gbias_col = [
        jnp.concatenate([turned[:, r + q : r + q + 1] for q in range(3)], axis=0)
        for r in (M_INPUT, M_INPUT + 3)
    ]
    c_lstm = jnp.concatenate(
        [bias_rows[M_LSTM + k : M_LSTM + k + 1, :] for k in range(4)], axis=1
    )
    c_head = bias_rows[M_HEAD : M_HEAD + 1, :]
    out_cols = [turned[k * NT : (k + 1) * NT, M_OUT : M_OUT + 1] for k in range(3)]
    gru_n[...] = gru[...].astype(bf16)
    for half in range(2):
        for q in range(3):
            gru_t[half, q * H : (q + 1) * H, :] = jnp.transpose(
                gru_n[half, :, q * H : (q + 1) * H]
            )
    ebias = jnp.concatenate([part[...] for part in ebias_parts], axis=0)
    b_high, b_low = split(ebias)

    def turn(i, carry):
        for k in range(parts):
            w_back[:, pl.ds(pl.multiple_of(k * own_rows * H + i * H, H), H)] = jnp.transpose(
                w_nat[k][:, columns(i * H, H)]
            )
        return carry

    lax.fori_loop(0, own_rows, turn, 0)

    for layer in range(LAYERS):
        low[layer] = jnp.zeros_like(low[layer])
    low[0, :, :atoms] = nodes[...]
    st[0] = nodes[...].astype(f32)
    st[LAYERS] = jnp.zeros_like(st[LAYERS])
    gm_rel[...] = jnp.zeros_like(gm_rel)
    for layer in range(LAYERS):
        acc[...] = jnp.zeros_like(acc)

        def move(b, carry, layer=layer):
            c, w = columns(b * LB, LB), window(b)
            source = mm(low[layer, :, w], hot_src[:, c]).astype(bf16)
            src_o[layer, :, c] = source
            for h in range(EH):
                z[h * H : (h + 1) * H, :] = hid_i[pl.ds(h, 1), c] * source
            moved = mm(jnp.concatenate([part[...] for part in w_fwd], axis=0), z[...])
            moved = moved + (mm(b_high, source) + mm(b_low, source))
            acc[:, w] += mm2(moved, hot_dst[:, c], NTR)
            return carry

        lax.fori_loop(0, blocks, move, 0)
        for k in range(parts):
            msg[layer, place(k), :] = acc[k * own_rows : (k + 1) * own_rows, :atoms].astype(bf16)

        def update(k, carry, layer=layer):
            c = columns(k * LB, LB)
            from_in = mm(gru_t[0], msg[layer, :, c]) + gbias_col[0]
            from_st = mm(gru_t[1], low[layer, :, c]) + gbias_col[1]
            reset = sigmoid(from_in[:H] + from_st[:H])
            upd = sigmoid(from_in[H : 2 * H] + from_st[H : 2 * H])
            fresh = jnp.tanh(from_in[2 * H :] + reset * from_st[2 * H :])
            new = (1.0 - upd) * fresh + upd * st[layer, :, c]
            st[layer + 1, :, c] = new
            if layer + 1 < LAYERS:
                low[layer + 1, :, c] = new.astype(bf16)
            keep[layer, 0, :, c] = reset
            keep[layer, 1, :, c] = upd
            keep[layer, 2, :, c] = fresh
            keep[layer, 3, :, c] = from_st[2 * H :]
            return carry

        lax.fori_loop(0, chunks, update, 0)

    lane = lax.broadcasted_iota(jnp.int32, (mols, atoms), 1).astype(f32)
    count_col = column_of(counts_s, mols).astype(f32)
    slot_of = lane - starts_of(count_col, mols)
    alive = (slot_of >= 0.0) & (slot_of < count_col)
    x = split(st[LAYERS])
    lstm = jnp.concatenate(
        [lstm_rows[0:H, :] + lstm_rows[2 * H : 3 * H, :], lstm_rows[H : 2 * H, :]], axis=0
    )
    lstm_w = split(lstm)
    zeros = jnp.zeros((mols, H), f32)
    hidden, read, cell = zeros, zeros, zeros
    saved = []
    for step in range(STEPS):
        query = jnp.concatenate([hidden, read], axis=1)
        if step == 0:
            gates = jnp.broadcast_to(c_lstm, (mols, 4 * H))
        else:
            gates = mm3(split(query), lstm_w) + c_lstm
        in_gate = sigmoid(gates[:, :H])
        forget = sigmoid(gates[:, H : 2 * H])
        part = jnp.tanh(gates[:, 2 * H : 3 * H])
        out_gate = sigmoid(gates[:, 3 * H :])
        before_cell = cell
        cell = forget * cell + in_gate * part
        squashed = jnp.tanh(cell)
        hidden = out_gate * squashed
        scores = jnp.where(alive, mm3(split(hidden), x), -1e30)
        weights = jnp.where(alive, jnp.exp(scores - jnp.max(scores, axis=1, keepdims=True)), 0.0)
        weights = weights / jnp.sum(weights, axis=1, keepdims=True)
        w_all[step * mols : (step + 1) * mols, :] = weights
        read = mm3(split(weights), x, NTR)
        saved.append((query, in_gate, forget, part, out_gate, before_cell, squashed, hidden))
    query = jnp.concatenate([hidden, read], axis=1)
    first_w = split(first[...])
    second_w = split(second[...])
    query_s = split(query)
    inner_pre = mm3(query_s, first_w) + c_head
    inner_sig = sigmoid(inner_pre)
    inner = inner_pre * inner_sig
    inner_s = split(inner)
    is_one = row_of(flags_s, mols) == 1
    predicted = (
        mm3(second_w, inner_s, NTR)
        + out_cols[0]
        + jnp.where(is_one, out_cols[2], out_cols[1])
    )
    there = present[...].astype(f32)
    diff = predicted - targets[...]
    lanes = lax.broadcasted_iota(jnp.int32, (1, 128), 1)
    loss = total_of(there * diff * diff)
    count = total_of(there)
    sums_o[...] = jnp.zeros_like(sums_o)
    sums_o[G_SUMS : G_SUMS + 1, :] = jnp.where(lanes == 0, loss, jnp.where(lanes == 1, count, 0.0))

    d_pred = 2.0 * there * diff
    d_pred_s = split(d_pred)
    pack[R_SECOND:R_MISC, :] = jnp.zeros((R_MISC - R_SECOND, 128), f32)
    pack[R_SECOND : R_SECOND + NT, :] = mm3(d_pred_s, inner_s)
    pack[R_MISC:R_EBIAS, :] = jnp.zeros((R_EBIAS - R_MISC, 128), f32)
    zero_pred = jnp.where(is_one, 0.0, d_pred)
    out_sums = jnp.concatenate([d_pred, zero_pred, d_pred - zero_pred], axis=0)
    out_high, out_low = split(out_sums)
    out_ones = jnp.ones((8, mols), bf16)
    pack[R_MISC + M_OUT : R_MISC + M_OUT + 1, : 3 * NT] = (
        mm(out_ones, out_high, NTR) + mm(out_ones, out_low, NTR)
    )[:1]
    d_inner = mm3(d_pred_s, second_w, TN)
    d_pre = d_inner * inner_sig * (1.0 + inner_pre * (1.0 - inner_sig))
    d_pre_s = split(d_pre)
    pack[R_FIRST:R_GRU, :] = mm3(query_s, d_pre_s, TN)
    pack[R_MISC + M_HEAD : R_MISC + M_HEAD + 1, :] = jnp.sum(d_pre, axis=0, keepdims=True)
    d_query = mm3(d_pre_s, first_w, NTR)
    d_hidden, d_read = d_query[:, :H], d_query[:, H:]
    d_cell = zeros
    d_gates_all = [None] * STEPS
    d_reads = [None] * STEPS
    for step in reversed(range(STEPS)):
        query, in_gate, forget, part, out_gate, before_cell, squashed, hid_t = saved[step]
        weights = w_all[step * mols : (step + 1) * mols, :]
        d_read_s = split(d_read)
        d_reads[step] = d_read
        d_weights = mm3(d_read_s, x)
        d_scores = weights * (d_weights - jnp.sum(weights * d_weights, axis=1, keepdims=True))
        ds_all[step * mols : (step + 1) * mols, :] = d_scores
        d_hidden = d_hidden + mm3(split(d_scores), x, NTR)
        d_out = d_hidden * squashed * out_gate * (1.0 - out_gate)
        d_cell = d_cell + d_hidden * out_gate * (1.0 - squashed * squashed)
        d_forget = d_cell * before_cell * forget * (1.0 - forget)
        d_in = d_cell * part * in_gate * (1.0 - in_gate)
        d_part = d_cell * in_gate * (1.0 - part * part)
        d_cell = d_cell * forget
        d_gates = jnp.concatenate([d_in, d_forget, d_part, d_out], axis=1)
        d_gates_all[step] = d_gates
        if step > 0:
            d_query = mm3(split(d_gates), lstm_w, NTR)
            d_hidden, d_read = d_query[:, :H], d_query[:, H:]
    queries = split(jnp.concatenate([saved[s][0] for s in range(STEPS)], axis=0))
    d_gates_cat = jnp.concatenate(d_gates_all, axis=0)
    d_gates_s = split(d_gates_cat)
    grad_lstm = mm3(queries, d_gates_s, TN)
    d_gates_sum = jnp.sum(d_gates_cat, axis=0, keepdims=True)
    for k in range(4):
        pack[R_LSTM + k * 256 : R_LSTM + (k + 1) * 256, :] = grad_lstm[:, k * H : (k + 1) * H]
        pack[R_MISC + M_LSTM + k : R_MISC + M_LSTM + k + 1, :] = d_gates_sum[:, k * H : (k + 1) * H]
    left = jnp.concatenate(d_reads + [saved[s][7] for s in range(STEPS)], axis=0)
    left_s = split(left)

    def spread(k, carry):
        c = columns(k * LB, LB)
        right = split(jnp.concatenate([w_all[:, c], ds_all[:, c]], axis=0))
        dst_acc[:, c] = mm3(left_s, right, TN)
        return carry

    dst_acc[...] = jnp.zeros_like(dst_acc)
    lax.fori_loop(0, chunks, spread, 0)

    pack[R_GRU:R_SECOND, :] = jnp.zeros((6 * H, 128), f32)
    gm[...] = jnp.zeros_like(gm)
    for layer in reversed(range(LAYERS)):

        def back(k, carry, layer=layer):
            c = columns(k * LB, LB)
            d_state = dst_acc[:, c]
            reset, upd = keep[layer, 0, :, c], keep[layer, 1, :, c]
            fresh, from_st = keep[layer, 2, :, c], keep[layer, 3, :, c]
            d_upd = d_state * (st[layer, :, c] - fresh) * upd * (1.0 - upd)
            d_fresh = d_state * (1.0 - upd) * (1.0 - fresh * fresh)
            d_reset = d_fresh * from_st * reset * (1.0 - reset)
            d_from_in = jnp.concatenate([d_reset, d_upd, d_fresh], axis=0)
            d_from_st = jnp.concatenate([d_reset, d_upd, d_fresh * reset], axis=0)
            in_s, st_s = split(d_from_in), split(d_from_st)
            gm[:, c] = (mm(gru_n[0], in_s[0]) + mm(gru_n[0], in_s[1])).astype(bf16)
            if layer > 0:
                dst_acc[:, c] = d_state * upd + (mm(gru_n[1], st_s[0]) + mm(gru_n[1], st_s[1]))
            ones = jnp.ones((8, LB), bf16)
            message, state_low = msg[layer, :, c], low[layer, :, c]
            for half, left_m, right_m in ((0, message, in_s), (1, state_low, st_s)):
                grad = mm(left_m, right_m[0], NTR) + mm(left_m, right_m[1], NTR)
                sums = (mm(ones, right_m[0], NTR) + mm(ones, right_m[1], NTR))[:1]
                for q in range(3):
                    r = R_GRU + (half * 3 + q) * H
                    pack[r : r + H, :] += grad[:, q * H : (q + 1) * H]
                    m = R_MISC + M_INPUT + half * 3 + q
                    pack[m : m + 1, :] += sums[:, q * H : (q + 1) * H]
            return carry

        lax.fori_loop(0, chunks, back, 0)
        for k in range(parts):
            gm_rel[k * own_rows : (k + 1) * own_rows, :atoms] = gm[place(k), :]
        if layer > 0:
            bt_high, bt_low = split(jnp.transpose(ebias))

            def pull(b, carry, layer=layer):
                c = columns(b * LB, LB)
                w = window(b)
                grad = mm(gm_rel[:, w], hot_dst[:, c])
                grad_low = grad.astype(bf16)
                g_o[layer, :, c] = grad_low
                hid = hid_i[:, c]
                for i in range(H):
                    z[i * EH : (i + 1) * EH, :] = g_o[layer, pl.ds(i, 1), c] * hid
                pulled = mm(w_back[...], z[...])
                pulled = pulled + (mm(bt_high, grad_low) + mm(bt_low, grad_low))
                dst_acc[:, w] += mm2(pulled, hot_src[:, c], NTR)
                return carry

            lax.fori_loop(0, blocks, pull, 0)
        else:

            def take(b, carry, layer=layer):
                c = columns(b * LB, LB)
                g_o[layer, :, c] = mm(gm_rel[:, window(b)], hot_dst[:, c]).astype(bf16)
                return carry

            lax.fori_loop(0, blocks, take, 0)
    acc_b = acc.at[:, :H]
    acc_b[...] = jnp.zeros((H, H), f32)

    def bias_sum(b, carry):
        c = columns(b * LB, LB)
        acc_b[...] += mm(g_o[0, :, c], src_o[0, :, c], NTR) + mm(
            g_o[1, :, c], src_o[1, :, c], NTR
        )
        return carry

    lax.fori_loop(0, blocks, bias_sum, 0)
    for k in range(parts):
        row = pl.multiple_of(R_EBIAS + places[k], 8)
        pack[pl.ds(row, own_rows), :] = acc_b[k * own_rows : (k + 1) * own_rows, :]
    pack[R_END:R_PACK, :] = jnp.zeros((R_PACK - R_END, 128), f32)


def body_edges(jobs, slots, extra_in, last, meta, *refs):
    n = len(jobs)
    ws, (src, g, hid), refs = refs[:n], refs[n : n + 3], refs[n + 3 :]
    if extra_in == "pack":
        (place, pack), refs = refs[:2], refs[2:]
    else:
        hid_before, refs = refs[0], refs[1:]
    if last:
        (before, feat, sums), refs = refs[:3], refs[3:]
    count = 1 + max(slot for slot, _ in slots)
    outs, result, refs = refs[:count], refs[count], refs[count + 1 :]
    built, acc = refs[:2]
    grad_hid = refs[2] if last else result
    blocks = meta[0]
    rows = ws[0].shape[1] // H
    span = rows * EH

    if extra_in == "pack":
        half = pack.shape[0] // 2
        sent = pack[pl.ds(pl.multiple_of(place[0] * half, half), half), :]
        high, low = split(sent)
        outs[0][span : span + half, :] = high
        outs[0][span + half : span + 2 * half, :] = low

    acc[...] = jnp.zeros_like(acc)

    def edges(b, carry):
        c = columns(b * LB, LB)
        s0, s1 = src[0, :, c].astype(f32), src[1, :, c].astype(f32)
        pulled = None if extra_in == "pack" else hid_before[:, c]
        for q, (rel, chunk) in enumerate(jobs):
            at = (rel * CHUNKS + chunk) * rows
            g0 = g[0, at : at + rows, c].astype(f32)
            g1 = g[1, at : at + rows, c].astype(f32)
            for i in range(rows):
                built[q % 2, i * H : (i + 1) * H, :] = (
                    g0[i : i + 1] * s0 + g1[i : i + 1] * s1
                ).astype(bf16)
            part = mm(ws[q][...], built[q % 2])
            pulled = part if pulled is None else pulled + part
            acc[q] += mm(hid[:, c], built[q % 2], NTR)
        grad_hid[:, c] = pulled
        return carry

    lax.fori_loop(0, blocks, edges, 0)
    for q, (slot, at) in enumerate(slots):
        for i in range(rows):
            r = at + i * EH
            outs[slot][r : r + EH, :] = acc[q, :, i * H : (i + 1) * H].astype(bf16)

    if last:
        result[...] = sums[...]

        def finish(b, carry):
            c = columns(b * LB, LB)
            ahead = before[:, c]
            sig = sigmoid(ahead)
            grad = split(grad_hid[:, c] * sig * (1.0 + ahead * (1.0 - sig)))
            rows_low = feat[:, c].astype(bf16)
            result[...] += mm(rows_low, grad[0], NTR) + mm(rows_low, grad[1], NTR)
            return carry

        lax.fori_loop(0, blocks, finish, 0)
        high, low = split(result[...])
        rest = result[...] - high.astype(f32) - low.astype(f32)
        outs[0][span : span + 32, :] = jnp.concatenate(
            [high.astype(f32), low.astype(f32), rest, jnp.zeros_like(rest)], axis=0
        ).astype(bf16)


def adamw(weight, grad, moment, second):
    moment_new = beta_one * moment + (1.0 - beta_one) * grad
    second_new = beta_two * second + (1.0 - beta_two) * grad * grad
    mean_hat = moment_new / (1.0 - beta_one**STEP_COUNT)
    square_hat = second_new / (1.0 - beta_two**STEP_COUNT)
    return (
        weight - rate * (mean_hat / (jnp.sqrt(square_hat) + epsilon) + decay * weight),
        moment_new,
        second_new,
    )


def body_adamw(own_rows, place, *refs):
    owns, refs = refs[:CHUNKS], refs[CHUNKS:]
    (pack, grad_in, squares), refs = refs[:3], refs[3:]
    params, moments, seconds = refs[0:8], refs[8:16], refs[16:24]
    outs = refs[24:48]
    loss, count, norm = refs[48:51]

    def step(index, grad, at=...):
        new = adamw(params[index][at], grad, moments[index][at], seconds[index][at])
        for kind in range(3):
            outs[kind * 8 + index][at] = new[kind]

    total = squares[0:1, 0:1] + total_of(jnp.square(grad_in[: G_BIAS + 1, :]))
    for k in range(4):
        total = total + total_of(jnp.square(pack[R_LSTM + k * 2 * H : R_LSTM + k * 2 * H + H, :]))
    loss[...] = grad_in[G_SUMS : G_SUMS + 1, 0:1]
    number = grad_in[G_SUMS : G_SUMS + 1, 1:2]
    count[...] = number
    grad_norm = jnp.sqrt(total) / number
    norm[...] = grad_norm
    factor = jnp.minimum(1.0, clip_norm / grad_norm) / number
    step(0, grad_in[:EIN, :] * factor)
    step(2, pack[pl.ds(pl.multiple_of(R_EBIAS + place[0], 8), own_rows), :] * factor)
    for half in range(2):
        for q in range(3):
            r = R_GRU + (half * 3 + q) * H
            step(3, pack[r : r + H, :] * factor, (half, slice(None), slice(q * H, (q + 1) * H)))
    for k in range(4):
        r = R_LSTM + k * 2 * H
        for block, start in ((0, 0), (1, H), (2, 0)):
            step(
                4,
                pack[r + start : r + start + H, :] * factor,
                (slice(block * H, (block + 1) * H), slice(k * H, (k + 1) * H)),
            )
    step(5, pack[R_FIRST:R_GRU, :] * factor)
    step(6, pack[R_SECOND : R_SECOND + NT, :] * factor)
    bias = jnp.concatenate(
        [grad_in[G_BIAS : G_BIAS + 1, :], pack[R_MISC + 1 : R_EBIAS, :]], axis=0
    )
    step(7, bias * factor)

    rows = own_rows // CHUNKS
    for c in range(CHUNKS):
        for i in range(rows):
            at = (c * rows + i) * H
            step(1, owns[c][i * EH : (i + 1) * EH, :] * factor, (slice(None), slice(at, at + H)))


VM = pl.BlockSpec(memory_space=pltpu.VMEM)
SM = pl.BlockSpec(memory_space=pltpu.SMEM)


def per_device(
    node_feats,
    edge_feats,
    edge_ends,
    atom_counts,
    dataset_flags,
    targets,
    present,
    edge_in,
    edge_out,
    edge_bias,
    gru_weights,
    lstm_weights,
    head_first,
    head_second,
    biases,
    *moments_seconds,
):
    row = lax.axis_index("row")
    row_count = lax.axis_size("row")
    mol = lax.axis_index("mol")
    mol_bits = lax.axis_size("mol").bit_length() - 1
    row_bits = row_count.bit_length() - 1
    mols = node_feats.shape[0]
    own_rows = edge_out.shape[1] // H
    atoms = -(-mols * ATOMS // LB) * LB
    space = -(-mols * LIVE // LB) * LB

    def row_swap(x, k):
        return lax.ppermute(x, "row", [(i, i ^ k) for i in range(row_count)])

    def mol_swap(x, bit):
        return lax.ppermute(x, "mol", [(i, i ^ (1 << bit)) for i in range(2**mol_bits)])

    def double(x, swap, bit):
        other = swap(x)
        return jnp.concatenate(
            [jnp.where(bit == 0, x, other), jnp.where(bit == 0, other, x)], axis=0
        )

    sds = jax.ShapeDtypeStruct
    n = row_count
    al = atoms + WINDOW - 128
    params = pltpu.CompilerParams(vmem_limit_bytes=56 * MIB)

    sent = edge_out.astype(bf16)
    bias_sent = edge_bias.reshape(own_rows, H)

    def forward_order(part):
        part = part.reshape(EH, own_rows, H)
        return part.transpose(1, 0, 2).reshape(own_rows, EH * H)

    parts, bias_parts = {0: sent}, {0: bias_sent}
    for bit in reversed(range(row_bits)):
        parts[1 << bit] = row_swap(sent, 1 << bit)
        bias_parts[1 << bit] = row_swap(bias_sent, 1 << bit)

    ends = lax.dynamic_slice_in_dim(edge_ends, row * mols, mols, 1)
    feats = lax.dynamic_slice_in_dim(edge_feats, row * mols * EM, mols * EM, 1)
    table = jnp.concatenate([feats.reshape(EIN, mols, EM), ends.astype(bf16)], axis=0)
    table = table.transpose(1, 0, 2).reshape(mols, (EIN + 2) * EM)
    places = jnp.stack([(row ^ k) * own_rows for k in range(row_count)]).astype(jnp.int32)
    bias_rows = jnp.pad(biases, (0, 16 * 128 - biases.shape[0])).reshape(16, 128)

    prepared = pl.pallas_call(
        functools.partial(body_prepare, mols),
        out_shape=(
            sds((2 + space // LB,), jnp.int32),
            sds((H, atoms), bf16),
            sds((EH, space), bf16),
            sds((EH, space), f32),
            sds((8, space), f32),
            sds((WINDOW, space), bf16),
            sds((WINDOW, space), bf16),
        ),
        in_specs=[SM] + [VM] * 4,
        out_specs=(SM,) + (VM,) * 6,
        scratch_shapes=[pltpu.VMEM((128, 128), f32), pltpu.VMEM((mols * PAD, H), f32)],
        compiler_params=params,
    )(atom_counts, table, node_feats, edge_in, bias_rows)
    forward = {k: forward_order(part) for k, part in parts.items() if k < n // 2}
    parts, bias_parts, prepared, forward = lax.optimization_barrier(
        (parts, bias_parts, prepared, forward)
    )
    meta, nodes, hid, before, feat, hot_src, hot_dst = prepared
    for bit in reversed(range(row_bits)):
        for k in [k for k in parts if k > 1 << bit and not k & (1 << bit)]:
            parts[k + (1 << bit)] = row_swap(parts[k], 1 << bit)
            bias_parts[k + (1 << bit)] = row_swap(bias_parts[k], 1 << bit)
    parts = [parts[k] for k in range(n)]
    bias_parts = [bias_parts[k] for k in range(n)]
    w_fwd = [forward[k] if k in forward else forward_order(parts[k]) for k in range(n)]

    def main(*refs):
        at = 10
        body_main(
            mols,
            own_rows,
            *refs[:at],
            refs[at : at + n],
            refs[at + n : at + 2 * n],
            refs[at + 2 * n : at + 3 * n],
            *refs[at + 3 * n :],
        )

    pack, sums, src, g = pl.pallas_call(
        main,
        out_shape=(
            sds((R_PACK, 128), f32),
            sds((8, 128), f32),
            sds((LAYERS, H, space), bf16),
            sds((LAYERS, H, space), bf16),
        ),
        in_specs=[SM] * 4 + [VM] * (11 + 3 * n),
        out_specs=(VM,) * 4,
        scratch_shapes=[
            pltpu.VMEM((H * EH, LB), bf16),
            pltpu.VMEM((LAYERS + 1, H, atoms), f32),
            pltpu.VMEM((LAYERS, H, al), bf16),
            pltpu.VMEM((LAYERS, H, atoms), bf16),
            pltpu.VMEM((LAYERS, 4, H, atoms), f32),
            pltpu.VMEM((H, al), f32),
            pltpu.VMEM((H, al), f32),
            pltpu.VMEM((H, atoms), bf16),
            pltpu.VMEM((H, al), bf16),
            pltpu.VMEM((H, H * EH), bf16),
            pltpu.VMEM((STEPS * mols, atoms), f32),
            pltpu.VMEM((STEPS * mols, atoms), f32),
            pltpu.VMEM((2, H, 3 * H), bf16),
            pltpu.VMEM((2, 3 * H, H), bf16),
            pltpu.VMEM((128, 128), f32),
        ],
        compiler_params=pltpu.CompilerParams(vmem_limit_bytes=60 * MIB),
    )(
        atom_counts,
        dataset_flags,
        places,
        meta,
        targets.T,
        present.T,
        nodes,
        hid,
        hot_src,
        hot_dst,
        *w_fwd,
        *parts,
        *bias_parts,
        gru_weights,
        bias_rows,
        lstm_weights,
        head_first,
        head_second.T,
    )

    span = own_rows * H // CHUNKS

    def edge_parts(jobs, slots, heights, extra, last):
        kind = "pack" if len(extra) == 2 else "sum"
        if last:
            extra = extra + (before, feat, sums)
        *found, result = pl.pallas_call(
            functools.partial(body_edges, jobs, slots, kind, last),
            grid=(1,),
            out_shape=tuple(sds((height, EH), bf16) for height in heights)
            + (sds((8, EH) if last else (EH, space), f32),),
            in_specs=[SM]
            + [pl.BlockSpec((EH, span), lambda i, c=chunk: (0, c)) for _, chunk in jobs]
            + [VM] * 3
            + ([SM, VM] if kind == "pack" else [VM] * len(extra)),
            out_specs=(VM,) * (len(heights) + 1),
            scratch_shapes=[
                pltpu.VMEM((2, span, LB), bf16),
                pltpu.VMEM((len(jobs), EH, span), f32),
            ]
            + ([pltpu.VMEM((EH, space), f32)] if last else []),
            compiler_params=params,
        )(meta, *(parts[k] for k, _ in jobs), src, g, hid, *extra)
        return found, result

    row_steps = [(functools.partial(row_swap, k=1 << b), (row >> b) & 1) for b in range(row_bits)]
    mol_steps = [(functools.partial(mol_swap, bit=b), (mol >> b) & 1) for b in range(mol_bits)]
    tie = lax.optimization_barrier
    (core, core_bit), (cross, cross_bit) = row_steps

    def halves(x, bit):
        both = x.reshape((2, x.shape[0] // 2) + x.shape[1:])
        return (
            lax.dynamic_index_in_dim(both, 1 - bit, 0, False),
            lax.dynamic_index_in_dim(both, bit, 0, False),
        )

    def as_low(x, count):
        found = []
        for _ in range(count):
            high = lax.reduce_precision(x, 8, 7)
            found.append(high)
            x = x - high
        return jnp.concatenate(found, axis=0).astype(bf16)

    def from_low(x, count):
        x = x.astype(f32).reshape(count, -1, 128)
        found = x[count - 1]
        for k in reversed(range(count - 1)):
            found = found + x[k]
        return found

    def chain(own, pack, beside):
        for swap, bit in mol_steps:
            own_sent, own = halves(own, bit)
            half = own.shape[0]
            sent = [own_sent.astype(bf16)]
            if pack is not None:
                pack_sent, pack = halves(pack, bit)
                sent.append(as_low(pack_sent, 2))
            if beside is not None:
                sent.append(as_low(beside["rows"], 3))
            came = yield swap, jnp.concatenate(sent, axis=0) if len(sent) > 1 else sent[0]
            own = own + came[:half].astype(f32)
            if pack is not None:
                pack = pack + from_low(came[half : half + 2 * pack.shape[0]], 2)
            if beside is not None:
                beside["rows"] = beside["rows"] + from_low(came[half:], 3)
        piece = own if pack is None else jnp.concatenate([own, pack], axis=0)
        height, rest = piece.shape[0], own.shape[0]
        largest = jnp.maximum(jnp.max(jnp.abs(piece)), 1e-30)
        power = 14.0 - jnp.ceil(jnp.log2(largest))
        sent = jnp.concatenate(
            [piece * jnp.exp2(power), jnp.broadcast_to(power, (16, 128))], axis=0
        ).astype(jnp.float16)
        for swap, bit in reversed(mol_steps):
            came = yield swap, sent
            sent = jnp.concatenate(
                [jnp.where(bit == 0, sent, came), jnp.where(bit == 0, came, sent)], axis=0
            )
        sent = sent.astype(f32).reshape(-1, height + 16, 128)
        back = jnp.exp2(-sent[:, height : height + 1, 0:1])
        own = (sent[:, :rest] * back).reshape(-1, 128)
        square = jnp.sum(own * own)
        if pack is not None:
            pack = (sent[:, rest:height] * back).reshape(-1, 128)
            square = square + jnp.sum(pack * pack)
        return own, pack, square

    core_place = (1 - core_bit).reshape(1).astype(jnp.int32)
    half = pack.shape[0] // 2
    (message, far), carry = edge_parts(
        ((2, 0), (3, 0)),
        ((1, 0), (0, 0)),
        (span + 2 * half, span),
        (core_place, pack),
        False,
    )
    came = core(message)
    pack = halves(pack, core_bit)[1]
    pack_sent, pack = halves(pack + from_low(came[span:], 2), cross_bit)
    sent = (far.astype(f32) + came[:span].astype(f32)).astype(bf16)
    sent = jnp.concatenate([sent, as_low(pack_sent, 2)], axis=0)
    sent, carry = tie((sent, carry))
    arrived = cross(sent)
    (message, near, far), carry = edge_parts(
        ((0, 0), (1, 0), (2, 1), (3, 1)),
        ((1, 0), (0, 0), (2, 0), (0, span)),
        (2 * span, span, span),
        (carry,),
        False,
    )
    message, arrived = tie((message, arrived))
    came = core(message)
    own = near.astype(f32) + came[:span].astype(f32) + arrived[:span].astype(f32)
    pack = pack + from_low(arrived[span:], 2)
    sent = (far.astype(f32) + came[span:].astype(f32)).astype(bf16)

    first = chain(own, pack, None)
    first_swap, first_sent = next(first)
    sent, first_sent, carry = tie((sent, first_sent, carry))
    arrived = cross(sent)
    first_came = first_swap(first_sent)
    (message, near), grad_in = edge_parts(
        ((0, 1), (1, 1)), ((1, 0), (0, 0)), (span + 32, span), (carry,), True
    )
    message, arrived, first_came = tie((message, arrived, first_came))
    came = core(message)
    beside = {"rows": grad_in + from_low(came[span : span + 24], 3)}
    own = near.astype(f32) + came[:span].astype(f32) + arrived.astype(f32)

    second = chain(own, None, beside)
    second_swap, second_sent = next(second)
    first_swap, first_sent = first.send(first_came)
    while True:
        first_sent, second_sent = tie((first_sent, second_sent))
        first_came, second_came = first_swap(first_sent), second_swap(second_sent)
        second_swap, second_sent = second.send(second_came)
        try:
            first_swap, first_sent = first.send(first_came)
        except StopIteration as end:
            first_own, pack, square = end.value
            break
    quarters = jnp.concatenate([pack, beside["rows"]], axis=0)
    quarters, second_sent = tie((quarters, second_sent))
    came, second_came = cross(quarters), second_swap(second_sent)
    try:
        second.send(second_came)
    except StopIteration as end:
        second_own, _, more = end.value
    grad_in = beside["rows"] + came[-8:]
    came = came[:-8]
    pack = jnp.concatenate(
        [jnp.where(cross_bit == 0, pack, came), jnp.where(cross_bit == 0, came, pack)], axis=0
    )
    pack = double(pack, core, core_bit)
    squares = jnp.broadcast_to(square + more, (8, 128))
    squares = (squares + row_swap(squares, 1)) + (row_swap(squares, 2) + row_swap(squares, 3))
    owns = [first_own, second_own]

    weights = [
        edge_in,
        edge_out,
        edge_bias,
        gru_weights,
        lstm_weights,
        head_first,
        head_second,
        biases,
    ]
    states = []
    for group in (weights, moments_seconds[:8], moments_seconds[8:]):
        group = list(group)
        group[2] = group[2].reshape(own_rows, H)
        group[6] = group[6].T
        if group[7] is biases:
            group[7] = bias_rows
        else:
            group[7] = jnp.pad(group[7], (0, 16 * 128 - group[7].shape[0])).reshape(16, 128)
        states += group
    shapes = [sds(state.shape, f32) for state in states]
    results = pl.pallas_call(
        functools.partial(body_adamw, own_rows),
        out_shape=tuple(shapes) + (sds((1, 1), f32),) * 3,
        in_specs=[SM] + [VM] * (CHUNKS + 3 + len(shapes)),
        out_specs=(VM,) * (len(shapes) + 3),
        compiler_params=params,
    )(places, *owns, pack, grad_in, squares, *states)
    results = list(results)
    for kind in range(3):
        results[kind * 8 + 2] = results[kind * 8 + 2].reshape(own_rows * H)
        results[kind * 8 + 6] = results[kind * 8 + 6].T
        results[kind * 8 + 7] = results[kind * 8 + 7].reshape(-1)[: biases.shape[0]]
    for index in range(24, 27):
        results[index] = results[index].reshape(())
    return tuple(results)


def solution(mesh):
    weights = (P(), P(None, "row"), P("row"), P(), P(), P(), P(), P())
    in_specs = (
        P(("mol", "row"), None, None),
        P(None, "mol"),
        P(None, "mol", None),
        P(("mol", "row")),
        P(("mol", "row")),
        P(("mol", "row"), None),
        P(("mol", "row"), None),
    ) + weights * 3
    out_specs = weights * 3 + (P(), P(), P())
    return jax.shard_map(
        per_device, mesh=mesh, in_specs=in_specs, out_specs=out_specs, check_vma=False
    )
```

```python
import functools
import math

import jax
import jax.numpy as jnp
from jax import lax
from jax.experimental import pallas as pl
from jax.experimental.pallas import tpu as pltpu
from jax.sharding import PartitionSpec as P

H = 128
EH = 128
EIN = 5
NT = 12
STEPS = 6
ATOMS = 29
EM = 64
LAYERS = 2
STEP_COUNT = 10

PAD = 32
LIVE = 2 * (ATOMS - 1)
LB = 256
MIB = 2**20

f32 = jnp.float32
bf16 = jnp.bfloat16
highest = lax.Precision.HIGHEST
beta_one = 0.9
beta_two = 0.999
rate = 0.05
epsilon = 1e-08
decay = 0.01
clip_norm = 0.1

R_LSTM, R_FIRST, R_GRU, R_SECOND, R_MISC, R_EBIAS, R_END = 0, 1024, 1280, 2048, 2064, 2080, 2208
R_PACK = 2560
M_INPUT, M_LSTM, M_HEAD, M_OUT = 1, 7, 11, 12
G_BIAS, G_SUMS = EIN, EIN + 1
WINDOW = 384
CHUNKS = 2

NN = ((1,), (0,))
NTR = ((1,), (1,))
TN = ((0,), (0,))


def mm(a, b, dims=NN):
    return lax.dot_general(a, b, (dims, ((), ())), preferred_element_type=f32)


def split(x):
    high = x.astype(bf16)
    return high, (x - high.astype(f32)).astype(bf16)


def mm3(a, b, dims=NN):
    if dims[0] == (1,) and a[0].shape[0] in (16, 32, 64):
        rows = a[0].shape[0]
        both = mm(jnp.concatenate(a, axis=0), b[0], dims)
        return both[:rows] + (both[rows:] + mm(a[0], b[1], dims))
    return mm(a[0], b[0], dims) + (mm(a[0], b[1], dims) + mm(a[1], b[0], dims))


def mm2(a, b, dims=NN):
    high, low = split(a)
    return mm(high, b, dims) + mm(low, b, dims)


def total_of(x):
    return jnp.sum(jnp.sum(x, axis=1, keepdims=True), axis=0, keepdims=True)


def columns(start, size):
    return pl.ds(pl.multiple_of(start, size), size)


def sigmoid(v):
    return jax.nn.sigmoid(v)


def column_of(values, size):
    at = lax.broadcasted_iota(jnp.int32, (size, 1), 0)
    found = jnp.zeros((size, 1), jnp.int32)
    for m in range(size):
        found = jnp.where(at == m, values[m], found)
    return found


def row_of(values, size):
    at = lax.broadcasted_iota(jnp.int32, (1, size), 1)
    found = jnp.zeros((1, size), jnp.int32)
    for m in range(size):
        found = jnp.where(at == m, values[m], found)
    return found


def starts_of(column, size):
    below = (
        lax.broadcasted_iota(jnp.int32, (size, size), 1)
        < lax.broadcasted_iota(jnp.int32, (size, size), 0)
    ).astype(bf16)
    return mm(below, jnp.broadcast_to(column, (size, 128)).astype(bf16))[:, :1]


def body_prepare(
    mols,
    counts_s,
    table,
    node_feats,
    edge_in,
    bias_rows,
    nat,
    meta,
    nodes_o,
    hid_o,
    before_o,
    feat_o,
    hot_src,
    hot_dst,
    turned_o,
    square,
    flat,
):
    lanes = nodes_o.shape[1]
    space = hid_o.shape[1]
    for b in range(space // LB):
        meta[2 + b] = jnp.int32(0)
    edges, atoms = jnp.int32(0), jnp.int32(0)
    for m in range(mols):
        live = 2 * (counts_s[m] - 1)
        block = lax.div(edges + (LB - 1), jnp.int32(LB))

        @pl.when(block * LB < edges + live)
        def _(block=block, atoms=atoms):
            meta[2 + block] = lax.div(atoms, jnp.int32(128)) * 128

        edges = edges + live
        atoms = atoms + counts_s[m]
    blocks = lax.div(edges + (LB - 1), jnp.int32(LB))
    meta[0] = blocks
    meta[1] = lax.div(atoms + (LB - 1), jnp.int32(LB))

    count_col = column_of(counts_s, mols).astype(f32)
    live_col = 2.0 * (count_col - 1.0)
    start_col = starts_of(live_col, mols)
    atom_col = starts_of(count_col, mols)

    width = nat[0].shape[1]

    def turn(i, carry):
        for k, part in enumerate(nat):
            turned_o[:, pl.ds(pl.multiple_of(k * width + i * H, H), H)] = jnp.transpose(
                part[:, columns(i * H, H)]
            )
        return carry

    lax.fori_loop(0, width // H, turn, 0)

    square[...] = jnp.zeros_like(square)
    square[0:EIN, :] = edge_in[...]
    square[8:24, :] = bias_rows[...]
    turned = jnp.transpose(square[...])
    in_t, b_in_col = turned[:, :8], turned[:, 8:9]
    e_high, e_low = split(in_t)
    e_rest = (in_t - e_high.astype(f32) - e_low.astype(f32)).astype(bf16)

    flat[...] = jnp.zeros_like(flat)
    for m in range(mols):
        flat[m * PAD : m * PAD + ATOMS, :] = node_feats[m].astype(f32)
    flat_low = flat[...].astype(bf16)
    nodes_o[...] = jnp.zeros_like(nodes_o)
    atom_at = lax.broadcasted_iota(jnp.int32, (mols * PAD, 1), 0)
    spread = (
        lax.broadcasted_iota(jnp.int32, (mols * PAD, mols), 0) // PAD
        == lax.broadcasted_iota(jnp.int32, (mols * PAD, mols), 1)
    ).astype(bf16)
    goal_high = jnp.floor(atom_col * (1.0 / 8.0))
    goal_parts = jnp.concatenate([goal_high, atom_col - 8.0 * goal_high, count_col], axis=1)
    goal = mm(
        spread,
        jnp.concatenate([goal_parts, jnp.zeros((mols, 125), f32)], axis=1).astype(bf16),
    )
    within = lax.rem(atom_at, jnp.int32(PAD)).astype(f32)
    target = jnp.where(
        within < goal[:, 2:3], 8.0 * goal[:, 0:1] + goal[:, 1:2] + within, -1.0
    ).astype(jnp.int32)

    def pack_atoms(k, carry):
        c = columns(k * LB, LB)
        at = lax.broadcasted_iota(jnp.int32, (mols * PAD, LB), 1) + k * LB
        hot = (at == target).astype(f32).astype(bf16)
        nodes_o[:, c] = mm(flat_low, hot, TN).astype(bf16)
        return carry

    lax.fori_loop(0, meta[1], pack_atoms, 0)

    def prepare(b, carry):
        c = columns(b * LB, LB)
        spot = (lax.broadcasted_iota(jnp.int32, (mols, LB), 1) + b * LB).astype(f32)
        mol_hot = ((spot >= start_col) & (spot < start_col + live_col)).astype(f32)
        rows = mm(table[...], mol_hot.astype(bf16), TN)
        start_row = jnp.sum(mol_hot * start_col, axis=0, keepdims=True)
        base = jnp.sum(mol_hot * atom_col, axis=0, keepdims=True)
        valid = jnp.sum(mol_hot, axis=0, keepdims=True)
        slot = spot[:1] - start_row
        slot_hot = (lax.broadcasted_iota(jnp.int32, (EM, LB), 0).astype(f32) == slot).astype(f32)
        picked = [
            jnp.sum(rows[r * EM : (r + 1) * EM] * slot_hot, axis=0, keepdims=True)
            for r in range(EIN + 2)
        ]
        feat = jnp.concatenate(picked[:EIN] + [valid, jnp.zeros((2, LB), f32)], axis=0)
        feat_o[:, c] = feat
        feat_low = feat.astype(bf16)
        before = mm(e_high, feat_low) + mm(e_low, feat_low) + mm(e_rest, feat_low) + b_in_col
        before_o[:, c] = before
        hid_o[:, c] = (before * sigmoid(before)).astype(bf16)
        atom = lax.broadcasted_iota(jnp.int32, (WINDOW, LB), 0)
        base = base - meta[2 + b].astype(f32)
        src = jnp.where(valid > 0.5, base + picked[EIN], -1.0).astype(jnp.int32)
        dst = jnp.where(valid > 0.5, base + picked[EIN + 1], -1.0).astype(jnp.int32)
        hot_src[:, c] = (atom == src).astype(f32).astype(bf16)
        hot_dst[:, c] = (atom == dst).astype(f32).astype(bf16)
        return carry

    lax.fori_loop(0, 2 * lax.div(blocks + 1, jnp.int32(2)), prepare, 0)


def body_main(
    mols,
    own_rows,
    counts_s,
    flags_s,
    places,
    meta,
    targets,
    present,
    nodes,
    hid_i,
    hot_src,
    hot_dst,
    w_fwd,
    turned_h,
    nat_h,
    ebias_parts,
    gru,
    bias_rows,
    lstm_rows,
    first,
    second,
    pack,
    sums_o,
    src_o,
    g_o,
    z,
    st,
    low,
    msg,
    keep,
    acc,
    dst_acc,
    gm,
    gm_rel,
    w_back,
    w_all,
    ds_all,
    gru_n,
    gru_t,
    square,
    moved_s,
    w_nat,
    late_sem,
):
    parts = len(w_fwd)
    blocks, chunks = meta[0], meta[1]
    turned_width = turned_h.shape[1]
    late = [pltpu.make_async_copy(turned_h, w_back.at[:, :turned_width], late_sem.at[0])]
    for k in range(len(nat_h)):
        late.append(pltpu.make_async_copy(nat_h[k], w_nat.at[k], late_sem.at[1 + k]))
    for copy in late:
        copy.start()
    atoms = w_all.shape[1]

    def place(k):
        return pl.ds(pl.multiple_of(places[k], own_rows), own_rows)

    def window(b):
        return pl.ds(pl.multiple_of(meta[2 + b], 128), WINDOW)

    square[...] = jnp.zeros_like(square)
    square[0:16, :] = bias_rows[...]
    turned = jnp.transpose(square[...])
    gbias_col = [
        jnp.concatenate([turned[:, r + q : r + q + 1] for q in range(3)], axis=0)
        for r in (M_INPUT, M_INPUT + 3)
    ]
    c_lstm = jnp.concatenate(
        [bias_rows[M_LSTM + k : M_LSTM + k + 1, :] for k in range(4)], axis=1
    )
    c_head = bias_rows[M_HEAD : M_HEAD + 1, :]
    out_cols = [turned[k * NT : (k + 1) * NT, M_OUT : M_OUT + 1] for k in range(3)]
    gru_n[...] = gru[...].astype(bf16)
    for half in range(2):
        for q in range(3):
            gru_t[half, q * H : (q + 1) * H, :] = jnp.transpose(
                gru_n[half, :, q * H : (q + 1) * H]
            )
    ebias = jnp.concatenate([part[...] for part in ebias_parts], axis=0)
    b_high, b_low = split(ebias)

    def in_pairs(step):
        def both(p, carry):
            step(2 * p)
            step(2 * p + 1)
            return carry

        lax.fori_loop(0, lax.div(blocks + 1, jnp.int32(2)), both, 0)

    def deliver(into, hot):
        def both(p, carry):
            found = []
            for u in range(2):
                c = columns((2 * p + u) * LB, LB)
                found.append(mm2(moved_s[:, c], hot[:, c], NTR))
            for u in range(2):
                into[:, window(2 * p + u)] += found[u]
            return carry

        lax.fori_loop(0, lax.div(blocks + 1, jnp.int32(2)), both, 0)

    b_fwd = jnp.concatenate([b_high, b_low], axis=1)
    moved_s[...] = jnp.zeros_like(moved_s)

    for layer in range(LAYERS):
        low[layer] = jnp.zeros_like(low[layer])
    low[0, :, :atoms] = nodes[...]
    st[0] = nodes[...].astype(f32)
    st[LAYERS] = jnp.zeros_like(st[LAYERS])
    gm_rel[...] = jnp.zeros_like(gm_rel)
    for layer in range(LAYERS):
        acc[...] = jnp.zeros_like(acc)

        def fetch(b, layer=layer):
            c = columns(b * LB, LB)
            src_o[layer, :, c] = mm(low[layer, :, window(b)], hot_src[:, c]).astype(bf16)

        def move(b, carry, layer=layer):
            c = columns(b * LB, LB)
            source = src_o[layer, :, c]
            for h in range(EH):
                z[h * H : (h + 1) * H, :] = hid_i[pl.ds(h, 1), c] * source
            moved_s[:, c] = mm(jnp.concatenate([part[...] for part in w_fwd], axis=0), z[...]) + mm(
                b_fwd, jnp.concatenate([source, source], axis=0)
            )
            return carry

        in_pairs(fetch)
        lax.fori_loop(0, blocks, move, 0)
        deliver(acc, hot_dst)
        for k in range(parts):
            msg[layer, place(k), :] = acc[k * own_rows : (k + 1) * own_rows, :atoms].astype(bf16)

        def update(k, carry, layer=layer):
            c = columns(k * LB, LB)
            from_in = mm(gru_t[0], msg[layer, :, c]) + gbias_col[0]
            from_st = mm(gru_t[1], low[layer, :, c]) + gbias_col[1]
            reset = sigmoid(from_in[:H] + from_st[:H])
            upd = sigmoid(from_in[H : 2 * H] + from_st[H : 2 * H])
            fresh = jnp.tanh(from_in[2 * H :] + reset * from_st[2 * H :])
            new = (1.0 - upd) * fresh + upd * st[layer, :, c]
            st[layer + 1, :, c] = new
            if layer + 1 < LAYERS:
                low[layer + 1, :, c] = new.astype(bf16)
            keep[layer, 0, :, c] = reset
            keep[layer, 1, :, c] = upd
            keep[layer, 2, :, c] = fresh
            keep[layer, 3, :, c] = from_st[2 * H :]
            return carry

        lax.fori_loop(0, chunks, update, 0)

    lane = lax.broadcasted_iota(jnp.int32, (mols, atoms), 1).astype(f32)
    count_col = column_of(counts_s, mols).astype(f32)
    slot_of = lane - starts_of(count_col, mols)
    alive = (slot_of >= 0.0) & (slot_of < count_col)
    x = split(st[LAYERS])
    lstm = jnp.concatenate(
        [lstm_rows[0:H, :] + lstm_rows[2 * H : 3 * H, :], lstm_rows[H : 2 * H, :]], axis=0
    )
    lstm_w = split(lstm)
    zeros = jnp.zeros((mols, H), f32)
    hidden, read, cell = zeros, zeros, zeros
    saved = []
    for step in range(STEPS):
        query = jnp.concatenate([hidden, read], axis=1)
        if step == 0:
            gates = jnp.broadcast_to(c_lstm, (mols, 4 * H))
        else:
            gates = mm3(split(query), lstm_w) + c_lstm
        in_gate = sigmoid(gates[:, :H])
        forget = sigmoid(gates[:, H : 2 * H])
        part = jnp.tanh(gates[:, 2 * H : 3 * H])
        out_gate = sigmoid(gates[:, 3 * H :])
        before_cell = cell
        cell = forget * cell + in_gate * part
        squashed = jnp.tanh(cell)
        hidden = out_gate * squashed
        scores = jnp.where(alive, mm3(split(hidden), x), -1e30)
        weights = jnp.where(alive, jnp.exp(scores - jnp.max(scores, axis=1, keepdims=True)), 0.0)
        weights = weights / jnp.sum(weights, axis=1, keepdims=True)
        w_all[step * mols : (step + 1) * mols, :] = weights
        read = mm3(split(weights), x, NTR)
        saved.append((query, in_gate, forget, part, out_gate, before_cell, squashed, hidden))
    query = jnp.concatenate([hidden, read], axis=1)
    first_w = split(first[...])
    second_w = split(second[...])
    query_s = split(query)
    inner_pre = mm3(query_s, first_w) + c_head
    inner_sig = sigmoid(inner_pre)
    inner = inner_pre * inner_sig
    inner_s = split(inner)
    is_one = row_of(flags_s, mols) == 1
    predicted = (
        mm3(second_w, inner_s, NTR)
        + out_cols[0]
        + jnp.where(is_one, out_cols[2], out_cols[1])
    )
    there = present[...].astype(f32)
    diff = predicted - targets[...]
    lanes = lax.broadcasted_iota(jnp.int32, (1, 128), 1)
    loss = total_of(there * diff * diff)
    count = total_of(there)
    sums_o[...] = jnp.zeros_like(sums_o)
    sums_o[G_SUMS : G_SUMS + 1, :] = jnp.where(lanes == 0, loss, jnp.where(lanes == 1, count, 0.0))

    d_pred = 2.0 * there * diff
    d_pred_s = split(d_pred)
    pack[R_SECOND:R_MISC, :] = jnp.zeros((R_MISC - R_SECOND, 128), f32)
    pack[R_SECOND : R_SECOND + NT, :] = mm3(d_pred_s, inner_s)
    pack[R_MISC:R_EBIAS, :] = jnp.zeros((R_EBIAS - R_MISC, 128), f32)
    zero_pred = jnp.where(is_one, 0.0, d_pred)
    out_sums = jnp.concatenate([d_pred, zero_pred, d_pred - zero_pred], axis=0)
    out_high, out_low = split(out_sums)
    out_ones = jnp.ones((8, mols), bf16)
    pack[R_MISC + M_OUT : R_MISC + M_OUT + 1, : 3 * NT] = (
        mm(out_ones, out_high, NTR) + mm(out_ones, out_low, NTR)
    )[:1]
    d_inner = mm3(d_pred_s, second_w, TN)
    d_pre = d_inner * inner_sig * (1.0 + inner_pre * (1.0 - inner_sig))
    d_pre_s = split(d_pre)
    pack[R_FIRST:R_GRU, :] = mm3(query_s, d_pre_s, TN)
    pack[R_MISC + M_HEAD : R_MISC + M_HEAD + 1, :] = jnp.sum(d_pre, axis=0, keepdims=True)
    d_query = mm3(d_pre_s, first_w, NTR)
    d_hidden, d_read = d_query[:, :H], d_query[:, H:]
    d_cell = zeros
    d_gates_all = [None] * STEPS
    d_reads = [None] * STEPS
    for step in reversed(range(STEPS)):
        query, in_gate, forget, part, out_gate, before_cell, squashed, hid_t = saved[step]
        weights = w_all[step * mols : (step + 1) * mols, :]
        d_read_s = split(d_read)
        d_reads[step] = d_read
        d_weights = mm3(d_read_s, x)
        d_scores = weights * (d_weights - jnp.sum(weights * d_weights, axis=1, keepdims=True))
        ds_all[step * mols : (step + 1) * mols, :] = d_scores
        d_hidden = d_hidden + mm3(split(d_scores), x, NTR)
        d_out = d_hidden * squashed * out_gate * (1.0 - out_gate)
        d_cell = d_cell + d_hidden * out_gate * (1.0 - squashed * squashed)
        d_forget = d_cell * before_cell * forget * (1.0 - forget)
        d_in = d_cell * part * in_gate * (1.0 - in_gate)
        d_part = d_cell * in_gate * (1.0 - part * part)
        d_cell = d_cell * forget
        d_gates = jnp.concatenate([d_in, d_forget, d_part, d_out], axis=1)
        d_gates_all[step] = d_gates
        if step > 0:
            d_query = mm3(split(d_gates), lstm_w, NTR)
            d_hidden, d_read = d_query[:, :H], d_query[:, H:]
    queries = split(jnp.concatenate([saved[s][0] for s in range(STEPS)], axis=0))
    d_gates_cat = jnp.concatenate(d_gates_all, axis=0)
    d_gates_s = split(d_gates_cat)
    grad_lstm = mm3(queries, d_gates_s, TN)
    d_gates_sum = jnp.sum(d_gates_cat, axis=0, keepdims=True)
    for k in range(4):
        pack[R_LSTM + k * 256 : R_LSTM + (k + 1) * 256, :] = grad_lstm[:, k * H : (k + 1) * H]
        pack[R_MISC + M_LSTM + k : R_MISC + M_LSTM + k + 1, :] = d_gates_sum[:, k * H : (k + 1) * H]
    left = jnp.concatenate(d_reads + [saved[s][7] for s in range(STEPS)], axis=0)
    left_s = split(left)

    def spread(k, carry):
        c = columns(k * LB, LB)
        right = split(jnp.concatenate([w_all[:, c], ds_all[:, c]], axis=0))
        dst_acc[:, c] = mm3(left_s, right, TN)
        return carry

    dst_acc[...] = jnp.zeros_like(dst_acc)
    lax.fori_loop(0, chunks, spread, 0)

    pack[R_GRU:R_SECOND, :] = jnp.zeros((6 * H, 128), f32)
    gm[...] = jnp.zeros_like(gm)
    for layer in reversed(range(LAYERS)):

        def back(k, carry, layer=layer):
            c = columns(k * LB, LB)
            d_state = dst_acc[:, c]
            reset, upd = keep[layer, 0, :, c], keep[layer, 1, :, c]
            fresh, from_st = keep[layer, 2, :, c], keep[layer, 3, :, c]
            d_upd = d_state * (st[layer, :, c] - fresh) * upd * (1.0 - upd)
            d_fresh = d_state * (1.0 - upd) * (1.0 - fresh * fresh)
            d_reset = d_fresh * from_st * reset * (1.0 - reset)
            d_from_in = jnp.concatenate([d_reset, d_upd, d_fresh], axis=0)
            d_from_st = jnp.concatenate([d_reset, d_upd, d_fresh * reset], axis=0)
            in_s, st_s = split(d_from_in), split(d_from_st)
            gm[:, c] = (mm(gru_n[0], in_s[0]) + mm(gru_n[0], in_s[1])).astype(bf16)
            if layer > 0:
                dst_acc[:, c] = d_state * upd + (mm(gru_n[1], st_s[0]) + mm(gru_n[1], st_s[1]))
            ones = jnp.ones((8, LB), bf16)
            message, state_low = msg[layer, :, c], low[layer, :, c]
            for half, left_m, right_m in ((0, message, in_s), (1, state_low, st_s)):
                grad = mm(left_m, right_m[0], NTR) + mm(left_m, right_m[1], NTR)
                sums = (mm(ones, right_m[0], NTR) + mm(ones, right_m[1], NTR))[:1]
                for q in range(3):
                    r = R_GRU + (half * 3 + q) * H
                    pack[r : r + H, :] += grad[:, q * H : (q + 1) * H]
                    m = R_MISC + M_INPUT + half * 3 + q
                    pack[m : m + 1, :] += sums[:, q * H : (q + 1) * H]
            return carry

        lax.fori_loop(0, chunks, back, 0)
        for k in range(parts):
            gm_rel[k * own_rows : (k + 1) * own_rows, :atoms] = gm[place(k), :]
        if layer > 0:
            b_pull = jnp.concatenate(split(jnp.transpose(ebias)), axis=1)
            for copy in late:
                copy.wait()

            def turn(i, carry):
                for k in range(len(nat_h)):
                    at = pl.multiple_of(turned_width + k * own_rows * H + i * H, H)
                    w_back[:, pl.ds(at, H)] = jnp.transpose(w_nat[k, :, columns(i * H, H)])
                return carry

            lax.fori_loop(0, own_rows, turn, 0)

            def take(b, layer=layer):
                c = columns(b * LB, LB)
                g_o[layer, :, c] = mm(gm_rel[:, window(b)], hot_dst[:, c]).astype(bf16)

            def pull(b, carry, layer=layer):
                c = columns(b * LB, LB)
                hid = hid_i[:, c]
                grad = g_o[layer, :, c]
                for i in range(H):
                    z[i * EH : (i + 1) * EH, :] = g_o[layer, pl.ds(i, 1), c] * hid
                moved_s[:, c] = mm(w_back[...], z[...]) + mm(
                    b_pull, jnp.concatenate([grad, grad], axis=0)
                )
                return carry

            in_pairs(take)
            lax.fori_loop(0, blocks, pull, 0)
            deliver(dst_acc, hot_src)
        else:

            def take(b, layer=layer):
                c = columns(b * LB, LB)
                g_o[layer, :, c] = mm(gm_rel[:, window(b)], hot_dst[:, c]).astype(bf16)

            in_pairs(take)
    acc_b = acc.at[:, :H]
    acc_b[...] = jnp.zeros((H, H), f32)

    def bias_sum(b, carry):
        c = columns(b * LB, LB)
        acc_b[...] += mm(g_o[0, :, c], src_o[0, :, c], NTR) + mm(
            g_o[1, :, c], src_o[1, :, c], NTR
        )
        return carry

    lax.fori_loop(0, blocks, bias_sum, 0)
    for k in range(parts):
        row = pl.multiple_of(R_EBIAS + places[k], 8)
        pack[pl.ds(row, own_rows), :] = acc_b[k * own_rows : (k + 1) * own_rows, :]
    pack[R_END:R_PACK, :] = jnp.zeros((R_PACK - R_END, 128), f32)


def body_edges(jobs, slots, extra_in, last, meta, *refs):
    n = len(jobs)
    ws, (src, g, hid), refs = refs[:n], refs[n : n + 3], refs[n + 3 :]
    if extra_in == "pack":
        (place, pack), refs = refs[:2], refs[2:]
    else:
        hid_before, refs = refs[0], refs[1:]
    if last:
        (before, feat, sums), refs = refs[:3], refs[3:]
    count = 1 + max(slot for slot, _ in slots)
    outs, result, refs = refs[:count], refs[count], refs[count + 1 :]
    built, acc = refs[:2]
    grad_hid = refs[2] if last else result
    blocks = meta[0]
    rows = ws[0].shape[1] // H
    span = rows * EH

    if extra_in == "pack":
        half = pack.shape[0] // 2
        sent = pack[pl.ds(pl.multiple_of(place[0] * half, half), half), :]
        high, low = split(sent)
        outs[0][span : span + half, :] = high
        outs[0][span + half : span + 2 * half, :] = low

    acc[...] = jnp.zeros_like(acc)

    def edges(b, carry):
        c = columns(b * LB, LB)
        s0, s1 = src[0, :, c].astype(f32), src[1, :, c].astype(f32)
        pulled = None if extra_in == "pack" else hid_before[:, c]
        for q, (rel, chunk) in enumerate(jobs):
            at = (rel * CHUNKS + chunk) * rows
            g0 = g[0, at : at + rows, c].astype(f32)
            g1 = g[1, at : at + rows, c].astype(f32)
            for i in range(rows):
                built[q % 2, i * H : (i + 1) * H, :] = (
                    g0[i : i + 1] * s0 + g1[i : i + 1] * s1
                ).astype(bf16)
            part = mm(ws[q][...], built[q % 2])
            pulled = part if pulled is None else pulled + part
            acc[q] += mm(hid[:, c], built[q % 2], NTR)
        grad_hid[:, c] = pulled
        return carry

    lax.fori_loop(0, blocks, edges, 0)
    for q, (slot, at) in enumerate(slots):
        for i in range(rows):
            r = at + i * EH
            outs[slot][r : r + EH, :] = acc[q, :, i * H : (i + 1) * H].astype(bf16)

    if last:
        result[...] = sums[...]

        def finish(b, carry):
            c = columns(b * LB, LB)
            ahead = before[:, c]
            sig = sigmoid(ahead)
            grad = split(grad_hid[:, c] * sig * (1.0 + ahead * (1.0 - sig)))
            rows_low = feat[:, c].astype(bf16)
            result[...] += mm(rows_low, grad[0], NTR) + mm(rows_low, grad[1], NTR)
            return carry

        lax.fori_loop(0, blocks, finish, 0)
        high, low = split(result[...])
        rest = result[...] - high.astype(f32) - low.astype(f32)
        outs[0][span : span + 32, :] = jnp.concatenate(
            [high.astype(f32), low.astype(f32), rest, jnp.zeros_like(rest)], axis=0
        ).astype(bf16)


def adamw(weight, grad, moment, second):
    moment_new = beta_one * moment + (1.0 - beta_one) * grad
    second_new = beta_two * second + (1.0 - beta_two) * grad * grad
    mean_hat = moment_new * (1.0 / (1.0 - beta_one**STEP_COUNT))
    square_hat = second_new * (1.0 / (1.0 - beta_two**STEP_COUNT))
    return (
        weight - rate * (mean_hat / (jnp.sqrt(square_hat) + epsilon) + decay * weight),
        moment_new,
        second_new,
    )


BIG = (1, 3, 4, 5)
WIDE = 1024


def body_adamw(own_rows, place, *refs):
    owns_h, refs = refs[:CHUNKS], refs[CHUNKS:]
    (pack_h, grad_in, squares), refs = refs[:3], refs[3:]
    states, outs, refs = refs[:24], refs[24:48], refs[48:]
    (loss, count, norm), refs = refs[:3], refs[3:]
    owns, pack, bufs, made, in_sem, out_sem = refs[0:CHUNKS], refs[2], refs[3:15], refs[15:27], refs[27], refs[28]
    columns_out = states[1].shape[1]
    waits, ins, going = {}, 0, []

    def fetch(key, source, target):
        nonlocal ins
        copy = pltpu.make_async_copy(source, target, in_sem.at[ins])
        copy.start()
        waits.setdefault(key, []).append(copy)
        ins += 1

    def buffer_of(group, kind, index):
        return group[kind * 4 + BIG.index(index)]

    fetch("pack", pack_h, pack)
    spans = [pl.ds(at, WIDE) for at in range(0, columns_out, WIDE)]
    per = len(spans) // CHUNKS
    for c in range(CHUNKS):
        fetch(("own", c), owns_h[c], owns[c])
        for k in range(c * per, (c + 1) * per):
            for kind in range(3):
                fetch(
                    (1, k),
                    states[kind * 8 + 1].at[:, spans[k]],
                    buffer_of(bufs, kind, 1).at[:, spans[k]],
                )
    for index in BIG[1:]:
        for kind in range(3):
            fetch((index, 0), states[kind * 8 + index], buffer_of(bufs, kind, index))

    def arrive(key):
        for copy in waits[key]:
            copy.wait()

    def send(source, target):
        copy = pltpu.make_async_copy(source, target, out_sem.at[len(going)])
        copy.start()
        going.append(copy)

    def step(index, grad, at=...):
        big = index in BIG
        now = [buffer_of(bufs, k, index) if big else states[k * 8 + index] for k in range(3)]
        new = adamw(now[0][at], grad, now[1][at], now[2][at])
        for kind in range(3):
            target = buffer_of(made, kind, index) if big else outs[kind * 8 + index]
            target[at] = new[kind]

    arrive("pack")
    total = squares[0:1, 0:1] + total_of(jnp.square(grad_in[: G_BIAS + 1, :]))
    for k in range(4):
        total = total + total_of(jnp.square(pack[R_LSTM + k * 2 * H : R_LSTM + k * 2 * H + H, :]))
    loss[...] = grad_in[G_SUMS : G_SUMS + 1, 0:1]
    number = grad_in[G_SUMS : G_SUMS + 1, 1:2]
    count[...] = number
    grad_norm = jnp.sqrt(total) / number
    norm[...] = grad_norm
    factor = jnp.minimum(1.0, clip_norm / grad_norm) / number
    rows = WIDE // H
    for k, span in enumerate(spans):
        c = k // per
        if k % per == 0:
            arrive(("own", c))
        arrive((1, k))
        for i in range(rows):
            at, r = k * WIDE + i * H, ((k % per) * rows + i) * EH
            step(1, owns[c][r : r + EH, :] * factor, (slice(None), slice(at, at + H)))
        for kind in range(3):
            send(buffer_of(made, kind, 1).at[:, span], outs[kind * 8 + 1].at[:, span])

    def finish(index):
        for kind in range(3):
            send(buffer_of(made, kind, index), outs[kind * 8 + index])

    arrive((3, 0))
    for half in range(2):
        for q in range(3):
            r = R_GRU + (half * 3 + q) * H
            step(3, pack[r : r + H, :] * factor, (half, slice(None), slice(q * H, (q + 1) * H)))
    finish(3)
    arrive((4, 0))
    for k in range(4):
        r = R_LSTM + k * 2 * H
        for block, start in ((0, 0), (1, H), (2, 0)):
            step(
                4,
                pack[r + start : r + start + H, :] * factor,
                (slice(block * H, (block + 1) * H), slice(k * H, (k + 1) * H)),
            )
    finish(4)
    arrive((5, 0))
    step(5, pack[R_FIRST:R_GRU, :] * factor)
    finish(5)
    step(0, grad_in[:EIN, :] * factor)
    step(2, pack[pl.ds(pl.multiple_of(R_EBIAS + place[0], 8), own_rows), :] * factor)
    step(6, pack[R_SECOND : R_SECOND + NT, :] * factor)
    bias = jnp.concatenate([grad_in[G_BIAS : G_BIAS + 1, :], pack[R_MISC + 1 : R_EBIAS, :]], axis=0)
    step(7, bias * factor)
    for copy in going:
        copy.wait()


VM = pl.BlockSpec(memory_space=pltpu.VMEM)
SM = pl.BlockSpec(memory_space=pltpu.SMEM)
HBM = pl.BlockSpec(memory_space=pl.ANY)


def per_device(
    node_feats,
    edge_feats,
    edge_ends,
    atom_counts,
    dataset_flags,
    targets,
    present,
    edge_in,
    edge_out,
    edge_bias,
    gru_weights,
    lstm_weights,
    head_first,
    head_second,
    biases,
    *moments_seconds,
):
    row = lax.axis_index("row")
    row_count = lax.axis_size("row")
    mol = lax.axis_index("mol")
    mol_bits = lax.axis_size("mol").bit_length() - 1
    row_bits = row_count.bit_length() - 1
    mols = node_feats.shape[0]
    own_rows = edge_out.shape[1] // H
    atoms = -(-mols * ATOMS // LB) * LB
    space = -(-mols * LIVE // (2 * LB)) * 2 * LB

    def row_swap(x, k):
        return lax.ppermute(x, "row", [(i, i ^ k) for i in range(row_count)])

    def mol_swap(x, bit):
        return lax.ppermute(x, "mol", [(i, i ^ (1 << bit)) for i in range(2**mol_bits)])

    def double(x, swap, bit):
        other = swap(x)
        return jnp.concatenate(
            [jnp.where(bit == 0, x, other), jnp.where(bit == 0, other, x)], axis=0
        )

    sds = jax.ShapeDtypeStruct
    n = row_count
    al = atoms + WINDOW - 128
    params = pltpu.CompilerParams(vmem_limit_bytes=56 * MIB)

    sent = edge_out.astype(bf16)
    bias_sent = edge_bias.reshape(own_rows, H)

    def forward_order(part):
        part = part.reshape(EH, own_rows, H)
        return part.transpose(1, 0, 2).reshape(own_rows, EH * H)

    parts, bias_parts = {0: sent}, {0: bias_sent}
    for bit in reversed(range(row_bits)):
        parts[1 << bit] = row_swap(sent, 1 << bit)
        bias_parts[1 << bit] = row_swap(bias_sent, 1 << bit)

    ends = lax.dynamic_slice_in_dim(edge_ends, row * mols, mols, 1)
    feats = lax.dynamic_slice_in_dim(edge_feats, row * mols * EM, mols * EM, 1)
    table = jnp.concatenate([feats.reshape(EIN, mols, EM), ends.astype(bf16)], axis=0)
    table = table.transpose(1, 0, 2).reshape(mols, (EIN + 2) * EM)
    places = jnp.stack([(row ^ k) * own_rows for k in range(row_count)]).astype(jnp.int32)
    bias_rows = jnp.pad(biases, (0, 16 * 128 - biases.shape[0])).reshape(16, 128)

    at_hand = [parts[k] for k in range(n // 2)]

    def prepare(*refs):
        body_prepare(mols, *refs[:5], refs[5 : 5 + n // 2], *refs[5 + n // 2 :])

    prepared = pl.pallas_call(
        prepare,
        out_shape=(
            sds((2 + space // LB,), jnp.int32),
            sds((H, atoms), bf16),
            sds((EH, space), bf16),
            sds((EH, space), f32),
            sds((8, space), f32),
            sds((WINDOW, space), bf16),
            sds((WINDOW, space), bf16),
            sds((H, n // 2 * own_rows * H), bf16),
        ),
        in_specs=[SM] + [VM] * (4 + n // 2),
        out_specs=(SM,) + (VM,) * 7,
        scratch_shapes=[pltpu.VMEM((128, 128), f32), pltpu.VMEM((mols * PAD, H), f32)],
        compiler_params=params,
    )(atom_counts, table, node_feats, edge_in, bias_rows, *at_hand)
    forward = {k: forward_order(part) for k, part in parts.items() if k < n // 2}
    parts, bias_parts, prepared, forward = lax.optimization_barrier(
        (parts, bias_parts, prepared, forward)
    )
    meta, nodes, hid, before, feat, hot_src, hot_dst, turned = prepared
    for bit in reversed(range(row_bits)):
        for k in [k for k in parts if k > 1 << bit and not k & (1 << bit)]:
            parts[k + (1 << bit)] = row_swap(parts[k], 1 << bit)
            bias_parts[k + (1 << bit)] = row_swap(bias_parts[k], 1 << bit)
    parts = [parts[k] for k in range(n)]
    bias_parts = [bias_parts[k] for k in range(n)]
    w_fwd = [forward[k] if k in forward else forward_order(parts[k]) for k in range(n)]

    away = n - n // 2

    def main(*refs):
        at = 10
        body_main(
            mols,
            own_rows,
            *refs[:at],
            refs[at : at + n],
            refs[at + n],
            refs[at + n + 1 : at + n + 1 + away],
            refs[at + n + 1 + away : at + 2 * n + 1 + away],
            *refs[at + 2 * n + 1 + away :],
        )

    pack, sums, src, g = pl.pallas_call(
        main,
        out_shape=(
            sds((R_PACK, 128), f32),
            sds((8, 128), f32),
            sds((LAYERS, H, space), bf16),
            sds((LAYERS, H, space), bf16),
        ),
        in_specs=[SM] * 4 + [VM] * (6 + n) + [HBM] * (1 + away) + [VM] * (n + 5),
        out_specs=(VM,) * 4,
        scratch_shapes=[
            pltpu.VMEM((H * EH, LB), bf16),
            pltpu.VMEM((LAYERS + 1, H, atoms), f32),
            pltpu.VMEM((LAYERS, H, al), bf16),
            pltpu.VMEM((LAYERS, H, atoms), bf16),
            pltpu.VMEM((LAYERS, 4, H, atoms), f32),
            pltpu.VMEM((H, al), f32),
            pltpu.VMEM((H, al), f32),
            pltpu.VMEM((H, atoms), bf16),
            pltpu.VMEM((H, al), bf16),
            pltpu.VMEM((H, H * EH), bf16),
            pltpu.VMEM((STEPS * mols, atoms), f32),
            pltpu.VMEM((STEPS * mols, atoms), f32),
            pltpu.VMEM((2, H, 3 * H), bf16),
            pltpu.VMEM((2, 3 * H, H), bf16),
            pltpu.VMEM((128, 128), f32),
            pltpu.VMEM((H, space), f32),
            pltpu.VMEM((n - n // 2, EH, own_rows * H), bf16),
            pltpu.SemaphoreType.DMA((1 + n - n // 2,)),
        ],
        compiler_params=pltpu.CompilerParams(vmem_limit_bytes=60 * MIB),
    )(
        atom_counts,
        dataset_flags,
        places,
        meta,
        targets.T,
        present.T,
        nodes,
        hid,
        hot_src,
        hot_dst,
        *w_fwd,
        turned,
        *parts[n // 2 :],
        *bias_parts,
        gru_weights,
        bias_rows,
        lstm_weights,
        head_first,
        head_second.T,
    )

    span = own_rows * H // CHUNKS

    def edge_parts(jobs, slots, heights, extra, last):
        kind = "pack" if len(extra) == 2 else "sum"
        if last:
            extra = extra + (before, feat, sums)
        *found, result = pl.pallas_call(
            functools.partial(body_edges, jobs, slots, kind, last),
            grid=(1,),
            out_shape=tuple(sds((height, EH), bf16) for height in heights)
            + (sds((8, EH) if last else (EH, space), f32),),
            in_specs=[SM]
            + [pl.BlockSpec((EH, span), lambda i, c=chunk: (0, c)) for _, chunk in jobs]
            + [VM] * 3
            + ([SM, VM] if kind == "pack" else [VM] * len(extra)),
            out_specs=(VM,) * (len(heights) + 1),
            scratch_shapes=[
                pltpu.VMEM((2, span, LB), bf16),
                pltpu.VMEM((len(jobs), EH, span), f32),
            ]
            + ([pltpu.VMEM((EH, space), f32)] if last else []),
            compiler_params=params,
        )(meta, *(parts[k] for k, _ in jobs), src, g, hid, *extra)
        return found, result

    row_steps = [(functools.partial(row_swap, k=1 << b), (row >> b) & 1) for b in range(row_bits)]
    mol_steps = [(functools.partial(mol_swap, bit=b), (mol >> b) & 1) for b in range(mol_bits)]
    tie = lax.optimization_barrier
    (core, core_bit), (cross, cross_bit) = row_steps

    def halves(x, bit):
        both = x.reshape((2, x.shape[0] // 2) + x.shape[1:])
        return (
            lax.dynamic_index_in_dim(both, 1 - bit, 0, False),
            lax.dynamic_index_in_dim(both, bit, 0, False),
        )

    def as_low(x, count):
        found = []
        for _ in range(count):
            high = lax.reduce_precision(x, 8, 7)
            found.append(high)
            x = x - high
        return jnp.concatenate(found, axis=0).astype(bf16)

    def from_low(x, count):
        x = x.astype(f32).reshape(count, -1, 128)
        found = x[count - 1]
        for k in reversed(range(count - 1)):
            found = found + x[k]
        return found

    def chain(own, pack, beside):
        for swap, bit in mol_steps:
            own_sent, own = halves(own, bit)
            half = own.shape[0]
            sent = [own_sent.astype(bf16)]
            if pack is not None:
                pack_sent, pack = halves(pack, bit)
                sent.append(as_low(pack_sent, 2))
            if beside is not None:
                sent.append(as_low(beside["rows"], 3))
            came = yield swap, jnp.concatenate(sent, axis=0) if len(sent) > 1 else sent[0]
            own = own + came[:half].astype(f32)
            if pack is not None:
                pack = pack + from_low(came[half : half + 2 * pack.shape[0]], 2)
            if beside is not None:
                beside["rows"] = beside["rows"] + from_low(came[half:], 3)
        piece = own if pack is None else jnp.concatenate([own, pack], axis=0)
        height, rest = piece.shape[0], own.shape[0]
        largest = jnp.maximum(jnp.max(jnp.abs(piece)), 1e-30)
        power = 14.0 - jnp.ceil(jnp.log2(largest))
        sent = jnp.concatenate(
            [piece * jnp.exp2(power), jnp.broadcast_to(power, (16, 128))], axis=0
        ).astype(jnp.float16)
        for swap, bit in reversed(mol_steps):
            came = yield swap, sent
            sent = jnp.concatenate(
                [jnp.where(bit == 0, sent, came), jnp.where(bit == 0, came, sent)], axis=0
            )
        raw, sent = sent, sent.astype(f32).reshape(-1, height + 16, 128)
        back = jnp.exp2(-sent[:, height : height + 1, 0:1])
        own = (sent[:, :rest] * back).reshape(-1, 128)
        square = jnp.sum(own * own)
        if pack is not None:
            pack = raw.reshape(-1, height + 16, 128)[:, rest:].reshape(-1, 128)
            square = square + jnp.sum(jnp.square(sent[:, rest:height] * back))
        return own, pack, square

    core_place = (1 - core_bit).reshape(1).astype(jnp.int32)
    half = pack.shape[0] // 2
    (message, far), carry = edge_parts(
        ((2, 0), (3, 0)),
        ((1, 0), (0, 0)),
        (span + 2 * half, span),
        (core_place, pack),
        False,
    )
    came = core(message)
    pack = halves(pack, core_bit)[1]
    pack_sent, pack = halves(pack + from_low(came[span:], 2), cross_bit)
    sent = (far.astype(f32) + came[:span].astype(f32)).astype(bf16)
    sent = jnp.concatenate([sent, as_low(pack_sent, 2)], axis=0)
    sent, carry = tie((sent, carry))
    arrived = cross(sent)
    (message, near, far), carry = edge_parts(
        ((0, 0), (1, 0), (2, 1), (3, 1)),
        ((1, 0), (0, 0), (2, 0), (0, span)),
        (2 * span, span, span),
        (carry,),
        False,
    )
    message, arrived = tie((message, arrived))
    came = core(message)
    own = near.astype(f32) + came[:span].astype(f32) + arrived[:span].astype(f32)
    pack = pack + from_low(arrived[span:], 2)
    sent = (far.astype(f32) + came[span:].astype(f32)).astype(bf16)

    first = chain(own, pack, None)
    first_swap, first_sent = next(first)
    sent, first_sent, carry = tie((sent, first_sent, carry))
    arrived = cross(sent)
    first_came = first_swap(first_sent)
    (message, near), grad_in = edge_parts(
        ((0, 1), (1, 1)), ((1, 0), (0, 0)), (span + 32, span), (carry,), True
    )
    message, arrived, first_came = tie((message, arrived, first_came))
    came = core(message)
    beside = {"rows": grad_in + from_low(came[span : span + 24], 3)}
    own = near.astype(f32) + came[:span].astype(f32) + arrived.astype(f32)

    second = chain(own, None, beside)
    second_swap, second_sent = next(second)
    first_swap, first_sent = first.send(first_came)
    while True:
        first_sent, second_sent = tie((first_sent, second_sent))
        first_came, second_came = first_swap(first_sent), second_swap(second_sent)
        second_swap, second_sent = second.send(second_came)
        try:
            first_swap, first_sent = first.send(first_came)
        except StopIteration as end:
            first_own, pack, square = end.value
            break
    second_came, came = second_swap(second_sent), cross(pack)
    grad_in = beside["rows"] + cross(beside["rows"])
    pack = jnp.concatenate(
        [jnp.where(cross_bit == 0, pack, came), jnp.where(cross_bit == 0, came, pack)], axis=0
    )
    came = core(pack)
    pack = jnp.concatenate(
        [jnp.where(core_bit == 0, pack, came), jnp.where(core_bit == 0, came, pack)], axis=0
    )
    pack = pack.astype(f32).reshape(n * 2**mol_bits, -1, 128)
    pack = (pack[:, :-16] * jnp.exp2(-pack[:, -16:-15, 0:1])).reshape(-1, 128)
    try:
        second.send(second_came)
    except StopIteration as end:
        second_own, _, more = end.value
    squares = jnp.broadcast_to(square + more, (8, 128))
    came = row_swap(squares, 3)
    came, pack, grad_in = tie((came, pack, grad_in))
    squares = (squares + row_swap(squares, 1)) + (row_swap(squares, 2) + came)
    owns = [first_own, second_own]

    weights = [
        edge_in,
        edge_out,
        edge_bias,
        gru_weights,
        lstm_weights,
        head_first,
        head_second,
        biases,
    ]
    states = []
    for group in (weights, moments_seconds[:8], moments_seconds[8:]):
        group = list(group)
        group[2] = group[2].reshape(own_rows, H)
        group[6] = group[6].T
        if group[7] is biases:
            group[7] = bias_rows
        else:
            group[7] = jnp.pad(group[7], (0, 16 * 128 - group[7].shape[0])).reshape(16, 128)
        states += group
    spots = [HBM if index in BIG else VM for index in range(8)] * 3
    copies = 3 * (own_rows * H // WIDE + len(BIG) - 1)
    shapes = [sds(state.shape, f32) for state in states]
    results = pl.pallas_call(
        functools.partial(body_adamw, own_rows),
        out_shape=tuple(shapes) + (sds((1, 1), f32),) * 3,
        in_specs=[SM] + [HBM] * (CHUNKS + 1) + [VM] * 2 + spots,
        out_specs=tuple(spots) + (VM,) * 3,
        scratch_shapes=[pltpu.VMEM(own.shape, f32) for own in owns]
        + [pltpu.VMEM(pack.shape, f32)]
        + [pltpu.VMEM(shapes[index].shape, f32) for _ in range(6) for index in BIG]
        + [pltpu.SemaphoreType.DMA((copies + CHUNKS + 1,)), pltpu.SemaphoreType.DMA((copies,))],
        compiler_params=params,
    )(places, *owns, pack, grad_in, squares, *states)
    results = list(results)
    for kind in range(3):
        results[kind * 8 + 2] = results[kind * 8 + 2].reshape(own_rows * H)
        results[kind * 8 + 6] = results[kind * 8 + 6].T
        results[kind * 8 + 7] = results[kind * 8 + 7].reshape(-1)[: biases.shape[0]]
    for index in range(24, 27):
        results[index] = results[index].reshape(())
    return tuple(results)


def solution(mesh):
    weights = (P(), P(None, "row"), P("row"), P(), P(), P(), P(), P())
    in_specs = (
        P(("mol", "row"), None, None),
        P(None, "mol"),
        P(None, "mol", None),
        P(("mol", "row")),
        P(("mol", "row")),
        P(("mol", "row"), None),
        P(("mol", "row"), None),
    ) + weights * 3
    out_specs = weights * 3 + (P(), P(), P())
    return jax.shard_map(
        per_device, mesh=mesh, in_specs=in_specs, out_specs=out_specs, check_vma=False
    )
```

```python
import functools
import math

import jax
import jax.numpy as jnp
from jax import lax
from jax.experimental import pallas as pl
from jax.experimental.pallas import tpu as pltpu
from jax.sharding import PartitionSpec as P

H = 128
EH = 128
EIN = 5
NT = 12
STEPS = 6
ATOMS = 29
EM = 64
LAYERS = 2
STEP_COUNT = 10

PAD = 32
LIVE = 2 * (ATOMS - 1)
LB = 256
MIB = 2**20

f32 = jnp.float32
bf16 = jnp.bfloat16
highest = lax.Precision.HIGHEST
beta_one = 0.9
beta_two = 0.999
rate = 0.05
epsilon = 1e-08
decay = 0.01
clip_norm = 0.1

R_LSTM, R_FIRST, R_GRU, R_SECOND, R_MISC, R_EBIAS, R_END = 0, 1024, 1280, 2048, 2064, 2080, 2208
R_PACK = 2560
M_INPUT, M_LSTM, M_HEAD, M_OUT = 1, 7, 11, 12
G_BIAS, G_SUMS = EIN, EIN + 1
WINDOW = 384
CHUNKS = 2

NN = ((1,), (0,))
NTR = ((1,), (1,))
TN = ((0,), (0,))


def mm(a, b, dims=NN):
    return lax.dot_general(a, b, (dims, ((), ())), preferred_element_type=f32)


def split(x):
    high = x.astype(bf16)
    return high, (x - high.astype(f32)).astype(bf16)


def mm3(a, b, dims=NN):
    if dims[0] == (1,) and a[0].shape[0] in (16, 32, 64):
        rows = a[0].shape[0]
        both = mm(jnp.concatenate(a, axis=0), b[0], dims)
        return both[:rows] + (both[rows:] + mm(a[0], b[1], dims))
    return mm(a[0], b[0], dims) + (mm(a[0], b[1], dims) + mm(a[1], b[0], dims))


def mm_stack(a, b):
    high, low = split(a)
    rows = a.shape[0]
    left = jnp.concatenate(
        [
            jnp.concatenate([high, high], axis=1),
            jnp.concatenate([low, jnp.zeros_like(low)], axis=1),
        ],
        axis=0,
    )
    both = mm(left, b)
    return both[:rows] + both[rows:]


def mm_stack_t(a, b):
    rows, width = a.shape[0], b.shape[0] // 2
    both = mm(jnp.concatenate(split(a), axis=0), b, NTR)
    return both[:rows, :width] + (both[rows:, :width] + both[:rows, width:])


def mm2(a, b, dims=NN):
    high, low = split(a)
    return mm(high, b, dims) + mm(low, b, dims)


def total_of(x):
    return jnp.sum(jnp.sum(x, axis=1, keepdims=True), axis=0, keepdims=True)


def columns(start, size):
    return pl.ds(pl.multiple_of(start, size), size)


def sigmoid(v):
    return jax.nn.sigmoid(v)


def column_of(values, size):
    at = lax.broadcasted_iota(jnp.int32, (size, 1), 0)
    found = jnp.zeros((size, 1), jnp.int32)
    for m in range(size):
        found = jnp.where(at == m, values[m], found)
    return found


def row_of(values, size):
    at = lax.broadcasted_iota(jnp.int32, (1, size), 1)
    found = jnp.zeros((1, size), jnp.int32)
    for m in range(size):
        found = jnp.where(at == m, values[m], found)
    return found


def starts_of(column, size):
    below = (
        lax.broadcasted_iota(jnp.int32, (size, size), 1)
        < lax.broadcasted_iota(jnp.int32, (size, size), 0)
    ).astype(bf16)
    return mm(below, jnp.broadcast_to(column, (size, 128)).astype(bf16))[:, :1]


def body_prepare(
    mols,
    counts_s,
    table,
    node_feats,
    edge_in,
    bias_rows,
    nat,
    meta,
    nodes_o,
    hid_o,
    before_o,
    feat_o,
    hot_src,
    hot_dst,
    turned_o,
    square,
    flat,
):
    lanes = nodes_o.shape[1]
    space = hid_o.shape[1]
    for b in range(space // LB):
        meta[2 + b] = jnp.int32(0)
    edges, atoms = jnp.int32(0), jnp.int32(0)
    for m in range(mols):
        live = 2 * (counts_s[m] - 1)
        block = lax.div(edges + (LB - 1), jnp.int32(LB))

        @pl.when(block * LB < edges + live)
        def _(block=block, atoms=atoms):
            meta[2 + block] = lax.div(atoms, jnp.int32(128)) * 128

        edges = edges + live
        atoms = atoms + counts_s[m]
    blocks = lax.div(edges + (LB - 1), jnp.int32(LB))
    meta[0] = blocks
    meta[1] = lax.div(atoms + (LB - 1), jnp.int32(LB))

    count_col = column_of(counts_s, mols).astype(f32)
    live_col = 2.0 * (count_col - 1.0)
    start_col = starts_of(live_col, mols)
    atom_col = starts_of(count_col, mols)

    width = nat[0].shape[1]

    def turn(i, carry):
        for k, part in enumerate(nat):
            turned_o[:, pl.ds(pl.multiple_of(k * width + i * H, H), H)] = jnp.transpose(
                part[:, columns(i * H, H)]
            )
        return carry

    lax.fori_loop(0, width // H, turn, 0)

    square[...] = jnp.zeros_like(square)
    square[0:EIN, :] = edge_in[...]
    square[8:24, :] = bias_rows[...]
    turned = jnp.transpose(square[...])
    in_t, b_in_col = turned[:, :8], turned[:, 8:9]
    e_high, e_low = split(in_t)
    e_rest = (in_t - e_high.astype(f32) - e_low.astype(f32)).astype(bf16)

    flat[...] = jnp.zeros_like(flat)
    for m in range(mols):
        flat[m * PAD : m * PAD + ATOMS, :] = node_feats[m].astype(f32)
    flat_low = flat[...].astype(bf16)
    nodes_o[...] = jnp.zeros_like(nodes_o)
    atom_at = lax.broadcasted_iota(jnp.int32, (mols * PAD, 1), 0)
    spread = (
        lax.broadcasted_iota(jnp.int32, (mols * PAD, mols), 0) // PAD
        == lax.broadcasted_iota(jnp.int32, (mols * PAD, mols), 1)
    ).astype(bf16)
    goal_high = jnp.floor(atom_col * (1.0 / 8.0))
    goal_parts = jnp.concatenate([goal_high, atom_col - 8.0 * goal_high, count_col], axis=1)
    goal = mm(
        spread,
        jnp.concatenate([goal_parts, jnp.zeros((mols, 125), f32)], axis=1).astype(bf16),
    )
    within = lax.rem(atom_at, jnp.int32(PAD)).astype(f32)
    target = jnp.where(
        within < goal[:, 2:3], 8.0 * goal[:, 0:1] + goal[:, 1:2] + within, -1.0
    ).astype(jnp.int32)

    def pack_atoms(k, carry):
        c = columns(k * LB, LB)
        at = lax.broadcasted_iota(jnp.int32, (mols * PAD, LB), 1) + k * LB
        hot = (at == target).astype(f32).astype(bf16)
        nodes_o[:, c] = mm(flat_low, hot, TN).astype(bf16)
        return carry

    lax.fori_loop(0, meta[1], pack_atoms, 0)

    def prepare(b, carry):
        c = columns(b * LB, LB)
        spot = (lax.broadcasted_iota(jnp.int32, (mols, LB), 1) + b * LB).astype(f32)
        mol_hot = ((spot >= start_col) & (spot < start_col + live_col)).astype(f32)
        rows = mm(table[...], mol_hot.astype(bf16), TN)
        start_row = jnp.sum(mol_hot * start_col, axis=0, keepdims=True)
        base = jnp.sum(mol_hot * atom_col, axis=0, keepdims=True)
        valid = jnp.sum(mol_hot, axis=0, keepdims=True)
        slot = spot[:1] - start_row
        slot_hot = (lax.broadcasted_iota(jnp.int32, (EM, LB), 0).astype(f32) == slot).astype(f32)
        picked = [
            jnp.sum(rows[r * EM : (r + 1) * EM] * slot_hot, axis=0, keepdims=True)
            for r in range(EIN + 2)
        ]
        feat = jnp.concatenate(picked[:EIN] + [valid, jnp.zeros((2, LB), f32)], axis=0)
        feat_o[:, c] = feat
        feat_low = feat.astype(bf16)
        before = mm(e_high, feat_low) + mm(e_low, feat_low) + mm(e_rest, feat_low) + b_in_col
        before_o[:, c] = before
        hid_o[:, c] = (before * sigmoid(before)).astype(bf16)
        atom = lax.broadcasted_iota(jnp.int32, (WINDOW, LB), 0)
        base = base - meta[2 + b].astype(f32)
        src = jnp.where(valid > 0.5, base + picked[EIN], -1.0).astype(jnp.int32)
        dst = jnp.where(valid > 0.5, base + picked[EIN + 1], -1.0).astype(jnp.int32)
        hot_src[:, c] = (atom == src).astype(f32).astype(bf16)
        hot_dst[:, c] = (atom == dst).astype(f32).astype(bf16)
        return carry

    lax.fori_loop(0, 2 * lax.div(blocks + 1, jnp.int32(2)), prepare, 0)


def body_main(
    mols,
    own_rows,
    counts_s,
    flags_s,
    places,
    meta,
    targets,
    present,
    nodes,
    hid_i,
    hot_src,
    hot_dst,
    w_fwd,
    turned_h,
    nat_h,
    ebias_parts,
    gru,
    bias_rows,
    lstm_rows,
    first,
    second,
    pack,
    sums_o,
    src_o,
    g_o,
    z,
    st,
    low,
    msg,
    keep,
    acc,
    dst_acc,
    gm,
    gm_rel,
    w_back,
    w_all,
    ds_all,
    gru_n,
    gru_t,
    square,
    moved_s,
    w_nat,
    late_sem,
):
    parts = len(w_fwd)
    blocks, chunks = meta[0], meta[1]
    turned_width = turned_h.shape[1]
    late = [pltpu.make_async_copy(turned_h, w_back.at[:, :turned_width], late_sem.at[0])]
    for k in range(len(nat_h)):
        late.append(pltpu.make_async_copy(nat_h[k], w_nat.at[k], late_sem.at[1 + k]))
    for copy in late:
        copy.start()
    atoms = w_all.shape[1]

    def place(k):
        return pl.ds(pl.multiple_of(places[k], own_rows), own_rows)

    def window(b):
        return pl.ds(pl.multiple_of(meta[2 + b], 128), WINDOW)

    square[...] = jnp.zeros_like(square)
    square[0:16, :] = bias_rows[...]
    turned = jnp.transpose(square[...])
    gbias_col = [
        jnp.concatenate([turned[:, r + q : r + q + 1] for q in range(3)], axis=0)
        for r in (M_INPUT, M_INPUT + 3)
    ]
    c_lstm = jnp.concatenate(
        [bias_rows[M_LSTM + k : M_LSTM + k + 1, :] for k in range(4)], axis=1
    )
    c_head = bias_rows[M_HEAD : M_HEAD + 1, :]
    out_cols = [turned[k * NT : (k + 1) * NT, M_OUT : M_OUT + 1] for k in range(3)]
    gru_n[...] = gru[...].astype(bf16)
    for half in range(2):
        for q in range(3):
            gru_t[half, q * H : (q + 1) * H, :] = jnp.transpose(
                gru_n[half, :, q * H : (q + 1) * H]
            )
    ebias = jnp.concatenate([part[...] for part in ebias_parts], axis=0)
    b_high, b_low = split(ebias)

    def in_pairs(step):
        def both(p, carry):
            step(2 * p)
            step(2 * p + 1)
            return carry

        lax.fori_loop(0, lax.div(blocks + 1, jnp.int32(2)), both, 0)

    def deliver(into, hot):
        def both(p, carry):
            found = []
            for u in range(2):
                c = columns((2 * p + u) * LB, LB)
                found.append(mm2(moved_s[:, c], hot[:, c], NTR))
            for u in range(2):
                into[:, window(2 * p + u)] += found[u]
            return carry

        lax.fori_loop(0, lax.div(blocks + 1, jnp.int32(2)), both, 0)

    b_fwd = jnp.concatenate([b_high, b_low], axis=1)
    moved_s[...] = jnp.zeros_like(moved_s)

    for layer in range(LAYERS):
        low[layer] = jnp.zeros_like(low[layer])
    low[0, :, :atoms] = nodes[...]
    st[0] = nodes[...].astype(f32)
    st[LAYERS] = jnp.zeros_like(st[LAYERS])
    gm_rel[...] = jnp.zeros_like(gm_rel)
    for layer in range(LAYERS):
        acc[...] = jnp.zeros_like(acc)

        def fetch(b, layer=layer):
            c = columns(b * LB, LB)
            src_o[layer, :, c] = mm(low[layer, :, window(b)], hot_src[:, c]).astype(bf16)

        def move(b, carry, layer=layer):
            c = columns(b * LB, LB)
            source = src_o[layer, :, c]
            for h in range(EH):
                z[h * H : (h + 1) * H, :] = hid_i[pl.ds(h, 1), c] * source
            moved_s[:, c] = mm(jnp.concatenate([part[...] for part in w_fwd], axis=0), z[...]) + mm(
                b_fwd, jnp.concatenate([source, source], axis=0)
            )
            return carry

        in_pairs(fetch)
        lax.fori_loop(0, blocks, move, 0)
        deliver(acc, hot_dst)
        for k in range(parts):
            msg[layer, place(k), :] = acc[k * own_rows : (k + 1) * own_rows, :atoms].astype(bf16)

        def update(k, carry, layer=layer):
            c = columns(k * LB, LB)
            from_in = mm(gru_t[0], msg[layer, :, c]) + gbias_col[0]
            from_st = mm(gru_t[1], low[layer, :, c]) + gbias_col[1]
            reset = sigmoid(from_in[:H] + from_st[:H])
            upd = sigmoid(from_in[H : 2 * H] + from_st[H : 2 * H])
            fresh = jnp.tanh(from_in[2 * H :] + reset * from_st[2 * H :])
            new = (1.0 - upd) * fresh + upd * st[layer, :, c]
            st[layer + 1, :, c] = new
            if layer + 1 < LAYERS:
                low[layer + 1, :, c] = new.astype(bf16)
            keep[layer, 0, :, c] = reset
            keep[layer, 1, :, c] = upd
            keep[layer, 2, :, c] = fresh
            keep[layer, 3, :, c] = from_st[2 * H :]
            return carry

        lax.fori_loop(0, chunks, update, 0)

    lane = lax.broadcasted_iota(jnp.int32, (mols, atoms), 1).astype(f32)
    count_col = column_of(counts_s, mols).astype(f32)
    slot_of = lane - starts_of(count_col, mols)
    alive = (slot_of >= 0.0) & (slot_of < count_col)
    x = jnp.concatenate(split(st[LAYERS]), axis=0)
    lstm = jnp.concatenate(
        [lstm_rows[0:H, :] + lstm_rows[2 * H : 3 * H, :], lstm_rows[H : 2 * H, :]], axis=0
    )
    lstm_w = split(lstm)
    zeros = jnp.zeros((mols, H), f32)
    hidden, read, cell = zeros, zeros, zeros
    saved = []
    for step in range(STEPS):
        query = jnp.concatenate([hidden, read], axis=1)
        if step == 0:
            gates = jnp.broadcast_to(c_lstm, (mols, 4 * H))
        else:
            gates = mm3(split(query), lstm_w) + c_lstm
        in_gate = sigmoid(gates[:, :H])
        forget = sigmoid(gates[:, H : 2 * H])
        part = jnp.tanh(gates[:, 2 * H : 3 * H])
        out_gate = sigmoid(gates[:, 3 * H :])
        before_cell = cell
        cell = forget * cell + in_gate * part
        squashed = jnp.tanh(cell)
        hidden = out_gate * squashed
        scores = jnp.where(alive, mm_stack(hidden, x), -1e30)
        weights = jnp.where(alive, jnp.exp(scores - jnp.max(scores, axis=1, keepdims=True)), 0.0)
        weights = weights / jnp.sum(weights, axis=1, keepdims=True)
        w_all[step * mols : (step + 1) * mols, :] = weights
        read = mm_stack_t(weights, x)
        saved.append((query, in_gate, forget, part, out_gate, before_cell, squashed, hidden))
    query = jnp.concatenate([hidden, read], axis=1)
    first_w = split(first[...])
    second_w = split(second[...])
    query_s = split(query)
    inner_pre = mm3(query_s, first_w) + c_head
    inner_sig = sigmoid(inner_pre)
    inner = inner_pre * inner_sig
    inner_s = split(inner)
    is_one = row_of(flags_s, mols) == 1
    predicted = (
        mm3(second_w, inner_s, NTR)
        + out_cols[0]
        + jnp.where(is_one, out_cols[2], out_cols[1])
    )
    there = present[...].astype(f32)
    diff = predicted - targets[...]
    lanes = lax.broadcasted_iota(jnp.int32, (1, 128), 1)
    loss = total_of(there * diff * diff)
    count = total_of(there)
    sums_o[...] = jnp.zeros_like(sums_o)
    sums_o[G_SUMS : G_SUMS + 1, :] = jnp.where(lanes == 0, loss, jnp.where(lanes == 1, count, 0.0))

    d_pred = 2.0 * there * diff
    d_pred_s = split(d_pred)
    pack[R_SECOND:R_MISC, :] = jnp.zeros((R_MISC - R_SECOND, 128), f32)
    pack[R_SECOND : R_SECOND + NT, :] = mm3(d_pred_s, inner_s)
    pack[R_MISC:R_EBIAS, :] = jnp.zeros((R_EBIAS - R_MISC, 128), f32)
    zero_pred = jnp.where(is_one, 0.0, d_pred)
    out_sums = jnp.concatenate([d_pred, zero_pred, d_pred - zero_pred], axis=0)
    out_high, out_low = split(out_sums)
    out_ones = jnp.ones((8, mols), bf16)
    pack[R_MISC + M_OUT : R_MISC + M_OUT + 1, : 3 * NT] = (
        mm(out_ones, out_high, NTR) + mm(out_ones, out_low, NTR)
    )[:1]
    d_inner = mm3(d_pred_s, second_w, TN)
    d_pre = d_inner * inner_sig * (1.0 + inner_pre * (1.0 - inner_sig))
    d_pre_s = split(d_pre)
    pack[R_FIRST:R_GRU, :] = mm3(query_s, d_pre_s, TN)
    pack[R_MISC + M_HEAD : R_MISC + M_HEAD + 1, :] = jnp.sum(d_pre, axis=0, keepdims=True)
    d_query = mm3(d_pre_s, first_w, NTR)
    d_hidden, d_read = d_query[:, :H], d_query[:, H:]
    d_cell = zeros
    d_gates_all = [None] * STEPS
    d_reads = [None] * STEPS
    for step in reversed(range(STEPS)):
        query, in_gate, forget, part, out_gate, before_cell, squashed, hid_t = saved[step]
        weights = w_all[step * mols : (step + 1) * mols, :]
        d_reads[step] = d_read
        d_weights = mm_stack(d_read, x)
        d_scores = weights * (d_weights - jnp.sum(weights * d_weights, axis=1, keepdims=True))
        ds_all[step * mols : (step + 1) * mols, :] = d_scores
        d_hidden = d_hidden + mm_stack_t(d_scores, x)
        d_out = d_hidden * squashed * out_gate * (1.0 - out_gate)
        d_cell = d_cell + d_hidden * out_gate * (1.0 - squashed * squashed)
        d_forget = d_cell * before_cell * forget * (1.0 - forget)
        d_in = d_cell * part * in_gate * (1.0 - in_gate)
        d_part = d_cell * in_gate * (1.0 - part * part)
        d_cell = d_cell * forget
        d_gates = jnp.concatenate([d_in, d_forget, d_part, d_out], axis=1)
        d_gates_all[step] = d_gates
        if step > 0:
            d_query = mm3(split(d_gates), lstm_w, NTR)
            d_hidden, d_read = d_query[:, :H], d_query[:, H:]
    queries = split(jnp.concatenate([saved[s][0] for s in range(STEPS)], axis=0))
    d_gates_cat = jnp.concatenate(d_gates_all, axis=0)
    d_gates_s = split(d_gates_cat)
    grad_lstm = mm3(queries, d_gates_s, TN)
    d_gates_sum = jnp.sum(d_gates_cat, axis=0, keepdims=True)
    for k in range(4):
        pack[R_LSTM + k * 256 : R_LSTM + (k + 1) * 256, :] = grad_lstm[:, k * H : (k + 1) * H]
        pack[R_MISC + M_LSTM + k : R_MISC + M_LSTM + k + 1, :] = d_gates_sum[:, k * H : (k + 1) * H]
    left = jnp.concatenate(d_reads + [saved[s][7] for s in range(STEPS)], axis=0)
    left_s = split(left)

    def spread(k, carry):
        c = columns(k * LB, LB)
        right = split(jnp.concatenate([w_all[:, c], ds_all[:, c]], axis=0))
        dst_acc[:, c] = mm3(left_s, right, TN)
        return carry

    dst_acc[...] = jnp.zeros_like(dst_acc)
    lax.fori_loop(0, chunks, spread, 0)

    pack[R_GRU:R_SECOND, :] = jnp.zeros((6 * H, 128), f32)
    gm[...] = jnp.zeros_like(gm)
    for layer in reversed(range(LAYERS)):

        def back(k, carry, layer=layer):
            c = columns(k * LB, LB)
            d_state = dst_acc[:, c]
            reset, upd = keep[layer, 0, :, c], keep[layer, 1, :, c]
            fresh, from_st = keep[layer, 2, :, c], keep[layer, 3, :, c]
            d_upd = d_state * (st[layer, :, c] - fresh) * upd * (1.0 - upd)
            d_fresh = d_state * (1.0 - upd) * (1.0 - fresh * fresh)
            d_reset = d_fresh * from_st * reset * (1.0 - reset)
            d_from_in = jnp.concatenate([d_reset, d_upd, d_fresh], axis=0)
            d_from_st = jnp.concatenate([d_reset, d_upd, d_fresh * reset], axis=0)
            in_s, st_s = split(d_from_in), split(d_from_st)
            gm[:, c] = (mm(gru_n[0], in_s[0]) + mm(gru_n[0], in_s[1])).astype(bf16)
            if layer > 0:
                dst_acc[:, c] = d_state * upd + (mm(gru_n[1], st_s[0]) + mm(gru_n[1], st_s[1]))
            ones = jnp.ones((8, LB), bf16)
            message, state_low = msg[layer, :, c], low[layer, :, c]
            for half, left_m, right_m in ((0, message, in_s), (1, state_low, st_s)):
                grad = mm(left_m, right_m[0], NTR) + mm(left_m, right_m[1], NTR)
                sums = (mm(ones, right_m[0], NTR) + mm(ones, right_m[1], NTR))[:1]
                for q in range(3):
                    r = R_GRU + (half * 3 + q) * H
                    pack[r : r + H, :] += grad[:, q * H : (q + 1) * H]
                    m = R_MISC + M_INPUT + half * 3 + q
                    pack[m : m + 1, :] += sums[:, q * H : (q + 1) * H]
            return carry

        lax.fori_loop(0, chunks, back, 0)
        for k in range(parts):
            gm_rel[k * own_rows : (k + 1) * own_rows, :atoms] = gm[place(k), :]
        if layer > 0:
            b_pull = jnp.concatenate(split(jnp.transpose(ebias)), axis=1)
            for copy in late:
                copy.wait()

            def turn(i, carry):
                for k in range(len(nat_h)):
                    at = pl.multiple_of(turned_width + k * own_rows * H + i * H, H)
                    w_back[:, pl.ds(at, H)] = jnp.transpose(w_nat[k, :, columns(i * H, H)])
                return carry

            lax.fori_loop(0, own_rows, turn, 0)

            def take(b, layer=layer):
                c = columns(b * LB, LB)
                g_o[layer, :, c] = mm(gm_rel[:, window(b)], hot_dst[:, c]).astype(bf16)

            def pull(b, carry, layer=layer):
                c = columns(b * LB, LB)
                hid = hid_i[:, c]
                grad = g_o[layer, :, c]
                for i in range(H):
                    z[i * EH : (i + 1) * EH, :] = g_o[layer, pl.ds(i, 1), c] * hid
                moved_s[:, c] = mm(w_back[...], z[...]) + mm(
                    b_pull, jnp.concatenate([grad, grad], axis=0)
                )
                return carry

            in_pairs(take)
            lax.fori_loop(0, blocks, pull, 0)
            deliver(dst_acc, hot_src)
        else:

            def take(b, layer=layer):
                c = columns(b * LB, LB)
                g_o[layer, :, c] = mm(gm_rel[:, window(b)], hot_dst[:, c]).astype(bf16)

            in_pairs(take)
    acc_b = acc.at[:, :H]
    acc_b[...] = jnp.zeros((H, H), f32)

    def bias_sum(b, carry):
        c = columns(b * LB, LB)
        acc_b[...] += mm(g_o[0, :, c], src_o[0, :, c], NTR) + mm(
            g_o[1, :, c], src_o[1, :, c], NTR
        )
        return carry

    lax.fori_loop(0, blocks, bias_sum, 0)
    for k in range(parts):
        row = pl.multiple_of(R_EBIAS + places[k], 8)
        pack[pl.ds(row, own_rows), :] = acc_b[k * own_rows : (k + 1) * own_rows, :]
    pack[R_END:R_PACK, :] = jnp.zeros((R_PACK - R_END, 128), f32)


def body_edges(jobs, slots, extra_in, last, meta, *refs):
    n = len(jobs)
    ws, (src, g, hid), refs = refs[:n], refs[n : n + 3], refs[n + 3 :]
    if extra_in == "pack":
        (place, pack), refs = refs[:2], refs[2:]
    else:
        hid_before, refs = refs[0], refs[1:]
    if last:
        (before, feat, sums), refs = refs[:3], refs[3:]
    count = 1 + max(slot for slot, _ in slots)
    outs, result, refs = refs[:count], refs[count], refs[count + 1 :]
    built, acc = refs[:2]
    grad_hid = refs[2] if last else result
    blocks = meta[0]
    rows = ws[0].shape[1] // H
    span = rows * EH

    if extra_in == "pack":
        half = pack.shape[0] // 2
        sent = pack[pl.ds(pl.multiple_of(place[0] * half, half), half), :]
        high, low = split(sent)
        outs[0][span : span + half, :] = high
        outs[0][span + half : span + 2 * half, :] = low

    acc[...] = jnp.zeros_like(acc)

    def edges(b, carry):
        c = columns(b * LB, LB)
        s0, s1 = src[0, :, c].astype(f32), src[1, :, c].astype(f32)
        pulled = None if extra_in == "pack" else hid_before[:, c]
        for q, (rel, chunk) in enumerate(jobs):
            at = (rel * CHUNKS + chunk) * rows
            g0 = g[0, at : at + rows, c].astype(f32)
            g1 = g[1, at : at + rows, c].astype(f32)
            for i in range(rows):
                built[q % 2, i * H : (i + 1) * H, :] = (
                    g0[i : i + 1] * s0 + g1[i : i + 1] * s1
                ).astype(bf16)
            part = mm(ws[q][...], built[q % 2])
            pulled = part if pulled is None else pulled + part
            acc[q] += mm(hid[:, c], built[q % 2], NTR)
        grad_hid[:, c] = pulled
        return carry

    lax.fori_loop(0, blocks, edges, 0)
    for q, (slot, at) in enumerate(slots):
        for i in range(rows):
            r = at + i * EH
            outs[slot][r : r + EH, :] = acc[q, :, i * H : (i + 1) * H].astype(bf16)

    if last:
        result[...] = sums[...]

        def finish(b, carry):
            c = columns(b * LB, LB)
            ahead = before[:, c]
            sig = sigmoid(ahead)
            grad = split(grad_hid[:, c] * sig * (1.0 + ahead * (1.0 - sig)))
            rows_low = feat[:, c].astype(bf16)
            result[...] += mm(rows_low, grad[0], NTR) + mm(rows_low, grad[1], NTR)
            return carry

        lax.fori_loop(0, blocks, finish, 0)
        high, low = split(result[...])
        rest = result[...] - high.astype(f32) - low.astype(f32)
        outs[0][span : span + 32, :] = jnp.concatenate(
            [high.astype(f32), low.astype(f32), rest, jnp.zeros_like(rest)], axis=0
        ).astype(bf16)


def adamw(weight, grad, moment, second):
    moment_new = beta_one * moment + (1.0 - beta_one) * grad
    second_new = beta_two * second + (1.0 - beta_two) * grad * grad
    mean_hat = moment_new * (1.0 / (1.0 - beta_one**STEP_COUNT))
    square_hat = second_new * (1.0 / (1.0 - beta_two**STEP_COUNT))
    return (
        weight - rate * (mean_hat / (jnp.sqrt(square_hat) + epsilon) + decay * weight),
        moment_new,
        second_new,
    )


BIG = (1, 3, 4, 5)
WIDE = 1024


def body_adamw(own_rows, place, *refs):
    owns_h, refs = refs[:CHUNKS], refs[CHUNKS:]
    (pack_h, grad_in, squares), refs = refs[:3], refs[3:]
    states, outs, refs = refs[:24], refs[24:48], refs[48:]
    (loss, count, norm), refs = refs[:3], refs[3:]
    owns, pack, bufs, made, in_sem, out_sem = refs[0:CHUNKS], refs[2], refs[3:15], refs[15:27], refs[27], refs[28]
    columns_out = states[1].shape[1]
    waits, ins, going = {}, 0, []

    def fetch(key, source, target):
        nonlocal ins
        copy = pltpu.make_async_copy(source, target, in_sem.at[ins])
        copy.start()
        waits.setdefault(key, []).append(copy)
        ins += 1

    def buffer_of(group, kind, index):
        return group[kind * 4 + BIG.index(index)]

    fetch("pack", pack_h, pack)
    spans = [pl.ds(at, WIDE) for at in range(0, columns_out, WIDE)]
    per = len(spans) // CHUNKS
    for c in range(CHUNKS):
        fetch(("own", c), owns_h[c], owns[c])
        for k in range(c * per, (c + 1) * per):
            for kind in range(3):
                fetch(
                    (1, k),
                    states[kind * 8 + 1].at[:, spans[k]],
                    buffer_of(bufs, kind, 1).at[:, spans[k]],
                )
    for index in BIG[1:]:
        for kind in range(3):
            fetch((index, 0), states[kind * 8 + index], buffer_of(bufs, kind, index))

    def arrive(key):
        for copy in waits[key]:
            copy.wait()

    def send(source, target):
        copy = pltpu.make_async_copy(source, target, out_sem.at[len(going)])
        copy.start()
        going.append(copy)

    def step(index, grad, at=...):
        big = index in BIG
        now = [buffer_of(bufs, k, index) if big else states[k * 8 + index] for k in range(3)]
        new = adamw(now[0][at], grad, now[1][at], now[2][at])
        for kind in range(3):
            target = buffer_of(made, kind, index) if big else outs[kind * 8 + index]
            target[at] = new[kind]

    arrive("pack")
    total = squares[0:1, 0:1] + total_of(jnp.square(grad_in[: G_BIAS + 1, :]))
    for k in range(4):
        total = total + total_of(jnp.square(pack[R_LSTM + k * 2 * H : R_LSTM + k * 2 * H + H, :]))
    loss[...] = grad_in[G_SUMS : G_SUMS + 1, 0:1]
    number = grad_in[G_SUMS : G_SUMS + 1, 1:2]
    count[...] = number
    grad_norm = jnp.sqrt(total) / number
    norm[...] = grad_norm
    factor = jnp.minimum(1.0, clip_norm / grad_norm) / number
    rows = WIDE // H
    for k, span in enumerate(spans):
        c = k // per
        if k % per == 0:
            arrive(("own", c))
        arrive((1, k))
        for i in range(rows):
            at, r = k * WIDE + i * H, ((k % per) * rows + i) * EH
            step(1, owns[c][r : r + EH, :] * factor, (slice(None), slice(at, at + H)))
        for kind in range(3):
            send(buffer_of(made, kind, 1).at[:, span], outs[kind * 8 + 1].at[:, span])

    def finish(index):
        for kind in range(3):
            send(buffer_of(made, kind, index), outs[kind * 8 + index])

    arrive((3, 0))
    for half in range(2):
        for q in range(3):
            r = R_GRU + (half * 3 + q) * H
            step(3, pack[r : r + H, :] * factor, (half, slice(None), slice(q * H, (q + 1) * H)))
    finish(3)
    arrive((4, 0))
    for k in range(4):
        r = R_LSTM + k * 2 * H
        for block, start in ((0, 0), (1, H), (2, 0)):
            step(
                4,
                pack[r + start : r + start + H, :] * factor,
                (slice(block * H, (block + 1) * H), slice(k * H, (k + 1) * H)),
            )
    finish(4)
    arrive((5, 0))
    step(5, pack[R_FIRST:R_GRU, :] * factor)
    finish(5)
    step(0, grad_in[:EIN, :] * factor)
    step(2, pack[pl.ds(pl.multiple_of(R_EBIAS + place[0], 8), own_rows), :] * factor)
    step(6, pack[R_SECOND : R_SECOND + NT, :] * factor)
    bias = jnp.concatenate([grad_in[G_BIAS : G_BIAS + 1, :], pack[R_MISC + 1 : R_EBIAS, :]], axis=0)
    step(7, bias * factor)
    for copy in going:
        copy.wait()


VM = pl.BlockSpec(memory_space=pltpu.VMEM)
SM = pl.BlockSpec(memory_space=pltpu.SMEM)
HBM = pl.BlockSpec(memory_space=pl.ANY)


def per_device(
    node_feats,
    edge_feats,
    edge_ends,
    atom_counts,
    dataset_flags,
    targets,
    present,
    edge_in,
    edge_out,
    edge_bias,
    gru_weights,
    lstm_weights,
    head_first,
    head_second,
    biases,
    *moments_seconds,
):
    row = lax.axis_index("row")
    row_count = lax.axis_size("row")
    mol = lax.axis_index("mol")
    mol_bits = lax.axis_size("mol").bit_length() - 1
    row_bits = row_count.bit_length() - 1
    mols = node_feats.shape[0]
    own_rows = edge_out.shape[1] // H
    atoms = -(-mols * ATOMS // LB) * LB
    space = -(-mols * LIVE // (2 * LB)) * 2 * LB

    def row_swap(x, k):
        return lax.ppermute(x, "row", [(i, i ^ k) for i in range(row_count)])

    def mol_swap(x, bit):
        return lax.ppermute(x, "mol", [(i, i ^ (1 << bit)) for i in range(2**mol_bits)])

    def double(x, swap, bit):
        other = swap(x)
        return jnp.concatenate(
            [jnp.where(bit == 0, x, other), jnp.where(bit == 0, other, x)], axis=0
        )

    sds = jax.ShapeDtypeStruct
    n = row_count
    al = atoms + WINDOW - 128
    params = pltpu.CompilerParams(vmem_limit_bytes=56 * MIB)

    sent = edge_out.astype(bf16)
    bias_sent = edge_bias.reshape(own_rows, H)

    def forward_order(part):
        part = part.reshape(EH, own_rows, H)
        return part.transpose(1, 0, 2).reshape(own_rows, EH * H)

    parts, bias_parts = {}, {0: bias_sent}
    for bit in reversed(range(row_bits)):
        for k in list(bias_parts):
            bias_parts[k + (1 << bit)] = row_swap(bias_parts[k], 1 << bit)
        if not parts:
            sent, bias_parts = lax.optimization_barrier((sent, bias_parts))
            parts[0] = sent
        parts[1 << bit] = row_swap(sent, 1 << bit)

    ends = lax.dynamic_slice_in_dim(edge_ends, row * mols, mols, 1)
    feats = lax.dynamic_slice_in_dim(edge_feats, row * mols * EM, mols * EM, 1)
    table = jnp.concatenate([feats.reshape(EIN, mols, EM), ends.astype(bf16)], axis=0)
    table = table.transpose(1, 0, 2).reshape(mols, (EIN + 2) * EM)
    places = jnp.stack([(row ^ k) * own_rows for k in range(row_count)]).astype(jnp.int32)
    bias_rows = jnp.pad(biases, (0, 16 * 128 - biases.shape[0])).reshape(16, 128)

    at_hand = [parts[k] for k in range(n // 2)]

    def prepare(*refs):
        body_prepare(mols, *refs[:5], refs[5 : 5 + n // 2], *refs[5 + n // 2 :])

    prepared = pl.pallas_call(
        prepare,
        out_shape=(
            sds((2 + space // LB,), jnp.int32),
            sds((H, atoms), bf16),
            sds((EH, space), bf16),
            sds((EH, space), f32),
            sds((8, space), f32),
            sds((WINDOW, space), bf16),
            sds((WINDOW, space), bf16),
            sds((H, n // 2 * own_rows * H), bf16),
        ),
        in_specs=[SM] + [VM] * (4 + n // 2),
        out_specs=(SM,) + (VM,) * 7,
        scratch_shapes=[pltpu.VMEM((128, 128), f32), pltpu.VMEM((mols * PAD, H), f32)],
        compiler_params=params,
    )(atom_counts, table, node_feats, edge_in, bias_rows, *at_hand)
    forward = {k: forward_order(part) for k, part in parts.items() if k < n // 2}
    parts, bias_parts, places, prepared, forward = lax.optimization_barrier(
        (parts, bias_parts, places, prepared, forward)
    )
    meta, nodes, hid, before, feat, hot_src, hot_dst, turned = prepared
    for bit in reversed(range(row_bits)):
        for k in [k for k in parts if k > 1 << bit and not k & (1 << bit)]:
            parts[k + (1 << bit)] = row_swap(parts[k], 1 << bit)
    parts = [parts[k] for k in range(n)]
    bias_parts = [bias_parts[k] for k in range(n)]
    w_fwd = [forward[k] if k in forward else forward_order(parts[k]) for k in range(n)]

    away = n - n // 2

    def main(*refs):
        at = 10
        body_main(
            mols,
            own_rows,
            *refs[:at],
            refs[at : at + n],
            refs[at + n],
            refs[at + n + 1 : at + n + 1 + away],
            refs[at + n + 1 + away : at + 2 * n + 1 + away],
            *refs[at + 2 * n + 1 + away :],
        )

    pack, sums, src, g = pl.pallas_call(
        main,
        out_shape=(
            sds((R_PACK, 128), f32),
            sds((8, 128), f32),
            sds((LAYERS, H, space), bf16),
            sds((LAYERS, H, space), bf16),
        ),
        in_specs=[SM] * 4 + [VM] * (6 + n) + [HBM] * (1 + away) + [VM] * (n + 5),
        out_specs=(VM,) * 4,
        scratch_shapes=[
            pltpu.VMEM((H * EH, LB), bf16),
            pltpu.VMEM((LAYERS + 1, H, atoms), f32),
            pltpu.VMEM((LAYERS, H, al), bf16),
            pltpu.VMEM((LAYERS, H, atoms), bf16),
            pltpu.VMEM((LAYERS, 4, H, atoms), f32),
            pltpu.VMEM((H, al), f32),
            pltpu.VMEM((H, al), f32),
            pltpu.VMEM((H, atoms), bf16),
            pltpu.VMEM((H, al), bf16),
            pltpu.VMEM((H, H * EH), bf16),
            pltpu.VMEM((STEPS * mols, atoms), f32),
            pltpu.VMEM((STEPS * mols, atoms), f32),
            pltpu.VMEM((2, H, 3 * H), bf16),
            pltpu.VMEM((2, 3 * H, H), bf16),
            pltpu.VMEM((128, 128), f32),
            pltpu.VMEM((H, space), f32),
            pltpu.VMEM((n - n // 2, EH, own_rows * H), bf16),
            pltpu.SemaphoreType.DMA((1 + n - n // 2,)),
        ],
        compiler_params=pltpu.CompilerParams(vmem_limit_bytes=60 * MIB),
    )(
        atom_counts,
        dataset_flags,
        places,
        meta,
        targets.T,
        present.T,
        nodes,
        hid,
        hot_src,
        hot_dst,
        *w_fwd,
        turned,
        *parts[n // 2 :],
        *bias_parts,
        gru_weights,
        bias_rows,
        lstm_weights,
        head_first,
        head_second.T,
    )

    span = own_rows * H // CHUNKS

    def edge_parts(jobs, slots, heights, extra, last):
        kind = "pack" if len(extra) == 2 else "sum"
        if last:
            extra = extra + (before, feat, sums)
        *found, result = pl.pallas_call(
            functools.partial(body_edges, jobs, slots, kind, last),
            grid=(1,),
            out_shape=tuple(sds((height, EH), bf16) for height in heights)
            + (sds((8, EH) if last else (EH, space), f32),),
            in_specs=[SM]
            + [pl.BlockSpec((EH, span), lambda i, c=chunk: (0, c)) for _, chunk in jobs]
            + [VM] * 3
            + ([SM, VM] if kind == "pack" else [VM] * len(extra)),
            out_specs=(VM,) * (len(heights) + 1),
            scratch_shapes=[
                pltpu.VMEM((2, span, LB), bf16),
                pltpu.VMEM((len(jobs), EH, span), f32),
            ]
            + ([pltpu.VMEM((EH, space), f32)] if last else []),
            compiler_params=params,
        )(meta, *(parts[k] for k, _ in jobs), src, g, hid, *extra)
        return found, result

    row_steps = [(functools.partial(row_swap, k=1 << b), (row >> b) & 1) for b in range(row_bits)]
    mol_steps = [(functools.partial(mol_swap, bit=b), (mol >> b) & 1) for b in range(mol_bits)]
    tie = lax.optimization_barrier
    (core, core_bit), (cross, cross_bit) = row_steps

    def halves(x, bit):
        both = x.reshape((2, x.shape[0] // 2) + x.shape[1:])
        return (
            lax.dynamic_index_in_dim(both, 1 - bit, 0, False),
            lax.dynamic_index_in_dim(both, bit, 0, False),
        )

    def as_low(x, count):
        found = []
        for _ in range(count):
            high = lax.reduce_precision(x, 8, 7)
            found.append(high)
            x = x - high
        return jnp.concatenate(found, axis=0).astype(bf16)

    def from_low(x, count):
        x = x.astype(f32).reshape(count, -1, 128)
        found = x[count - 1]
        for k in reversed(range(count - 1)):
            found = found + x[k]
        return found

    def chain(own, pack, beside):
        for swap, bit in mol_steps:
            own_sent, own = halves(own, bit)
            half = own.shape[0]
            sent = [own_sent.astype(bf16)]
            if pack is not None:
                pack_sent, pack = halves(pack, bit)
                sent.append(as_low(pack_sent, 2))
            if beside is not None:
                sent.append(as_low(beside["rows"], 3))
            came = yield swap, jnp.concatenate(sent, axis=0) if len(sent) > 1 else sent[0]
            own = own + came[:half].astype(f32)
            if pack is not None:
                pack = pack + from_low(came[half : half + 2 * pack.shape[0]], 2)
            if beside is not None:
                beside["rows"] = beside["rows"] + from_low(came[half:], 3)
        piece = own if pack is None else jnp.concatenate([own, pack], axis=0)
        height, rest = piece.shape[0], own.shape[0]
        largest = jnp.maximum(jnp.max(jnp.abs(piece)), 1e-30)
        power = 14.0 - jnp.ceil(jnp.log2(largest))
        sent = jnp.concatenate(
            [piece * jnp.exp2(power), jnp.broadcast_to(power, (16, 128))], axis=0
        ).astype(jnp.float16)
        for swap, bit in reversed(mol_steps):
            came = yield swap, sent
            sent = jnp.concatenate(
                [jnp.where(bit == 0, sent, came), jnp.where(bit == 0, came, sent)], axis=0
            )
        raw, sent = sent, sent.astype(f32).reshape(-1, height + 16, 128)
        back = jnp.exp2(-sent[:, height : height + 1, 0:1])
        own = (sent[:, :rest] * back).reshape(-1, 128)
        square = jnp.sum(own * own)
        if pack is not None:
            pack = raw.reshape(-1, height + 16, 128)[:, rest:].reshape(-1, 128)
            square = square + jnp.sum(jnp.square(sent[:, rest:height] * back))
        return own, pack, square

    core_place = (1 - core_bit).reshape(1).astype(jnp.int32)
    half = pack.shape[0] // 2
    (message, far), carry = edge_parts(
        ((2, 0), (3, 0)),
        ((1, 0), (0, 0)),
        (span + 2 * half, span),
        (core_place, pack),
        False,
    )
    came = core(message)
    pack = halves(pack, core_bit)[1]
    pack_sent, pack = halves(pack + from_low(came[span:], 2), cross_bit)
    sent = (far.astype(f32) + came[:span].astype(f32)).astype(bf16)
    sent = jnp.concatenate([sent, as_low(pack_sent, 2)], axis=0)
    sent, carry = tie((sent, carry))
    arrived = cross(sent)
    (message, near, far), carry = edge_parts(
        ((0, 0), (1, 0), (2, 1), (3, 1)),
        ((1, 0), (0, 0), (2, 0), (0, span)),
        (2 * span, span, span),
        (carry,),
        False,
    )
    message, arrived = tie((message, arrived))
    came = core(message)
    own = near.astype(f32) + came[:span].astype(f32) + arrived[:span].astype(f32)
    pack = pack + from_low(arrived[span:], 2)
    sent = (far.astype(f32) + came[span:].astype(f32)).astype(bf16)

    first = chain(own, pack, None)
    first_swap, first_sent = next(first)
    sent, first_sent, carry = tie((sent, first_sent, carry))
    arrived = cross(sent)
    first_came = first_swap(first_sent)
    (message, near), grad_in = edge_parts(
        ((0, 1), (1, 1)), ((1, 0), (0, 0)), (span + 32, span), (carry,), True
    )
    message, arrived, first_came = tie((message, arrived, first_came))
    came = core(message)
    beside = {"rows": grad_in + from_low(came[span : span + 24], 3)}
    own = near.astype(f32) + came[:span].astype(f32) + arrived.astype(f32)

    second = chain(own, None, beside)
    second_swap, second_sent = next(second)
    first_swap, first_sent = first.send(first_came)
    while True:
        first_came, second_came = first_swap(first_sent), second_swap(second_sent)
        second_swap, second_sent = second.send(second_came)
        try:
            first_swap, first_sent = first.send(first_came)
        except StopIteration as end:
            first_own, pack, square = end.value
            break
    second_came, came = second_swap(second_sent), cross(pack)
    rows, pack = tie((beside["rows"], pack))
    came_rows = cross(rows)
    try:
        second.send(second_came)
    except StopIteration as end:
        second_own, _, more = end.value
    squares = jnp.broadcast_to(square + more, (8, 128))
    came, came_rows, _ = tie((came, came_rows, squares))
    grad_in = rows + came_rows
    pack = jnp.concatenate(
        [jnp.where(cross_bit == 0, pack, came), jnp.where(cross_bit == 0, came, pack)], axis=0
    )
    came = core(pack)
    pack = jnp.concatenate(
        [jnp.where(core_bit == 0, pack, came), jnp.where(core_bit == 0, came, pack)], axis=0
    )
    pack = pack.astype(f32).reshape(n * 2**mol_bits, -1, 128)
    pack = (pack[:, :-16] * jnp.exp2(-pack[:, -16:-15, 0:1])).reshape(-1, 128)
    came = row_swap(squares, 3)
    came, pack, grad_in = tie((came, pack, grad_in))
    squares = (squares + row_swap(squares, 1)) + (row_swap(squares, 2) + came)
    owns = [first_own, second_own]

    weights = [
        edge_in,
        edge_out,
        edge_bias,
        gru_weights,
        lstm_weights,
        head_first,
        head_second,
        biases,
    ]
    states = []
    for group in (weights, moments_seconds[:8], moments_seconds[8:]):
        group = list(group)
        group[2] = group[2].reshape(own_rows, H)
        group[6] = group[6].T
        if group[7] is biases:
            group[7] = bias_rows
        else:
            group[7] = jnp.pad(group[7], (0, 16 * 128 - group[7].shape[0])).reshape(16, 128)
        states += group
    spots = [HBM if index in BIG else VM for index in range(8)] * 3
    copies = 3 * (own_rows * H // WIDE + len(BIG) - 1)
    shapes = [sds(state.shape, f32) for state in states]
    results = pl.pallas_call(
        functools.partial(body_adamw, own_rows),
        out_shape=tuple(shapes) + (sds((1, 1), f32),) * 3,
        in_specs=[SM] + [HBM] * (CHUNKS + 1) + [VM] * 2 + spots,
        out_specs=tuple(spots) + (VM,) * 3,
        scratch_shapes=[pltpu.VMEM(own.shape, f32) for own in owns]
        + [pltpu.VMEM(pack.shape, f32)]
        + [pltpu.VMEM(shapes[index].shape, f32) for _ in range(6) for index in BIG]
        + [pltpu.SemaphoreType.DMA((copies + CHUNKS + 1,)), pltpu.SemaphoreType.DMA((copies,))],
        compiler_params=params,
    )(places, *owns, pack, grad_in, squares, *states)
    results = list(results)
    for kind in range(3):
        results[kind * 8 + 2] = results[kind * 8 + 2].reshape(own_rows * H)
        results[kind * 8 + 6] = results[kind * 8 + 6].T
        results[kind * 8 + 7] = results[kind * 8 + 7].reshape(-1)[: biases.shape[0]]
    for index in range(24, 27):
        results[index] = results[index].reshape(())
    return tuple(results)


def solution(mesh):
    weights = (P(), P(None, "row"), P("row"), P(), P(), P(), P(), P())
    in_specs = (
        P(("mol", "row"), None, None),
        P(None, "mol"),
        P(None, "mol", None),
        P(("mol", "row")),
        P(("mol", "row")),
        P(("mol", "row"), None),
        P(("mol", "row"), None),
    ) + weights * 3
    out_specs = weights * 3 + (P(), P(), P())
    return jax.shard_map(
        per_device, mesh=mesh, in_specs=in_specs, out_specs=out_specs, check_vma=False
    )
```

```python
import functools
import math

import jax
import jax.numpy as jnp
from jax import lax
from jax.experimental import pallas as pl
from jax.experimental.pallas import tpu as pltpu
from jax.sharding import PartitionSpec as P

H = 128
EH = 128
EIN = 5
NT = 12
STEPS = 6
ATOMS = 29
EM = 64
LAYERS = 2
STEP_COUNT = 10

PAD = 32
LIVE = 2 * (ATOMS - 1)
LB = 256
MIB = 2**20

f32 = jnp.float32
bf16 = jnp.bfloat16
highest = lax.Precision.HIGHEST
beta_one = 0.9
beta_two = 0.999
rate = 0.05
epsilon = 1e-08
decay = 0.01
clip_norm = 0.1

R_LSTM, R_FIRST, R_GRU, R_SECOND, R_MISC, R_EBIAS, R_END = 0, 1024, 1280, 2048, 2064, 2080, 2208
R_PACK = 2560
M_INPUT, M_LSTM, M_HEAD, M_OUT = 1, 7, 11, 12
G_BIAS, G_SUMS = EIN, EIN + 1
WINDOW = 384
CHUNKS = 2

NN = ((1,), (0,))
NTR = ((1,), (1,))
TN = ((0,), (0,))


def mm(a, b, dims=NN):
    return lax.dot_general(a, b, (dims, ((), ())), preferred_element_type=f32)


def split(x):
    high = x.astype(bf16)
    return high, (x - high.astype(f32)).astype(bf16)


def mm3(a, b, dims=NN):
    if dims[0] == (1,) and a[0].shape[0] in (16, 32, 64):
        rows = a[0].shape[0]
        both = mm(jnp.concatenate(a, axis=0), b[0], dims)
        return both[:rows] + (both[rows:] + mm(a[0], b[1], dims))
    return mm(a[0], b[0], dims) + (mm(a[0], b[1], dims) + mm(a[1], b[0], dims))


def mm_stack(a, b):
    high, low = split(a)
    rows = a.shape[0]
    left = jnp.concatenate(
        [
            jnp.concatenate([high, high], axis=1),
            jnp.concatenate([low, jnp.zeros_like(low)], axis=1),
        ],
        axis=0,
    )
    both = mm(left, b)
    return both[:rows] + both[rows:]


def mm_stack_t(a, b):
    rows, width = a.shape[0], b.shape[0] // 2
    both = mm(jnp.concatenate(split(a), axis=0), b, NTR)
    return both[:rows, :width] + (both[rows:, :width] + both[:rows, width:])


def mm2(a, b, dims=NN):
    high, low = split(a)
    return mm(high, b, dims) + mm(low, b, dims)


def total_of(x):
    return jnp.sum(jnp.sum(x, axis=1, keepdims=True), axis=0, keepdims=True)


def columns(start, size):
    return pl.ds(pl.multiple_of(start, size), size)


def sigmoid(v):
    return jax.nn.sigmoid(v)


def column_of(values, size):
    at = lax.broadcasted_iota(jnp.int32, (size, 1), 0)
    found = jnp.zeros((size, 1), jnp.int32)
    for m in range(size):
        found = jnp.where(at == m, values[m], found)
    return found


def row_of(values, size):
    at = lax.broadcasted_iota(jnp.int32, (1, size), 1)
    found = jnp.zeros((1, size), jnp.int32)
    for m in range(size):
        found = jnp.where(at == m, values[m], found)
    return found


def starts_of(column, size):
    below = (
        lax.broadcasted_iota(jnp.int32, (size, size), 1)
        < lax.broadcasted_iota(jnp.int32, (size, size), 0)
    ).astype(bf16)
    return mm(below, jnp.broadcast_to(column, (size, 128)).astype(bf16))[:, :1]


def body_prepare(
    mols,
    counts_s,
    table,
    node_feats,
    edge_in,
    bias_rows,
    nat,
    meta,
    nodes_o,
    hid_o,
    before_o,
    feat_o,
    hot_src,
    hot_dst,
    turned_o,
    square,
    flat,
):
    lanes = nodes_o.shape[1]
    space = hid_o.shape[1]
    for b in range(space // LB):
        meta[2 + b] = jnp.int32(0)
    edges, atoms = jnp.int32(0), jnp.int32(0)
    for m in range(mols):
        live = 2 * (counts_s[m] - 1)
        block = lax.div(edges + (LB - 1), jnp.int32(LB))

        @pl.when(block * LB < edges + live)
        def _(block=block, atoms=atoms):
            meta[2 + block] = lax.div(atoms, jnp.int32(128)) * 128

        edges = edges + live
        atoms = atoms + counts_s[m]
    blocks = lax.div(edges + (LB - 1), jnp.int32(LB))
    meta[0] = blocks
    meta[1] = lax.div(atoms + (LB - 1), jnp.int32(LB))

    count_col = column_of(counts_s, mols).astype(f32)
    live_col = 2.0 * (count_col - 1.0)
    start_col = starts_of(live_col, mols)
    atom_col = starts_of(count_col, mols)

    width = nat[0].shape[1]

    def turn(i, carry):
        for k, part in enumerate(nat):
            turned_o[:, pl.ds(pl.multiple_of(k * width + i * H, H), H)] = jnp.transpose(
                part[:, columns(i * H, H)]
            )
        return carry

    lax.fori_loop(0, width // H, turn, 0)

    square[...] = jnp.zeros_like(square)
    square[0:EIN, :] = edge_in[...]
    square[8:24, :] = bias_rows[...]
    turned = jnp.transpose(square[...])
    in_t, b_in_col = turned[:, :8], turned[:, 8:9]
    e_high, e_low = split(in_t)
    e_rest = (in_t - e_high.astype(f32) - e_low.astype(f32)).astype(bf16)

    flat[...] = jnp.zeros_like(flat)
    for m in range(mols):
        flat[m * PAD : m * PAD + ATOMS, :] = node_feats[m].astype(f32)
    flat_low = flat[...].astype(bf16)
    nodes_o[...] = jnp.zeros_like(nodes_o)
    atom_at = lax.broadcasted_iota(jnp.int32, (mols * PAD, 1), 0)
    spread = (
        lax.broadcasted_iota(jnp.int32, (mols * PAD, mols), 0) // PAD
        == lax.broadcasted_iota(jnp.int32, (mols * PAD, mols), 1)
    ).astype(bf16)
    goal_high = jnp.floor(atom_col * (1.0 / 8.0))
    goal_parts = jnp.concatenate([goal_high, atom_col - 8.0 * goal_high, count_col], axis=1)
    goal = mm(
        spread,
        jnp.concatenate([goal_parts, jnp.zeros((mols, 125), f32)], axis=1).astype(bf16),
    )
    within = lax.rem(atom_at, jnp.int32(PAD)).astype(f32)
    target = jnp.where(
        within < goal[:, 2:3], 8.0 * goal[:, 0:1] + goal[:, 1:2] + within, -1.0
    ).astype(jnp.int32)

    def pack_atoms(k, carry):
        c = columns(k * LB, LB)
        at = lax.broadcasted_iota(jnp.int32, (mols * PAD, LB), 1) + k * LB
        hot = (at == target).astype(f32).astype(bf16)
        nodes_o[:, c] = mm(flat_low, hot, TN).astype(bf16)
        return carry

    lax.fori_loop(0, meta[1], pack_atoms, 0)

    def prepare(b, carry):
        c = columns(b * LB, LB)
        spot = (lax.broadcasted_iota(jnp.int32, (mols, LB), 1) + b * LB).astype(f32)
        mol_hot = ((spot >= start_col) & (spot < start_col + live_col)).astype(f32)
        rows = mm(table[...], mol_hot.astype(bf16), TN)
        start_row = jnp.sum(mol_hot * start_col, axis=0, keepdims=True)
        base = jnp.sum(mol_hot * atom_col, axis=0, keepdims=True)
        valid = jnp.sum(mol_hot, axis=0, keepdims=True)
        slot = spot[:1] - start_row
        slot_hot = (lax.broadcasted_iota(jnp.int32, (EM, LB), 0).astype(f32) == slot).astype(f32)
        picked = [
            jnp.sum(rows[r * EM : (r + 1) * EM] * slot_hot, axis=0, keepdims=True)
            for r in range(EIN + 2)
        ]
        feat = jnp.concatenate(picked[:EIN] + [valid, jnp.zeros((2, LB), f32)], axis=0)
        feat_o[:, c] = feat
        feat_low = feat.astype(bf16)
        before = mm(e_high, feat_low) + mm(e_low, feat_low) + mm(e_rest, feat_low) + b_in_col
        before_o[:, c] = before
        hid_o[:, c] = (before * sigmoid(before)).astype(bf16)
        atom = lax.broadcasted_iota(jnp.int32, (WINDOW, LB), 0)
        base = base - meta[2 + b].astype(f32)
        src = jnp.where(valid > 0.5, base + picked[EIN], -1.0).astype(jnp.int32)
        dst = jnp.where(valid > 0.5, base + picked[EIN + 1], -1.0).astype(jnp.int32)
        hot_src[:, c] = (atom == src).astype(f32).astype(bf16)
        hot_dst[:, c] = (atom == dst).astype(f32).astype(bf16)
        return carry

    lax.fori_loop(0, 2 * lax.div(blocks + 1, jnp.int32(2)), prepare, 0)


def body_main(
    mols,
    own_rows,
    counts_s,
    flags_s,
    places,
    meta,
    targets,
    present,
    nodes,
    hid_i,
    hot_src,
    hot_dst,
    w_fwd,
    turned_h,
    nat_h,
    ebias_parts,
    gru,
    bias_rows,
    lstm_rows,
    first,
    second,
    pack,
    sums_o,
    src_o,
    g_o,
    z,
    st,
    low,
    msg,
    keep,
    acc,
    dst_acc,
    gm,
    gm_rel,
    w_back,
    w_all,
    ds_all,
    gru_n,
    gru_t,
    square,
    moved_s,
    w_nat,
    late_sem,
):
    parts = len(w_fwd)
    blocks, chunks = meta[0], meta[1]
    turned_width = turned_h.shape[1]
    late = [pltpu.make_async_copy(turned_h, w_back.at[:, :turned_width], late_sem.at[0])]
    for k in range(len(nat_h)):
        late.append(pltpu.make_async_copy(nat_h[k], w_nat.at[k], late_sem.at[1 + k]))
    for copy in late:
        copy.start()
    atoms = w_all.shape[1]

    def place(k):
        return pl.ds(pl.multiple_of(places[k], own_rows), own_rows)

    def window(b):
        return pl.ds(pl.multiple_of(meta[2 + b], 128), WINDOW)

    square[...] = jnp.zeros_like(square)
    square[0:16, :] = bias_rows[...]
    turned = jnp.transpose(square[...])
    gbias_col = [
        jnp.concatenate([turned[:, r + q : r + q + 1] for q in range(3)], axis=0)
        for r in (M_INPUT, M_INPUT + 3)
    ]
    c_lstm = jnp.concatenate(
        [bias_rows[M_LSTM + k : M_LSTM + k + 1, :] for k in range(4)], axis=1
    )
    c_head = bias_rows[M_HEAD : M_HEAD + 1, :]
    out_cols = [turned[k * NT : (k + 1) * NT, M_OUT : M_OUT + 1] for k in range(3)]
    gru_n[...] = gru[...].astype(bf16)
    for half in range(2):
        for q in range(3):
            gru_t[half, q * H : (q + 1) * H, :] = jnp.transpose(
                gru_n[half, :, q * H : (q + 1) * H]
            )
    ebias = jnp.concatenate([part[...] for part in ebias_parts], axis=0)
    b_high, b_low = split(ebias)

    def in_pairs(step):
        def both(p, carry):
            step(2 * p)
            step(2 * p + 1)
            return carry

        lax.fori_loop(0, lax.div(blocks + 1, jnp.int32(2)), both, 0)

    def deliver(into, hot):
        def both(p, carry):
            found = []
            for u in range(2):
                c = columns((2 * p + u) * LB, LB)
                found.append(mm2(moved_s[:, c], hot[:, c], NTR))
            for u in range(2):
                into[:, window(2 * p + u)] += found[u]
            return carry

        lax.fori_loop(0, lax.div(blocks + 1, jnp.int32(2)), both, 0)

    b_fwd = jnp.concatenate([b_high, b_low], axis=1)
    moved_s[...] = jnp.zeros_like(moved_s)

    for layer in range(LAYERS):
        low[layer] = jnp.zeros_like(low[layer])
    low[0, :, :atoms] = nodes[...]
    st[0] = nodes[...].astype(f32)
    st[LAYERS] = jnp.zeros_like(st[LAYERS])
    gm_rel[...] = jnp.zeros_like(gm_rel)
    for layer in range(LAYERS):
        acc[...] = jnp.zeros_like(acc)

        def fetch(b, layer=layer):
            c = columns(b * LB, LB)
            src_o[layer, :, c] = mm(low[layer, :, window(b)], hot_src[:, c]).astype(bf16)

        def move(b, carry, layer=layer):
            c = columns(b * LB, LB)
            source = src_o[layer, :, c]
            for h in range(EH):
                z[h * H : (h + 1) * H, :] = hid_i[pl.ds(h, 1), c] * source
            moved_s[:, c] = mm(jnp.concatenate([part[...] for part in w_fwd], axis=0), z[...]) + mm(
                b_fwd, jnp.concatenate([source, source], axis=0)
            )
            return carry

        in_pairs(fetch)
        lax.fori_loop(0, blocks, move, 0)
        deliver(acc, hot_dst)
        for k in range(parts):
            msg[layer, place(k), :] = acc[k * own_rows : (k + 1) * own_rows, :atoms].astype(bf16)

        def update(k, carry, layer=layer):
            c = columns(k * LB, LB)
            from_in = mm(gru_t[0], msg[layer, :, c]) + gbias_col[0]
            from_st = mm(gru_t[1], low[layer, :, c]) + gbias_col[1]
            reset = sigmoid(from_in[:H] + from_st[:H])
            upd = sigmoid(from_in[H : 2 * H] + from_st[H : 2 * H])
            fresh = jnp.tanh(from_in[2 * H :] + reset * from_st[2 * H :])
            new = (1.0 - upd) * fresh + upd * st[layer, :, c]
            st[layer + 1, :, c] = new
            if layer + 1 < LAYERS:
                low[layer + 1, :, c] = new.astype(bf16)
            keep[layer, 0, :, c] = reset
            keep[layer, 1, :, c] = upd
            keep[layer, 2, :, c] = fresh
            keep[layer, 3, :, c] = from_st[2 * H :]
            return carry

        lax.fori_loop(0, chunks, update, 0)

    lane = lax.broadcasted_iota(jnp.int32, (mols, atoms), 1).astype(f32)
    count_col = column_of(counts_s, mols).astype(f32)
    slot_of = lane - starts_of(count_col, mols)
    alive = (slot_of >= 0.0) & (slot_of < count_col)
    x = jnp.concatenate(split(st[LAYERS]), axis=0)
    lstm = jnp.concatenate(
        [lstm_rows[0:H, :] + lstm_rows[2 * H : 3 * H, :], lstm_rows[H : 2 * H, :]], axis=0
    )
    lstm_w = split(lstm)
    zeros = jnp.zeros((mols, H), f32)
    hidden, read, cell = zeros, zeros, zeros
    saved = []
    for step in range(STEPS):
        query = jnp.concatenate([hidden, read], axis=1)
        if step == 0:
            gates = jnp.broadcast_to(c_lstm, (mols, 4 * H))
        else:
            gates = mm3(split(query), lstm_w) + c_lstm
        in_gate = sigmoid(gates[:, :H])
        forget = sigmoid(gates[:, H : 2 * H])
        part = jnp.tanh(gates[:, 2 * H : 3 * H])
        out_gate = sigmoid(gates[:, 3 * H :])
        before_cell = cell
        cell = forget * cell + in_gate * part
        squashed = jnp.tanh(cell)
        hidden = out_gate * squashed
        scores = jnp.where(alive, mm_stack(hidden, x), -1e30)
        weights = jnp.where(alive, jnp.exp(scores - jnp.max(scores, axis=1, keepdims=True)), 0.0)
        weights = weights / jnp.sum(weights, axis=1, keepdims=True)
        w_all[step * mols : (step + 1) * mols, :] = weights
        read = mm_stack_t(weights, x)
        saved.append((query, in_gate, forget, part, out_gate, before_cell, squashed, hidden))
    query = jnp.concatenate([hidden, read], axis=1)
    first_w = split(first[...])
    second_w = split(second[...])
    query_s = split(query)
    inner_pre = mm3(query_s, first_w) + c_head
    inner_sig = sigmoid(inner_pre)
    inner = inner_pre * inner_sig
    inner_s = split(inner)
    is_one = row_of(flags_s, mols) == 1
    predicted = (
        mm3(second_w, inner_s, NTR)
        + out_cols[0]
        + jnp.where(is_one, out_cols[2], out_cols[1])
    )
    there = present[...].astype(f32)
    diff = predicted - targets[...]
    lanes = lax.broadcasted_iota(jnp.int32, (1, 128), 1)
    loss = total_of(there * diff * diff)
    count = total_of(there)
    sums_o[...] = jnp.zeros_like(sums_o)
    sums_o[G_SUMS : G_SUMS + 1, :] = jnp.where(lanes == 0, loss, jnp.where(lanes == 1, count, 0.0))

    d_pred = 2.0 * there * diff
    d_pred_s = split(d_pred)
    pack[R_SECOND:R_MISC, :] = jnp.zeros((R_MISC - R_SECOND, 128), f32)
    pack[R_SECOND : R_SECOND + NT, :] = mm3(d_pred_s, inner_s)
    pack[R_MISC:R_EBIAS, :] = jnp.zeros((R_EBIAS - R_MISC, 128), f32)
    zero_pred = jnp.where(is_one, 0.0, d_pred)
    out_sums = jnp.concatenate([d_pred, zero_pred, d_pred - zero_pred], axis=0)
    out_high, out_low = split(out_sums)
    out_ones = jnp.ones((8, mols), bf16)
    pack[R_MISC + M_OUT : R_MISC + M_OUT + 1, : 3 * NT] = (
        mm(out_ones, out_high, NTR) + mm(out_ones, out_low, NTR)
    )[:1]
    d_inner = mm3(d_pred_s, second_w, TN)
    d_pre = d_inner * inner_sig * (1.0 + inner_pre * (1.0 - inner_sig))
    d_pre_s = split(d_pre)
    pack[R_FIRST:R_GRU, :] = mm3(query_s, d_pre_s, TN)
    pack[R_MISC + M_HEAD : R_MISC + M_HEAD + 1, :] = jnp.sum(d_pre, axis=0, keepdims=True)
    d_query = mm3(d_pre_s, first_w, NTR)
    d_hidden, d_read = d_query[:, :H], d_query[:, H:]
    d_cell = zeros
    d_gates_all = [None] * STEPS
    d_reads = [None] * STEPS
    for step in reversed(range(STEPS)):
        query, in_gate, forget, part, out_gate, before_cell, squashed, hid_t = saved[step]
        weights = w_all[step * mols : (step + 1) * mols, :]
        d_reads[step] = d_read
        d_weights = mm_stack(d_read, x)
        d_scores = weights * (d_weights - jnp.sum(weights * d_weights, axis=1, keepdims=True))
        ds_all[step * mols : (step + 1) * mols, :] = d_scores
        d_hidden = d_hidden + mm_stack_t(d_scores, x)
        d_out = d_hidden * squashed * out_gate * (1.0 - out_gate)
        d_cell = d_cell + d_hidden * out_gate * (1.0 - squashed * squashed)
        d_forget = d_cell * before_cell * forget * (1.0 - forget)
        d_in = d_cell * part * in_gate * (1.0 - in_gate)
        d_part = d_cell * in_gate * (1.0 - part * part)
        d_cell = d_cell * forget
        d_gates = jnp.concatenate([d_in, d_forget, d_part, d_out], axis=1)
        d_gates_all[step] = d_gates
        if step > 0:
            d_query = mm3(split(d_gates), lstm_w, NTR)
            d_hidden, d_read = d_query[:, :H], d_query[:, H:]
    queries = split(jnp.concatenate([saved[s][0] for s in range(STEPS)], axis=0))
    d_gates_cat = jnp.concatenate(d_gates_all, axis=0)
    d_gates_s = split(d_gates_cat)
    grad_lstm = mm3(queries, d_gates_s, TN)
    d_gates_sum = jnp.sum(d_gates_cat, axis=0, keepdims=True)
    for k in range(4):
        pack[R_LSTM + k * 256 : R_LSTM + (k + 1) * 256, :] = grad_lstm[:, k * H : (k + 1) * H]
        pack[R_MISC + M_LSTM + k : R_MISC + M_LSTM + k + 1, :] = d_gates_sum[:, k * H : (k + 1) * H]
    left = jnp.concatenate(d_reads + [saved[s][7] for s in range(STEPS)], axis=0)
    left_s = split(left)

    def spread(k, carry):
        c = columns(k * LB, LB)
        right = split(jnp.concatenate([w_all[:, c], ds_all[:, c]], axis=0))
        dst_acc[:, c] = mm3(left_s, right, TN)
        return carry

    dst_acc[...] = jnp.zeros_like(dst_acc)
    lax.fori_loop(0, chunks, spread, 0)

    pack[R_GRU:R_SECOND, :] = jnp.zeros((6 * H, 128), f32)
    gm[...] = jnp.zeros_like(gm)
    for layer in reversed(range(LAYERS)):

        def back(k, carry, layer=layer):
            c = columns(k * LB, LB)
            d_state = dst_acc[:, c]
            reset, upd = keep[layer, 0, :, c], keep[layer, 1, :, c]
            fresh, from_st = keep[layer, 2, :, c], keep[layer, 3, :, c]
            d_upd = d_state * (st[layer, :, c] - fresh) * upd * (1.0 - upd)
            d_fresh = d_state * (1.0 - upd) * (1.0 - fresh * fresh)
            d_reset = d_fresh * from_st * reset * (1.0 - reset)
            d_from_in = jnp.concatenate([d_reset, d_upd, d_fresh], axis=0)
            d_from_st = jnp.concatenate([d_reset, d_upd, d_fresh * reset], axis=0)
            in_s, st_s = split(d_from_in), split(d_from_st)
            gm[:, c] = (mm(gru_n[0], in_s[0]) + mm(gru_n[0], in_s[1])).astype(bf16)
            if layer > 0:
                dst_acc[:, c] = d_state * upd + (mm(gru_n[1], st_s[0]) + mm(gru_n[1], st_s[1]))
            ones = jnp.ones((8, LB), bf16)
            message, state_low = msg[layer, :, c], low[layer, :, c]
            for half, left_m, right_m in ((0, message, in_s), (1, state_low, st_s)):
                grad = mm(left_m, right_m[0], NTR) + mm(left_m, right_m[1], NTR)
                sums = (mm(ones, right_m[0], NTR) + mm(ones, right_m[1], NTR))[:1]
                for q in range(3):
                    r = R_GRU + (half * 3 + q) * H
                    pack[r : r + H, :] += grad[:, q * H : (q + 1) * H]
                    m = R_MISC + M_INPUT + half * 3 + q
                    pack[m : m + 1, :] += sums[:, q * H : (q + 1) * H]
            return carry

        lax.fori_loop(0, chunks, back, 0)
        for k in range(parts):
            gm_rel[k * own_rows : (k + 1) * own_rows, :atoms] = gm[place(k), :]
        if layer > 0:
            b_pull = jnp.concatenate(split(jnp.transpose(ebias)), axis=1)
            for copy in late:
                copy.wait()

            def turn(i, carry):
                for k in range(len(nat_h)):
                    at = pl.multiple_of(turned_width + k * own_rows * H + i * H, H)
                    w_back[:, pl.ds(at, H)] = jnp.transpose(w_nat[k, :, columns(i * H, H)])
                return carry

            lax.fori_loop(0, own_rows, turn, 0)

            def take(b, layer=layer):
                c = columns(b * LB, LB)
                g_o[layer, :, c] = mm(gm_rel[:, window(b)], hot_dst[:, c]).astype(bf16)

            def pull(b, carry, layer=layer):
                c = columns(b * LB, LB)
                hid = hid_i[:, c]
                grad = g_o[layer, :, c]
                for i in range(H):
                    z[i * EH : (i + 1) * EH, :] = g_o[layer, pl.ds(i, 1), c] * hid
                moved_s[:, c] = mm(w_back[...], z[...]) + mm(
                    b_pull, jnp.concatenate([grad, grad], axis=0)
                )
                return carry

            in_pairs(take)
            lax.fori_loop(0, blocks, pull, 0)
            deliver(dst_acc, hot_src)
        else:

            def take(b, layer=layer):
                c = columns(b * LB, LB)
                g_o[layer, :, c] = mm(gm_rel[:, window(b)], hot_dst[:, c]).astype(bf16)

            in_pairs(take)
    acc_b = acc.at[:, :H]
    acc_b[...] = jnp.zeros((H, H), f32)

    def bias_sum(b, carry):
        c = columns(b * LB, LB)
        acc_b[...] += mm(g_o[0, :, c], src_o[0, :, c], NTR) + mm(
            g_o[1, :, c], src_o[1, :, c], NTR
        )
        return carry

    lax.fori_loop(0, blocks, bias_sum, 0)
    for k in range(parts):
        row = pl.multiple_of(R_EBIAS + places[k], 8)
        pack[pl.ds(row, own_rows), :] = acc_b[k * own_rows : (k + 1) * own_rows, :]
    pack[R_END:R_PACK, :] = jnp.zeros((R_PACK - R_END, 128), f32)


def body_edges(jobs, slots, extra_in, last, meta, *refs):
    n = len(jobs)
    ws, (src, g, hid), refs = refs[:n], refs[n : n + 3], refs[n + 3 :]
    if extra_in == "pack":
        (place, pack), refs = refs[:2], refs[2:]
    else:
        hid_before, refs = refs[0], refs[1:]
    if last:
        (before, feat, sums), refs = refs[:3], refs[3:]
    count = 1 + max(slot for slot, _ in slots)
    outs, result, refs = refs[:count], refs[count], refs[count + 1 :]
    built, acc = refs[:2]
    grad_hid = refs[2] if last else result
    blocks = meta[0]
    rows = ws[0].shape[1] // H
    span = rows * EH

    if extra_in == "pack":
        half = pack.shape[0] // 2
        sent = pack[pl.ds(pl.multiple_of(place[0] * half, half), half), :]
        high, low = split(sent)
        outs[0][span : span + half, :] = high
        outs[0][span + half : span + 2 * half, :] = low

    acc[...] = jnp.zeros_like(acc)

    def edges(b, carry):
        c = columns(b * LB, LB)
        s0, s1 = src[0, :, c].astype(f32), src[1, :, c].astype(f32)
        pulled = None if extra_in == "pack" else hid_before[:, c]
        for q, (rel, chunk) in enumerate(jobs):
            at = (rel * CHUNKS + chunk) * rows
            g0 = g[0, at : at + rows, c].astype(f32)
            g1 = g[1, at : at + rows, c].astype(f32)
            for i in range(rows):
                built[q % 2, i * H : (i + 1) * H, :] = (
                    g0[i : i + 1] * s0 + g1[i : i + 1] * s1
                ).astype(bf16)
            part = mm(ws[q][...], built[q % 2])
            pulled = part if pulled is None else pulled + part
            acc[q] += mm(hid[:, c], built[q % 2], NTR)
        grad_hid[:, c] = pulled
        return carry

    lax.fori_loop(0, blocks, edges, 0)
    for q, (slot, at) in enumerate(slots):
        for i in range(rows):
            r = at + i * EH
            outs[slot][r : r + EH, :] = acc[q, :, i * H : (i + 1) * H].astype(bf16)

    if last:
        result[...] = sums[...]

        def finish(b, carry):
            c = columns(b * LB, LB)
            ahead = before[:, c]
            sig = sigmoid(ahead)
            grad = split(grad_hid[:, c] * sig * (1.0 + ahead * (1.0 - sig)))
            rows_low = feat[:, c].astype(bf16)
            result[...] += mm(rows_low, grad[0], NTR) + mm(rows_low, grad[1], NTR)
            return carry

        lax.fori_loop(0, blocks, finish, 0)


def adamw(weight, grad, moment, second):
    moment_new = beta_one * moment + (1.0 - beta_one) * grad
    second_new = beta_two * second + (1.0 - beta_two) * grad * grad
    mean_hat = moment_new * (1.0 / (1.0 - beta_one**STEP_COUNT))
    square_hat = second_new * (1.0 / (1.0 - beta_two**STEP_COUNT))
    return (
        weight - rate * (mean_hat / (jnp.sqrt(square_hat) + epsilon) + decay * weight),
        moment_new,
        second_new,
    )


BIG = (1, 3, 4, 5)
WIDE = 1024


def body_adamw(own_rows, place, *refs):
    owns_h, refs = refs[:CHUNKS], refs[CHUNKS:]
    (pack_h, grad_in, squares), refs = refs[:3], refs[3:]
    states, outs, refs = refs[:24], refs[24:48], refs[48:]
    (loss, count, norm), refs = refs[:3], refs[3:]
    owns, pack, bufs, made, in_sem, out_sem = refs[0:CHUNKS], refs[2], refs[3:15], refs[15:27], refs[27], refs[28]
    columns_out = states[1].shape[1]
    waits, ins, going = {}, 0, []

    def fetch(key, source, target):
        nonlocal ins
        copy = pltpu.make_async_copy(source, target, in_sem.at[ins])
        copy.start()
        waits.setdefault(key, []).append(copy)
        ins += 1

    def buffer_of(group, kind, index):
        return group[kind * 4 + BIG.index(index)]

    fetch("pack", pack_h, pack)
    spans = [pl.ds(at, WIDE) for at in range(0, columns_out, WIDE)]
    per = len(spans) // CHUNKS
    for c in range(CHUNKS):
        fetch(("own", c), owns_h[c], owns[c])
        for k in range(c * per, (c + 1) * per):
            for kind in range(3):
                fetch(
                    (1, k),
                    states[kind * 8 + 1].at[:, spans[k]],
                    buffer_of(bufs, kind, 1).at[:, spans[k]],
                )
    for index in BIG[1:]:
        for kind in range(3):
            fetch((index, 0), states[kind * 8 + index], buffer_of(bufs, kind, index))

    def arrive(key):
        for copy in waits[key]:
            copy.wait()

    def send(source, target):
        copy = pltpu.make_async_copy(source, target, out_sem.at[len(going)])
        copy.start()
        going.append(copy)

    def step(index, grad, at=...):
        big = index in BIG
        now = [buffer_of(bufs, k, index) if big else states[k * 8 + index] for k in range(3)]
        new = adamw(now[0][at], grad, now[1][at], now[2][at])
        for kind in range(3):
            target = buffer_of(made, kind, index) if big else outs[kind * 8 + index]
            target[at] = new[kind]

    arrive("pack")
    total = squares[0:1, 0:1] + total_of(jnp.square(grad_in[: G_BIAS + 1, :]))
    for k in range(4):
        total = total + total_of(jnp.square(pack[R_LSTM + k * 2 * H : R_LSTM + k * 2 * H + H, :]))
    loss[...] = grad_in[G_SUMS : G_SUMS + 1, 0:1]
    number = grad_in[G_SUMS : G_SUMS + 1, 1:2]
    count[...] = number
    grad_norm = jnp.sqrt(total) / number
    norm[...] = grad_norm
    factor = jnp.minimum(1.0, clip_norm / grad_norm) / number
    rows = WIDE // H
    for k, span in enumerate(spans):
        c = k // per
        if k % per == 0:
            arrive(("own", c))
        arrive((1, k))
        for i in range(rows):
            at, r = k * WIDE + i * H, ((k % per) * rows + i) * EH
            step(1, owns[c][r : r + EH, :] * factor, (slice(None), slice(at, at + H)))
        for kind in range(3):
            send(buffer_of(made, kind, 1).at[:, span], outs[kind * 8 + 1].at[:, span])

    def finish(index):
        for kind in range(3):
            send(buffer_of(made, kind, index), outs[kind * 8 + index])

    arrive((3, 0))
    for half in range(2):
        for q in range(3):
            r = R_GRU + (half * 3 + q) * H
            step(3, pack[r : r + H, :] * factor, (half, slice(None), slice(q * H, (q + 1) * H)))
    finish(3)
    arrive((4, 0))
    for k in range(4):
        r = R_LSTM + k * 2 * H
        for block, start in ((0, 0), (1, H), (2, 0)):
            step(
                4,
                pack[r + start : r + start + H, :] * factor,
                (slice(block * H, (block + 1) * H), slice(k * H, (k + 1) * H)),
            )
    finish(4)
    arrive((5, 0))
    step(5, pack[R_FIRST:R_GRU, :] * factor)
    finish(5)
    step(0, grad_in[:EIN, :] * factor)
    step(2, pack[pl.ds(pl.multiple_of(R_EBIAS + place[0], 8), own_rows), :] * factor)
    step(6, pack[R_SECOND : R_SECOND + NT, :] * factor)
    bias = jnp.concatenate([grad_in[G_BIAS : G_BIAS + 1, :], pack[R_MISC + 1 : R_EBIAS, :]], axis=0)
    step(7, bias * factor)
    for copy in going:
        copy.wait()


VM = pl.BlockSpec(memory_space=pltpu.VMEM)
SM = pl.BlockSpec(memory_space=pltpu.SMEM)
HBM = pl.BlockSpec(memory_space=pl.ANY)


def per_device(
    node_feats,
    edge_feats,
    edge_ends,
    atom_counts,
    dataset_flags,
    targets,
    present,
    edge_in,
    edge_out,
    edge_bias,
    gru_weights,
    lstm_weights,
    head_first,
    head_second,
    biases,
    *moments_seconds,
):
    row = lax.axis_index("row")
    row_count = lax.axis_size("row")
    mol = lax.axis_index("mol")
    mol_bits = lax.axis_size("mol").bit_length() - 1
    row_bits = row_count.bit_length() - 1
    mols = node_feats.shape[0]
    own_rows = edge_out.shape[1] // H
    atoms = -(-mols * ATOMS // LB) * LB
    space = -(-mols * LIVE // (2 * LB)) * 2 * LB

    def row_swap(x, k):
        return lax.ppermute(x, "row", [(i, i ^ k) for i in range(row_count)])

    def mol_swap(x, bit):
        return lax.ppermute(x, "mol", [(i, i ^ (1 << bit)) for i in range(2**mol_bits)])

    def double(x, swap, bit):
        other = swap(x)
        return jnp.concatenate(
            [jnp.where(bit == 0, x, other), jnp.where(bit == 0, other, x)], axis=0
        )

    sds = jax.ShapeDtypeStruct
    n = row_count
    al = atoms + WINDOW - 128
    params = pltpu.CompilerParams(vmem_limit_bytes=56 * MIB)

    sent = edge_out.astype(bf16)
    bias_sent = edge_bias.reshape(own_rows, H)

    def forward_order(part):
        part = part.reshape(EH, own_rows, H)
        return part.transpose(1, 0, 2).reshape(own_rows, EH * H)

    parts, bias_parts = {}, {0: bias_sent}
    for bit in reversed(range(row_bits)):
        for k in list(bias_parts):
            bias_parts[k + (1 << bit)] = row_swap(bias_parts[k], 1 << bit)
        if not parts:
            sent, bias_parts = lax.optimization_barrier((sent, bias_parts))
            parts[0] = sent
        parts[1 << bit] = row_swap(sent, 1 << bit)

    ends = lax.dynamic_slice_in_dim(edge_ends, row * mols, mols, 1)
    feats = lax.dynamic_slice_in_dim(edge_feats, row * mols * EM, mols * EM, 1)
    table = jnp.concatenate([feats.reshape(EIN, mols, EM), ends.astype(bf16)], axis=0)
    table = table.transpose(1, 0, 2).reshape(mols, (EIN + 2) * EM)
    places = jnp.stack([(row ^ k) * own_rows for k in range(row_count)]).astype(jnp.int32)
    bias_rows = jnp.pad(biases, (0, 16 * 128 - biases.shape[0])).reshape(16, 128)

    at_hand = [parts[k] for k in range(n // 2)]

    def prepare(*refs):
        body_prepare(mols, *refs[:5], refs[5 : 5 + n // 2], *refs[5 + n // 2 :])

    prepared = pl.pallas_call(
        prepare,
        out_shape=(
            sds((2 + space // LB,), jnp.int32),
            sds((H, atoms), bf16),
            sds((EH, space), bf16),
            sds((EH, space), f32),
            sds((8, space), f32),
            sds((WINDOW, space), bf16),
            sds((WINDOW, space), bf16),
            sds((H, n // 2 * own_rows * H), bf16),
        ),
        in_specs=[SM] + [VM] * (4 + n // 2),
        out_specs=(SM,) + (VM,) * 7,
        scratch_shapes=[pltpu.VMEM((128, 128), f32), pltpu.VMEM((mols * PAD, H), f32)],
        compiler_params=params,
    )(atom_counts, table, node_feats, edge_in, bias_rows, *at_hand)
    forward = {k: forward_order(part) for k, part in parts.items() if k < n // 2}
    parts, bias_parts, places, prepared, forward = lax.optimization_barrier(
        (parts, bias_parts, places, prepared, forward)
    )
    meta, nodes, hid, before, feat, hot_src, hot_dst, turned = prepared
    for bit in reversed(range(row_bits)):
        for k in [k for k in parts if k > 1 << bit and not k & (1 << bit)]:
            parts[k + (1 << bit)] = row_swap(parts[k], 1 << bit)
    parts = [parts[k] for k in range(n)]
    bias_parts = [bias_parts[k] for k in range(n)]
    w_fwd = [forward[k] if k in forward else forward_order(parts[k]) for k in range(n)]

    away = n - n // 2

    def main(*refs):
        at = 10
        body_main(
            mols,
            own_rows,
            *refs[:at],
            refs[at : at + n],
            refs[at + n],
            refs[at + n + 1 : at + n + 1 + away],
            refs[at + n + 1 + away : at + 2 * n + 1 + away],
            *refs[at + 2 * n + 1 + away :],
        )

    pack, sums, src, g = pl.pallas_call(
        main,
        out_shape=(
            sds((R_PACK, 128), f32),
            sds((8, 128), f32),
            sds((LAYERS, H, space), bf16),
            sds((LAYERS, H, space), bf16),
        ),
        in_specs=[SM] * 4 + [VM] * (6 + n) + [HBM] * (1 + away) + [VM] * (n + 5),
        out_specs=(VM,) * 4,
        scratch_shapes=[
            pltpu.VMEM((H * EH, LB), bf16),
            pltpu.VMEM((LAYERS + 1, H, atoms), f32),
            pltpu.VMEM((LAYERS, H, al), bf16),
            pltpu.VMEM((LAYERS, H, atoms), bf16),
            pltpu.VMEM((LAYERS, 4, H, atoms), f32),
            pltpu.VMEM((H, al), f32),
            pltpu.VMEM((H, al), f32),
            pltpu.VMEM((H, atoms), bf16),
            pltpu.VMEM((H, al), bf16),
            pltpu.VMEM((H, H * EH), bf16),
            pltpu.VMEM((STEPS * mols, atoms), f32),
            pltpu.VMEM((STEPS * mols, atoms), f32),
            pltpu.VMEM((2, H, 3 * H), bf16),
            pltpu.VMEM((2, 3 * H, H), bf16),
            pltpu.VMEM((128, 128), f32),
            pltpu.VMEM((H, space), f32),
            pltpu.VMEM((n - n // 2, EH, own_rows * H), bf16),
            pltpu.SemaphoreType.DMA((1 + n - n // 2,)),
        ],
        compiler_params=pltpu.CompilerParams(vmem_limit_bytes=60 * MIB),
    )(
        atom_counts,
        dataset_flags,
        places,
        meta,
        targets.T,
        present.T,
        nodes,
        hid,
        hot_src,
        hot_dst,
        *w_fwd,
        turned,
        *parts[n // 2 :],
        *bias_parts,
        gru_weights,
        bias_rows,
        lstm_weights,
        head_first,
        head_second.T,
    )

    span = own_rows * H // CHUNKS

    def edge_parts(jobs, slots, heights, extra, last):
        kind = "pack" if len(extra) == 2 else "sum"
        if last:
            extra = extra + (before, feat, sums)
        *found, result = pl.pallas_call(
            functools.partial(body_edges, jobs, slots, kind, last),
            grid=(1,),
            out_shape=tuple(sds((height, EH), bf16) for height in heights)
            + (sds((8, EH) if last else (EH, space), f32),),
            in_specs=[SM]
            + [pl.BlockSpec((EH, span), lambda i, c=chunk: (0, c)) for _, chunk in jobs]
            + [VM] * 3
            + ([SM, VM] if kind == "pack" else [VM] * len(extra)),
            out_specs=(VM,) * (len(heights) + 1),
            scratch_shapes=[
                pltpu.VMEM((2, span, LB), bf16),
                pltpu.VMEM((len(jobs), EH, span), f32),
            ]
            + ([pltpu.VMEM((EH, space), f32)] if last else []),
            compiler_params=params,
        )(meta, *(parts[k] for k, _ in jobs), src, g, hid, *extra)
        return found, result

    row_steps = [(functools.partial(row_swap, k=1 << b), (row >> b) & 1) for b in range(row_bits)]
    mol_steps = [(functools.partial(mol_swap, bit=b), (mol >> b) & 1) for b in range(mol_bits)]
    tie = lax.optimization_barrier
    (core, core_bit), (cross, cross_bit) = row_steps

    def halves(x, bit):
        both = x.reshape((2, x.shape[0] // 2) + x.shape[1:])
        return (
            lax.dynamic_index_in_dim(both, 1 - bit, 0, False),
            lax.dynamic_index_in_dim(both, bit, 0, False),
        )

    def as_low(x, count):
        found = []
        for _ in range(count):
            high = lax.reduce_precision(x, 8, 7)
            found.append(high)
            x = x - high
        return jnp.concatenate(found, axis=0).astype(bf16)

    def from_low(x, count):
        x = x.astype(f32).reshape(count, -1, 128)
        found = x[count - 1]
        for k in reversed(range(count - 1)):
            found = found + x[k]
        return found

    def chain(own, pack, beside):
        for swap, bit in mol_steps:
            own_sent, own = halves(own, bit)
            half = own.shape[0]
            sent = [own_sent.astype(bf16)]
            if pack is not None:
                pack_sent, pack = halves(pack, bit)
                sent.append(as_low(pack_sent, 2))
            if beside is not None:
                sent.append(as_low(beside["rows"], 3))
            came = yield swap, jnp.concatenate(sent, axis=0) if len(sent) > 1 else sent[0]
            own = own + came[:half].astype(f32)
            if pack is not None:
                pack = pack + from_low(came[half : half + 2 * pack.shape[0]], 2)
            if beside is not None:
                beside["rows"] = beside["rows"] + from_low(came[half:], 3)
        piece = own if pack is None else jnp.concatenate([own, pack], axis=0)
        height, rest = piece.shape[0], own.shape[0]
        largest = jnp.maximum(jnp.max(jnp.abs(piece)), 1e-30)
        power = 14.0 - jnp.ceil(jnp.log2(largest))
        sent = jnp.concatenate(
            [piece * jnp.exp2(power), jnp.broadcast_to(power, (16, 128))], axis=0
        ).astype(jnp.float16)
        for swap, bit in reversed(mol_steps):
            came = yield swap, sent
            sent = jnp.concatenate(
                [jnp.where(bit == 0, sent, came), jnp.where(bit == 0, came, sent)], axis=0
            )
        raw, sent = sent, sent.astype(f32).reshape(-1, height + 16, 128)
        back = jnp.exp2(-sent[:, height : height + 1, 0:1])
        own = (sent[:, :rest] * back).reshape(-1, 128)
        square = jnp.sum(own * own)
        if pack is not None:
            pack = raw.reshape(-1, height + 16, 128)[:, rest:].reshape(-1, 128)
            square = square + jnp.sum(jnp.square(sent[:, rest:height] * back))
        return own, pack, square

    core_place = (1 - core_bit).reshape(1).astype(jnp.int32)
    half = pack.shape[0] // 2
    (message, far), carry = edge_parts(
        ((2, 0), (3, 0)),
        ((1, 0), (0, 0)),
        (span + 2 * half, span),
        (core_place, pack),
        False,
    )
    came = core(message)
    pack = halves(pack, core_bit)[1]
    pack_sent, pack = halves(pack + from_low(came[span:], 2), cross_bit)
    sent = (far.astype(f32) + came[:span].astype(f32)).astype(bf16)
    sent = jnp.concatenate([sent, as_low(pack_sent, 2)], axis=0)
    sent, carry = tie((sent, carry))
    arrived = cross(sent)
    (message, near, far), carry = edge_parts(
        ((0, 0), (1, 0), (2, 1), (3, 1), (1, 1)),
        ((1, 0), (0, 0), (2, 0), (0, span), (0, 2 * span)),
        (3 * span, span, span),
        (carry,),
        False,
    )
    message, arrived = tie((message, arrived))
    came = core(message)
    own = near.astype(f32) + came[:span].astype(f32) + arrived[:span].astype(f32)
    pack = pack + from_low(arrived[span:], 2)
    sent = (far.astype(f32) + came[span : 2 * span].astype(f32)).astype(bf16)
    near_came = came[2 * span :]

    first = chain(own, pack, None)
    first_swap, first_sent = next(first)
    sent, first_sent, carry = tie((sent, first_sent, carry))
    arrived = cross(sent)
    first_came = first_swap(first_sent)
    (near,), grad_in = edge_parts(((0, 1),), ((0, 0),), (span,), (carry,), True)
    near, arrived, first_came = tie((near, arrived, first_came))
    beside = {"rows": grad_in}
    own = near.astype(f32) + near_came.astype(f32) + arrived.astype(f32)

    second = chain(own, None, beside)
    second_swap, second_sent = next(second)
    first_swap, first_sent = first.send(first_came)
    while True:
        first_sent, second_sent = tie((first_sent, second_sent))
        first_came, second_came = first_swap(first_sent), second_swap(second_sent)
        second_swap, second_sent = second.send(second_came)
        try:
            first_swap, first_sent = first.send(first_came)
        except StopIteration as end:
            first_own, pack, square = end.value
            break
    second_came, came = second_swap(second_sent), cross(pack)
    rows, pack = tie((beside["rows"], pack))
    came_rows = cross(rows)
    try:
        second.send(second_came)
    except StopIteration as end:
        second_own, _, more = end.value
    squares = jnp.broadcast_to(square + more, (8, 128))
    came, came_rows, _ = tie((came, came_rows, squares))
    grad_in = rows + came_rows
    grad_in = grad_in + core(grad_in)
    pack = jnp.concatenate(
        [jnp.where(cross_bit == 0, pack, came), jnp.where(cross_bit == 0, came, pack)], axis=0
    )
    came = core(pack)
    pack = jnp.concatenate(
        [jnp.where(core_bit == 0, pack, came), jnp.where(core_bit == 0, came, pack)], axis=0
    )
    pack = pack.astype(f32).reshape(n * 2**mol_bits, -1, 128)
    pack = (pack[:, :-16] * jnp.exp2(-pack[:, -16:-15, 0:1])).reshape(-1, 128)
    came = row_swap(squares, 3)
    came, pack, grad_in = tie((came, pack, grad_in))
    squares = (squares + row_swap(squares, 1)) + (row_swap(squares, 2) + came)
    owns = [first_own, second_own]

    weights = [
        edge_in,
        edge_out,
        edge_bias,
        gru_weights,
        lstm_weights,
        head_first,
        head_second,
        biases,
    ]
    states = []
    for group in (weights, moments_seconds[:8], moments_seconds[8:]):
        group = list(group)
        group[2] = group[2].reshape(own_rows, H)
        group[6] = group[6].T
        if group[7] is biases:
            group[7] = bias_rows
        else:
            group[7] = jnp.pad(group[7], (0, 16 * 128 - group[7].shape[0])).reshape(16, 128)
        states += group
    spots = [HBM if index in BIG else VM for index in range(8)] * 3
    copies = 3 * (own_rows * H // WIDE + len(BIG) - 1)
    shapes = [sds(state.shape, f32) for state in states]
    results = pl.pallas_call(
        functools.partial(body_adamw, own_rows),
        out_shape=tuple(shapes) + (sds((1, 1), f32),) * 3,
        in_specs=[SM] + [HBM] * (CHUNKS + 1) + [VM] * 2 + spots,
        out_specs=tuple(spots) + (VM,) * 3,
        scratch_shapes=[pltpu.VMEM(own.shape, f32) for own in owns]
        + [pltpu.VMEM(pack.shape, f32)]
        + [pltpu.VMEM(shapes[index].shape, f32) for _ in range(6) for index in BIG]
        + [pltpu.SemaphoreType.DMA((copies + CHUNKS + 1,)), pltpu.SemaphoreType.DMA((copies,))],
        compiler_params=params,
    )(places, *owns, pack, grad_in, squares, *states)
    results = list(results)
    for kind in range(3):
        results[kind * 8 + 2] = results[kind * 8 + 2].reshape(own_rows * H)
        results[kind * 8 + 6] = results[kind * 8 + 6].T
        results[kind * 8 + 7] = results[kind * 8 + 7].reshape(-1)[: biases.shape[0]]
    for index in range(24, 27):
        results[index] = results[index].reshape(())
    return tuple(results)


def solution(mesh):
    weights = (P(), P(None, "row"), P("row"), P(), P(), P(), P(), P())
    in_specs = (
        P(("mol", "row"), None, None),
        P(None, "mol"),
        P(None, "mol", None),
        P(("mol", "row")),
        P(("mol", "row")),
        P(("mol", "row"), None),
        P(("mol", "row"), None),
    ) + weights * 3
    out_specs = weights * 3 + (P(), P(), P())
    return jax.shard_map(
        per_device, mesh=mesh, in_specs=in_specs, out_specs=out_specs, check_vma=False
    )
```
